128 devices in a mesh: gx: 8 (over x, core), gy: 16 (over y, z).
Axes of the slice: x: 4, y: 4, z: 4, core: 2. Of those that a mesh axis runs over, the one named last changes fastest.
Arguments:
- pressure_source: float32 [128, 512, 256], P('gx', 'gy'), may hold values from -6 to 6
- conductance: float32 [128, 512, 256], P('gx', 'gy'), may hold values from 0.1 to 10
- coarse_inverse: bfloat16 [8, 32, 128, 128], P('gx', 'gy'), may hold values from -4 to 4
Outputs:
- pressure_correction: float32 [128, 512, 256], P('gx', 'gy')
The draws below stay inside these ranges and needn't reach their ends.
All inputs are finite; a program needn't handle non-finite values.
Results may differ from the reference program's by a relative error of at most 0.0024.
Values may be sent and summed in bfloat16 or wider, within the bound.
A program may use at most 128 MiB of HBM per device.

```python
import math
import jax
import jax.numpy as jnp
from jax import lax

NZ = 256
DEG = 3
LEVELS = 4
NX = 128
NY = 512
NZC = 32
BLOCK = 128
N_GX = 8


def level_of(stream_key, extent, pieces, smallest, top_value):
    loudness = 1.0
    for axis_at, shards_of in pieces:
        steps = jax.random.uniform(jax.random.fold_in(jax.random.fold_in(stream_key, 6), axis_at), (shards_of,), jnp.float32, smallest / len(pieces), top_value / len(pieces))
        loudness = loudness * jnp.repeat(jnp.exp(steps), extent[axis_at] // shards_of).reshape((-1,) + (1,) * (len(extent) - 1 - axis_at))
    return loudness


def scatter_about(key, dims, spread, bound, split=(), held_as=jnp.bfloat16):
    values = spread * jax.random.normal(key, dims, jnp.float32)
    if split:
        values = values * level_of(key, dims, split, -0.22, 0.18)
    return jnp.clip(values, -bound, bound).astype(held_as)


def setup_inputs(seed: int = 0) -> dict:
    seeds = jax.random.split(jax.random.key(seed), 4)
    return {
        "pressure_source": scatter_about(seeds[0], (NX, NY, NZ), 1.0, 6.0, ((0, 8), (1, 16)), jnp.float32),
        "conductance": jnp.clip(jnp.exp(math.log(10.0) - 4.6051702 * jax.random.uniform(seeds[1], (NX, NY, NZ), jnp.float32) ** level_of(seeds[1], (NX, NY, NZ), ((0, 8), (1, 16)), -0.2, 0.2)), 0.1, 10.0),
        "coarse_inverse": scatter_about(seeds[2], (N_GX, NZC, BLOCK, BLOCK), (BLOCK // 64) ** -0.5, 4.0, ((0, 8), (1, 16))),
    }


LMAX = 2.0
LMIN = 0.25


def chebyshev_bounds():
    theta = 0.5 * (LMAX + LMIN)
    delta = 0.5 * (LMAX - LMIN)
    return theta, delta, theta / delta


def shift_upward(array):
    return jnp.concatenate([array[:, :, 1:], jnp.zeros_like(array[:, :, :1])], axis=2)


def shift_downward(array):
    return jnp.concatenate([jnp.zeros_like(array[:, :, :1]), array[:, :, :-1]], axis=2)


def setup(kappa_level, scale):
    padded = jnp.pad(kappa_level, ((1, 1), (1, 1), (0, 0)))
    center = padded[1:-1, 1:-1]
    couplings = (0.5 * (center + padded[2:, 1:-1]), 0.5 * (center + padded[:-2, 1:-1]),
                 0.5 * (center + padded[1:-1, 2:]), 0.5 * (center + padded[1:-1, :-2]),
                 0.5 * (center + shift_upward(center)), 0.5 * (center + shift_downward(center)))
    diagonal = scale * (((((couplings[0] + couplings[1]) + couplings[2]) + couplings[3]) + couplings[4]) + couplings[5])
    return couplings, 1.0 / diagonal


def operate(field, couplings, scale):
    padded = jnp.pad(field, ((1, 1), (1, 1), (0, 0)))
    center = padded[1:-1, 1:-1]
    flux = couplings[0] * (center - padded[2:, 1:-1]) + couplings[1] * (center - padded[:-2, 1:-1])
    flux = flux + couplings[2] * (center - padded[1:-1, 2:]) + couplings[3] * (center - padded[1:-1, :-2])
    flux = flux + couplings[4] * (center - shift_upward(center)) + couplings[5] * (center - shift_downward(center))
    return scale * flux


def smooth(field, source, couplings, inverse_diagonal, scale):
    theta, delta, sigma = chebyshev_bounds()
    if field is None:
        update = inverse_diagonal * source
    else:
        update = inverse_diagonal * (source - operate(field, couplings, scale))
    direction = update / theta
    ratio = 1.0 / sigma
    for sweep in range(DEG - 1):
        field = direction if field is None else field + direction
        update = inverse_diagonal * (source - operate(field, couplings, scale))
        ratio_next = 1.0 / (2.0 * sigma - ratio)
        direction = (ratio_next * ratio) * direction + (2.0 * ratio_next / delta) * update
        ratio = ratio_next
    return direction if field is None else field + direction


def restrict(array):
    first, second, third = array.shape
    return array.reshape(first // 2, 2, second // 2, 2, third // 2, 2).mean(axis=(1, 3, 5))


def prolong(array):
    first, second, third = array.shape
    wide = jnp.broadcast_to(array[:, None, :, None, :, None], (first, 2, second, 2, third, 2))
    return wide.reshape(2 * first, 2 * second, 2 * third)


def reference(pressure_source, conductance, coarse_inverse):
    source = pressure_source
    kappa_level = conductance
    saved = []
    for level in range(LEVELS - 1):
        scale = 0.25 ** level
        couplings, inverse_diagonal = setup(kappa_level, scale)
        field = smooth(None, source, couplings, inverse_diagonal, scale)
        residual = source - operate(field, couplings, scale)
        saved.append((source, field, kappa_level))
        source = restrict(residual)
        kappa_level = restrict(kappa_level)
    coarse_x, coarse_y, coarse_z = source.shape
    slab = coarse_x // N_GX
    rounded = source.astype(jnp.bfloat16)
    blocks = rounded.reshape(N_GX, slab, coarse_y, coarse_z).transpose(0, 3, 1, 2).reshape(N_GX, coarse_z, slab * coarse_y)
    solved = jnp.einsum("pkij,pkj->pki", coarse_inverse.astype(jnp.float32), blocks.astype(jnp.float32),
                        precision=lax.Precision.HIGHEST)
    correction = solved.reshape(N_GX, coarse_z, slab, coarse_y).transpose(0, 2, 3, 1).reshape(coarse_x, coarse_y, coarse_z)
    for level in reversed(range(LEVELS - 1)):
        scale = 0.25 ** level
        source, field, kappa_level = saved[level]
        couplings, inverse_diagonal = setup(kappa_level, scale)
        correction = smooth(field + prolong(correction), source, couplings, inverse_diagonal, scale)
    return correction
```

```python
import functools

import jax
import jax.numpy as jnp
from jax import lax
from jax.experimental import pallas as pl
from jax.experimental.pallas import tpu as pltpu
from jax.sharding import PartitionSpec as P

MESH = pl.DeviceIdType.MESH

LMAX = 2.0
LMIN = 0.25
THETA = 0.5 * (LMAX + LMIN)
DELTA = 0.5 * (LMAX - LMIN)
SIGMA = THETA / DELTA
RATIO_0 = 1.0 / SIGMA
RATIO_1 = 1.0 / (2.0 * SIGMA - RATIO_0)
RATIO_2 = 1.0 / (2.0 * SIGMA - RATIO_1)
STEP_1 = (RATIO_1 * RATIO_0, 2.0 * RATIO_1 / DELTA)
STEP_2 = (RATIO_2 * RATIO_1, 2.0 * RATIO_2 / DELTA)

F32 = jnp.float32
BF16 = jnp.bfloat16

AROUND = [(a, b) for a in (-1, 0, 1) for b in (-1, 0, 1) if (a, b) != (0, 0)]
WIDE = [(a, b) for a in (-2, -1, 0, 1, 2) for b in (-1, 0, 1) if (a, b) != (0, 0)]


class Level:
    def __init__(self, nx, ny, X, x0, R, J, hold, row0, erow, xc):
        self.nx, self.ny, self.X, self.x0, self.R, self.J = nx, ny, X, x0, R, J
        self.hold, self.row0, self.erow, self.xc = hold, row0, erow, xc
        self.rows = 16 + ny

    def scratch(self, coarse_x):
        X, R, J = self.X, self.R, self.J
        vm = lambda *shape: pltpu.VMEM(shape + (128,), F32)
        return dict(
            NS=vm(X, R, self.rows),
            NK=vm(X, R, self.rows),
            NV=vm(X, R, self.rows),
            SV=vm(self.nx + 2, R, self.rows),
            RN=vm(self.nx, R, self.rows),
            E=vm(coarse_x, R, 2 * (self.ny // 2 + 16) if self.nx > 4 else 24),
            HK=vm(X, R, J + 2, 8),
            CX=vm(X + 1, R, J, 8),
            CY=vm(X, R, J + 1, 8),
            CM=vm(X, R, J, 8),
            CP=vm(X, R, J, 8),
            Q=vm(X, R, J, 8),
            G=vm(X, R, J, 8),
            D=vm(X, R, J, 8),
            DIR=vm(X, R, J, 8),
            VA=vm(X, R, J + 2, 8),
            VB=vm(X, R, J + 2, 8),
        )


LEVELS = (
    Level(16, 32, 24, 4, 2, 5, 1, 4, 12, 6),
    Level(8, 16, 24, 8, 1, 4, 1, 0, 8, 4),
    Level(4, 8, 20, 8, 1, 3, 2, 0, 0, 0),
)
COARSE_X = (24, 20, 10)


def lanes():
    return lax.broadcasted_iota(jnp.int32, (8, 128), 1)


def sublanes():
    return lax.broadcasted_iota(jnp.int32, (8, 128), 0)


def turn(value, shift, axis):
    return pltpu.roll(value, shift % value.shape[axis], axis)


def pick(value, index):
    return jnp.take_along_axis(value, index, axis=1, mode="promise_in_bounds")


def rows_of(L, j):
    return pl.ds(L.row0 + j, 8, stride=L.J)


def beside_z(L, parts):
    h = L.hold
    down = [turn(p, h, 1) for p in parts]
    up = [turn(p, -h, 1) for p in parts]
    if L.R == 2:
        lane = lanes()
        down[1] = jnp.where(lane == 0, down[0], down[1])
        up[0] = jnp.where(lane == 127, up[1], up[0])
    return down, up


def store_wrapped(ref, x, r, J, values):
    for j in range(J):
        ref[x, r, j + 1] = values[j]
    ref[x, r, 0] = turn(values[J - 1], 1, 0)
    ref[x, r, J + 1] = turn(values[0], -1, 0)


def loop(lo, hi, body):
    def step(x, carry):
        body(x)
        return carry

    lax.fori_loop(lo, hi, step, 0)


def prepare(L, M, lo, hi, gx, gy, count_x, count_y):
    J, R = L.J, L.R
    sub, lane = sublanes(), lanes()
    first = gy * L.ny - 8 + L.row0
    keep = []
    for j in range(J):
        place = first + j + J * sub
        keep.append(jnp.where((place >= 0) & (place < L.ny * count_y), 0.5, 0.0).astype(F32))

    def halves(x):
        place = gx * L.nx + x - L.x0
        inside = jnp.where((place >= 0) & (place < L.nx * count_x), 1.0, 0.0).astype(F32)
        for r in range(R):
            store_wrapped(M["HK"], x, r, J, [M["NK"][x, r, rows_of(L, j), :] * (keep[j] * inside) for j in range(J)])

    loop(lo - 1, hi + 1, halves)
    HK = M["HK"]
    for r in range(R):
        for j in range(J):
            M["CX"][lo, r, j] = HK[lo - 1, r, j + 1] + HK[lo, r, j + 1]

    def couple(x):
        for j in range(J):
            mine = [HK[x, r, j + 1] for r in range(R)]
            down, up = beside_z(L, mine)
            down[0] = jnp.where(lane < L.hold, 0.0, down[0])
            up[R - 1] = jnp.where(lane >= 128 - L.hold, 0.0, up[R - 1])
            for r in range(R):
                h = mine[r]
                xm, xp = HK[x - 1, r, j + 1], HK[x + 1, r, j + 1]
                ym, yp = HK[x, r, j], HK[x, r, j + 2]
                diagonal = (xm + xp) + (ym + yp) + (down[r] + up[r]) + 6.0 * h
                M["CX"][x + 1, r, j] = h + xp
                M["CY"][x, r, j] = h + ym
                if j == J - 1:
                    M["CY"][x, r, J] = h + yp
                low, high = h + down[r], h + up[r]
                if r == 0:
                    low = jnp.where(lane < L.hold, 0.0, low)
                if r == R - 1:
                    high = jnp.where(lane >= 128 - L.hold, 0.0, high)
                M["CM"][x, r, j] = low
                M["CP"][x, r, j] = high
                M["D"][x, r, j] = diagonal
                M["Q"][x, r, j] = jnp.where(h > 0.0, 1.0 / diagonal, 0.0)

    loop(lo, hi, couple)


def scale_source(L, M, lo, hi, start):
    J = L.J

    def body(x):
        for r in range(L.R):
            values = []
            for j in range(J):
                g = M["Q"][x, r, j] * M["NS"][x, r, rows_of(L, j), :]
                M["G"][x, r, j] = g
                values.append(g * (1.0 / THETA))
            if start:
                store_wrapped(M["VA"], x, r, J, values)

    loop(lo, hi, body)


def sweep(L, M, src, dst, lo, hi, kind, step=None, keep_rows=None, emit=None):
    J, R = L.J, L.R
    V = M[src]

    def body(x):
        new = [[None] * J for _ in range(R)]
        for j in range(J):
            mine = [V[x, r, j + 1] for r in range(R)]
            down, up = beside_z(L, mine)
            for r in range(R):
                c = mine[r]
                near = M["CX"][x, r, j] * V[x - 1, r, j + 1] + M["CX"][x + 1, r, j] * V[x + 1, r, j + 1]
                near = near + (M["CY"][x, r, j] * V[x, r, j] + M["CY"][x, r, j + 1] * V[x, r, j + 2])
                near = near + (M["CM"][x, r, j] * down[r] + M["CP"][x, r, j] * up[r])
                update = (M["G"][x, r, j] - c) + M["Q"][x, r, j] * near
                if kind == "residual":
                    M["RN"][x - L.x0, r, rows_of(L, j), :] = M["D"][x, r, j] * update
                    continue
                if kind == "first":
                    direction = update * (1.0 / THETA)
                elif kind == "from_zero":
                    direction = step[0] * c + step[1] * update
                else:
                    direction = step[0] * M["DIR"][x, r, j] + step[1] * update
                if kind != "last":
                    M["DIR"][x, r, j] = direction
                new[r][j] = c + direction
        if kind == "residual":
            return
        for r in range(R):
            if dst is not None:
                store_wrapped(M[dst], x, r, J, new[r])
            if keep_rows is not None:
                for j in range(J):
                    keep_rows[x - L.x0 + 1, r, rows_of(L, j), :] = new[r][j]
        if emit is not None:
            emit(x, new)

    loop(lo, hi, body)


def descend(L, M):
    lo, hi = L.x0, L.x0 + L.nx
    sweep(L, M, "VA", "VB", lo - 2, hi + 2, "from_zero", STEP_1)
    sweep(L, M, "VB", "VA", lo - 1, hi + 1, "last", STEP_2, keep_rows=M["SV"])
    sweep(L, M, "VA", None, lo, hi, "residual")


def ascend(L, M, margin, emit):
    lo, hi = L.x0, L.x0 + L.nx

    def begin(x):
        xc = lax.shift_right_logical(x, 1) + L.xc
        for r in range(L.R):
            values = []
            for j in range(L.J):
                added = M["E"][xc, r, pl.ds(L.erow + j, 8, stride=L.J), :]
                total = M["NV"][x, r, rows_of(L, j), :] + added
                values.append(jnp.where(M["HK"][x, r, j + 1] > 0.0, total, 0.0))
            store_wrapped(M["VA"], x, r, L.J, values)

    loop(lo - margin, hi + margin, begin)
    margin -= 1
    sweep(L, M, "VA", "VB", lo - margin, hi + margin, "first")
    margin -= 1
    sweep(L, M, "VB", "VA", lo - margin, hi + margin, "next", STEP_1)
    margin -= 1
    sweep(L, M, "VA", None, lo - margin, hi + margin, "last", STEP_2, emit=emit)


def coarsen(L, src, sx0, scale, put):
    lane = lanes()
    even = (lane * 2) & 127

    def body(x):
        for t in range(max(1, L.ny // 16)):
            sums = []
            for r in range(L.R):
                rows = [
                    src[sx0 + 2 * x + dx, r, pl.ds(8 + 16 * t + b, 8, stride=2), :] for dx in (0, 1) for b in (0, 1)
                ]
                total = (rows[0] + rows[1]) + (rows[2] + rows[3])
                if L.R == 2:
                    sums.append(pick(total + turn(total, -1, 1), even))
                else:
                    other = jnp.where((lane & L.hold) == 0, turn(total, -L.hold, 1), turn(total, L.hold, 1))
                    sums.append(total + other)
            value = jnp.where(lane < 64, sums[0], sums[1]) if L.R == 2 else sums[0]
            put(x, t, value * scale)

    return body


def coarsen_into(L, src, sx0, scale, nxt, dst):
    def put(x, t, value):
        dst[nxt.x0 + x, 0, 8 + 8 * t : 16 + 8 * t, :] = value

    loop(0, L.nx // 2, coarsen(L, src, sx0, scale, put))


def kernel(gx_size, gy_size, names, source, conductance, inverse, out, *refs):
    S = dict(zip(names, refs))
    M = [{k[1:]: v for k, v in S.items() if k[0] == str(l)} for l in range(3)]
    gx, gy = lax.axis_index("gx"), lax.axis_index("gy")
    L0, L1, L2 = LEVELS

    def device(a, b):
        return {"gx": lax.rem(gx + a + gx_size, gx_size), "gy": lax.rem(gy + b + gy_size, gy_size)}

    def remote(src, dst, name, n, a, b):
        return pltpu.make_async_remote_copy(
            src_ref=src,
            dst_ref=dst,
            send_sem=S["send_" + name].at[n],
            recv_sem=S["recv_" + name].at[n],
            device_id=device(a, b),
            device_id_type=MESH,
        )

    def exchange(L, src, sx0, dst, width, where, name):
        copies = []
        for n, (a, b) in enumerate(where):
            if a == 0:
                xs, xd, wx = sx0, L.x0, L.nx
            elif abs(a) == 2:
                xs, xd, wx = sx0, L.x0 - (a // 2) * 2 * L.nx, L.nx
            elif a == 1:
                xs, xd, wx = sx0 + L.nx - width, L.x0 - width, width
            else:
                xs, xd, wx = sx0, L.x0 + L.nx, width
            if b == 0:
                ys, yd, wy = 8, 8, L.ny
            elif b == 1:
                ys, yd, wy = L.ny, 0, 8
            else:
                ys, yd, wy = 8, 8 + L.ny, 8
            copies.append(
                remote(
                    src.at[pl.ds(xs, wx), :, pl.ds(ys, wy), :],
                    dst.at[pl.ds(xd, wx), :, pl.ds(yd, wy), :],
                    name,
                    n,
                    a,
                    b,
                )
            )
        for copy in copies:
            copy.start()
        return copies

    def arrive(copies):
        for copy in copies:
            copy.wait_recv()

    sent = []

    peers = list(WIDE) + [(0, b) for b in range(2, gy_size - 1)]
    barrier = pltpu.get_barrier_semaphore()
    for a, b in peers:
        pl.semaphore_signal(barrier, inc=1, device_id=device(a, b), device_id_type=MESH)

    loads = []
    for n, (src, dst) in enumerate(((conductance, M[0]["NK"]), (source, M[0]["NS"]))):
        for r in range(2):
            copy = pltpu.make_async_copy(
                src.at[:, :, pl.ds(128 * r, 128)],
                dst.at[pl.ds(4, 16), r, pl.ds(8, 32), :],
                S["local"].at[2 * n + r],
            )
            copy.start()
            loads.append(copy)
    for copy in loads:
        copy.wait()

    sub, lane = sublanes(), lanes()
    XP, YP, XR, YR = S["xp"], S["yp"], S["xr"], S["yr"]
    fields = (M[0]["NK"], M[0]["NS"])

    def pack_x(i):
        for a in range(2):
            for r in range(2):
                XP[0, a, i, r] = fields[a][4 + i, r, 8:40, :].astype(BF16)
                XP[1, a, i, r] = fields[a][16 + i, r, 8:40, :].astype(BF16)

    loop(0, 4, pack_x)

    def pack_y(i):
        for a in range(2):
            low, high = [], []
            for d in range(2):
                x = 4 + 2 * i + d
                near, far = fields[a][x, 0, 8:16, :], fields[a][x, 1, 8:16, :]
                low.append(jnp.where(sub < 4, near, turn(far, 4, 0)))
                near, far = fields[a][x, 0, 32:40, :], fields[a][x, 1, 32:40, :]
                high.append(jnp.where(sub < 4, turn(near, 4, 0), far))
            YP[0, a, i] = jnp.concatenate(low, axis=0).astype(BF16)
            YP[1, a, i] = jnp.concatenate(high, axis=0).astype(BF16)

    loop(0, 8, pack_y)

    pl.semaphore_wait(barrier, len(peers))

    fine = []
    for n, (a, b) in enumerate(AROUND):
        if b == 0:
            fine.append(remote(XP.at[(a + 1) // 2], XR.at[(1 - a) // 2], "fine", n, a, b))
        else:
            xs, xd, wx = {0: (0, 2, 8), 1: (6, 0, 2), -1: (0, 10, 2)}[a]
            fine.append(
                remote(
                    YP.at[(b + 1) // 2, :, pl.ds(xs, wx)],
                    YR.at[(1 - b) // 2, :, pl.ds(xd, wx)],
                    "fine",
                    n,
                    a,
                    b,
                )
            )
    for copy in fine:
        copy.start()
    sent += fine

    coarsen_into(L0, M[0]["NK"], 4, 0.125, L1, M[1]["NK"])
    kappa_1 = exchange(L1, M[1]["NK"], 8, M[1]["NK"], 6, AROUND, "kappa_1")
    coarsen_into(L1, M[1]["NK"], 8, 0.125, L2, M[2]["NK"])
    kappa_2 = exchange(L2, M[2]["NK"], 8, M[2]["NK"], 4, WIDE, "kappa_2")
    sent += kappa_1 + kappa_2

    one = lambda mask: jnp.where(mask, 1.0, 0.0).astype(BF16)
    row = lax.broadcasted_iota(jnp.int32, (128, 128), 0)
    column = lax.broadcasted_iota(jnp.int32, (128, 128), 1)
    order = one(row == ((column >> 2) & 1) * 64 + (column >> 3) * 4 + (column & 3))
    for k in range(2):
        S["mp"][128 * k : 128 * (k + 1), :] = jnp.dot(
            inverse[0, k], order, preferred_element_type=F32
        ).astype(BF16)

    row = lax.broadcasted_iota(jnp.int32, (48, 256), 0)
    column = lax.broadcasted_iota(jnp.int32, (48, 256), 1)
    layer = jnp.where(row >= 24, 1, 0)
    row = row - 24 * layer
    half = jnp.where(row >= 12, 1, 0)
    row = row - 12 * half
    base = layer * 128 + half * 64

    def share(d):
        chosen = one(column == base + ((row + (4 * d + 60)) & 63))
        S["ms"][d] = jnp.dot(chosen, S["mp"][...], preferred_element_type=F32).astype(BF16)

    loop(0, gy_size, share)
    matrices = []
    for n in range(gy_size - 1):
        there = lax.rem(gy + n + 1, gy_size)
        matrices.append(remote(S["ms"].at[there], S["mm"].at[gy], "matrix", n, 0, n + 1))
    for copy in matrices:
        copy.start()
    sent += matrices
    S["mm"][gy] = S["ms"][gy]

    arrive(fine)

    def unpack_x(i):
        for a in range(2):
            for r in range(2):
                fields[a][i, r, 8:40, :] = XR[0, a, i, r].astype(F32)
                fields[a][20 + i, r, 8:40, :] = XR[1, a, i, r].astype(F32)

    loop(0, 4, unpack_x)

    def unpack_y(i):
        for a in range(2):
            low, high = YR[0, a, i].astype(F32), YR[1, a, i].astype(F32)
            for d in range(2):
                x = 2 * i + d
                part = low[8 * d : 8 * d + 8]
                fields[a][x, 0, 0:8, :] = turn(part, 4, 0)
                fields[a][x, 1, 0:8, :] = part
                part = high[8 * d : 8 * d + 8]
                fields[a][x, 0, 40:48, :] = part
                fields[a][x, 1, 40:48, :] = turn(part, 4, 0)

    loop(0, 12, unpack_y)

    place = (gx, gy, gx_size, gy_size)
    prepare(L0, M[0], 1, 23, *place)
    scale_source(L0, M[0], 1, 23, True)
    descend(L0, M[0])
    coarsen_into(L0, M[0]["RN"], 0, 0.5, L1, M[1]["NS"])
    source_1 = exchange(L1, M[1]["NS"], 8, M[1]["NS"], 4, AROUND, "source_1")
    smooth_0 = exchange(L0, M[0]["SV"], 1, M[0]["NV"], 3, AROUND, "smooth_0")
    sent += source_1 + smooth_0

    arrive(kappa_1)
    prepare(L1, M[1], 3, 21, *place)
    arrive(source_1)
    scale_source(L1, M[1], 4, 20, True)
    descend(L1, M[1])
    coarsen_into(L1, M[1]["RN"], 0, 0.5, L2, M[2]["NS"])
    source_2 = exchange(L2, M[2]["NS"], 8, M[2]["NS"], 4, WIDE, "source_2")
    smooth_1 = exchange(L1, M[1]["SV"], 1, M[1]["NV"], 5, AROUND, "smooth_1")
    sent += source_2 + smooth_1

    arrive(kappa_2)
    prepare(L2, M[2], 3, 17, *place)
    arrive(source_2)
    scale_source(L2, M[2], 3, 17, True)
    descend(L2, M[2])
    tiles = []
    make = coarsen(L2, M[2]["RN"], 0, 1.0 / 128.0, lambda x, t, value: tiles.append(value))
    make(0)
    make(1)
    rounded = jnp.where(sub < 4, tiles[0], turn(tiles[1], 4, 0)).astype(BF16).astype(F32)
    S["mine"][...] = rounded
    gathered = []
    for n in range(gy_size - 1):
        gathered.append(remote(S["mine"], S["all"].at[gy], "gather", n, 0, n + 1))
    for copy in gathered:
        copy.start()
    smooth_2 = exchange(L2, M[2]["SV"], 1, M[2]["NV"], 4, WIDE, "smooth_2")
    sent += gathered + smooth_2
    S["all"][gy] = rounded

    kept = []
    for l, L in enumerate(LEVELS):
        copy = pltpu.make_async_copy(
            M[l]["SV"].at[pl.ds(1, L.nx), :, pl.ds(8, L.ny), :],
            M[l]["NV"].at[pl.ds(L.x0, L.nx), :, pl.ds(8, L.ny), :],
            S["local"].at[l],
        )
        copy.start()
        kept.append(copy)
    for copy in kept:
        copy.wait()

    arrive(matrices)
    arrive(gathered)
    right = S["all"][...].reshape(gy_size * 8, 128).astype(BF16)
    layer_of = lax.broadcasted_iota(jnp.int32, (24, 128), 1) >> 2

    def solve(d, total):
        product = jnp.dot(S["mm"][d], right, preferred_element_type=F32)
        total = total + jnp.where(layer_of == 2 * d, product[:24], 0.0)
        return total + jnp.where(layer_of == 2 * d + 1, product[24:], 0.0)

    S["corr"][2] = lax.fori_loop(0, gy_size, solve, jnp.zeros((24, 128), F32))
    coarse = []
    for n, a in enumerate((-2, -1, 1, 2)):
        coarse.append(remote(S["corr"].at[2], S["corr"].at[2 - a], "coarse", n, a, 0))
    for copy in coarse:
        copy.start()
    sent += coarse
    arrive(smooth_2)
    arrive(coarse)

    for slab in range(5):
        for d in range(2):
            for b in range(2):
                M[2]["E"][2 * slab + d, 0, pl.ds(b, 8, stride=2), :] = S["corr"][slab, 12 * d : 12 * d + 8, :]
                M[2]["E"][2 * slab + d, 0, pl.ds(16 + b, 4, stride=2), :] = S["corr"][slab, 12 * d + 8 : 12 * d + 12, :]

    def emit_2(x, new):
        for j in range(L2.J):
            for b in range(2):
                M[1]["E"][x, 0, pl.ds(2 * j + b, 8, stride=2 * L2.J), :] = new[0][j]

    def emit_1(x, new):
        for j in range(L1.J):
            for r in range(2):
                value = pick(new[0][j], (lane >> 1) + 64 * r)
                for b in range(2):
                    M[0]["E"][x, r, pl.ds(2 * j + b, 8, stride=2 * L1.J), :] = value

    def emit_0(x, new):
        for r in range(2):
            for j in range(L0.J):
                S["result"][x - L0.x0, r, rows_of(L0, j), :] = new[r][j]

    ascend(L2, M[2], 6, emit_2)
    arrive(smooth_1)
    ascend(L1, M[1], 5, emit_1)
    arrive(smooth_0)
    ascend(L0, M[0], 3, emit_0)

    stores = []
    for r in range(2):
        copy = pltpu.make_async_copy(
            S["result"].at[:, r, pl.ds(8, 32), :], out.at[:, :, pl.ds(128 * r, 128)], S["local"].at[r]
        )
        copy.start()
        stores.append(copy)
    for copy in sent:
        copy.wait_send()
    for copy in stores:
        copy.wait()


def solution(mesh):
    gx_size, gy_size = mesh.shape["gx"], mesh.shape["gy"]
    scratch = {}
    for l, L in enumerate(LEVELS):
        for name, shape in L.scratch(COARSE_X[l]).items():
            scratch[str(l) + name] = shape
    scratch["xp"] = pltpu.VMEM((2, 2, 4, 2, 32, 128), BF16)
    scratch["xr"] = pltpu.VMEM((2, 2, 4, 2, 32, 128), BF16)
    scratch["yp"] = pltpu.VMEM((2, 2, 8, 16, 128), BF16)
    scratch["yr"] = pltpu.VMEM((2, 2, 12, 16, 128), BF16)
    scratch["mp"] = pltpu.VMEM((256, 128), BF16)
    scratch["ms"] = pltpu.VMEM((gy_size, 48, 128), BF16)
    scratch["mm"] = pltpu.VMEM((gy_size, 48, 128), BF16)
    scratch["mine"] = pltpu.VMEM((8, 128), F32)
    scratch["all"] = pltpu.VMEM((gy_size, 8, 128), F32)
    scratch["corr"] = pltpu.VMEM((5, 24, 128), F32)
    scratch["result"] = pltpu.VMEM((16, 2, 48, 128), F32)
    scratch["local"] = pltpu.SemaphoreType.DMA((4,))
    line = gy_size - 1
    counts = dict(
        fine=8, kappa_1=8, kappa_2=14, matrix=line, source_1=8, smooth_0=8, source_2=14, smooth_1=8,
        gather=line, smooth_2=14, coarse=4,
    )
    for name, count in counts.items():
        scratch["send_" + name] = pltpu.SemaphoreType.DMA((count,))
        scratch["recv_" + name] = pltpu.SemaphoreType.DMA((count,))

    def local(pressure_source, conductance, coarse_inverse):
        return pl.pallas_call(
            functools.partial(kernel, gx_size, gy_size, tuple(scratch)),
            out_shape=jax.ShapeDtypeStruct(pressure_source.shape, F32),
            in_specs=[
                pl.BlockSpec(memory_space=pl.ANY),
                pl.BlockSpec(memory_space=pl.ANY),
                pl.BlockSpec(memory_space=pltpu.VMEM),
            ],
            out_specs=pl.BlockSpec(memory_space=pl.ANY),
            scratch_shapes=list(scratch.values()),
            compiler_params=pltpu.CompilerParams(
                collective_id=0, has_side_effects=True, vmem_limit_bytes=56 * 2**20
            ),
        )(pressure_source, conductance, coarse_inverse)

    in_specs = (P("gx", "gy", None), P("gx", "gy", None), P("gx", "gy", None, None))
    return jax.shard_map(local, mesh=mesh, in_specs=in_specs, out_specs=P("gx", "gy", None), check_vma=False)
```

```python
import functools

import jax
import jax.numpy as jnp
from jax import lax
from jax.experimental import pallas as pl
from jax.experimental.pallas import tpu as pltpu
from jax.sharding import PartitionSpec as P

MESH = pl.DeviceIdType.MESH

LMAX = 2.0
LMIN = 0.25
THETA = 0.5 * (LMAX + LMIN)
DELTA = 0.5 * (LMAX - LMIN)
SIGMA = THETA / DELTA
RATIO_0 = 1.0 / SIGMA
RATIO_1 = 1.0 / (2.0 * SIGMA - RATIO_0)
RATIO_2 = 1.0 / (2.0 * SIGMA - RATIO_1)
STEP_1 = (RATIO_1 * RATIO_0, 2.0 * RATIO_1 / DELTA)
STEP_2 = (RATIO_2 * RATIO_1, 2.0 * RATIO_2 / DELTA)

F32 = jnp.float32
BF16 = jnp.bfloat16

AROUND = [(a, b) for a in (-1, 0, 1) for b in (-1, 0, 1) if (a, b) != (0, 0)]
WIDE = [(a, b) for a in (-2, -1, 0, 1, 2) for b in (-1, 0, 1) if (a, b) != (0, 0)]


class Level:
    def __init__(self, nx, ny, X, x0, R, J, hold, row0, erow, xc, most):
        self.nx, self.ny, self.X, self.x0, self.R, self.J = nx, ny, X, x0, R, J
        self.hold, self.row0, self.erow, self.xc = hold, row0, erow, xc
        self.rows, self.most = 16 + ny, most

    def scratch(self, coarse_x):
        X, R, J = self.X, self.R, self.J
        vm = lambda *shape: pltpu.VMEM(shape + (128,), F32)
        return dict(
            NS=vm(X, R, self.rows),
            NK=vm(X, R, self.rows),
            NV=vm(X, R, self.rows),
            SV=vm(self.nx + 2, R, self.rows),
            RN=vm(self.nx, R, self.rows),
            E=vm(coarse_x, R, 2 * (self.ny // 2 + 16) if self.nx > 4 else 24),
            HK=vm(X, R, J + 2, 8),
            CX=vm(X + 1, R, J, 8),
            CY=vm(X, R, J + 1, 8),
            CM=vm(X, R, J, 8),
            CP=vm(X, R, J, 8),
            Q=vm(X, R, J, 8),
            G=vm(X, R, J, 8),
            D=vm(X, R, J, 8),
            DIR=vm(X, R, J, 8),
            VA=vm(X, R, J + 2, 8),
            VB=vm(X, R, J + 2, 8),
        )


LEVELS = (
    Level(16, 32, 24, 4, 2, 5, 1, 4, 12, 6, 6),
    Level(8, 16, 24, 8, 1, 4, 1, 0, 8, 4, 16),
    Level(4, 8, 20, 8, 1, 3, 2, 0, 0, 0, 16),
)
COARSE_X = (24, 20, 10)


def lanes():
    return lax.broadcasted_iota(jnp.int32, (8, 128), 1)


def sublanes():
    return lax.broadcasted_iota(jnp.int32, (8, 128), 0)


def turn(value, shift, axis):
    return pltpu.roll(value, shift % value.shape[axis], axis)


def pick(value, index):
    return jnp.take_along_axis(value, index, axis=1, mode="promise_in_bounds")


def rows_of(L, j):
    return pl.ds(L.row0 + j, 8, stride=L.J)


def beside_z(L, parts):
    h = L.hold
    down = [turn(p, h, 1) for p in parts]
    up = [turn(p, -h, 1) for p in parts]
    if L.R == 2:
        lane = lanes()
        down[1] = jnp.where(lane == 0, down[0], down[1])
        up[0] = jnp.where(lane == 127, up[1], up[0])
    return down, up


def store_wrapped(ref, x, r, J, values):
    for j in range(J):
        ref[x, r, j + 1] = values[j]
    ref[x, r, 0] = turn(values[J - 1], 1, 0)
    ref[x, r, J + 1] = turn(values[0], -1, 0)


def loop(lo, hi, body, most=1):
    count = hi - lo
    U = max(u for u in range(1, most + 1) if count % u == 0)
    if U == count:
        body(lo, U)
        return

    def step(i, carry):
        body(lo + i * U, U)
        return carry

    lax.fori_loop(0, count // U, step, 0)


def prepare(L, M, lo, hi, gx, gy, count_x, count_y):
    J, R = L.J, L.R
    sub, lane = sublanes(), lanes()
    first = gy * L.ny - 8 + L.row0
    keep = []
    for j in range(J):
        place = first + j + J * sub
        keep.append(jnp.where((place >= 0) & (place < L.ny * count_y), 0.5, 0.0).astype(F32))

    def halves(x, U):
        NK, HK = M["NK"].at[pl.ds(x, U)], M["HK"].at[pl.ds(x, U)]
        for u in range(U):
            place = gx * L.nx + x + u - L.x0
            inside = jnp.where((place >= 0) & (place < L.nx * count_x), 1.0, 0.0).astype(F32)
            for r in range(R):
                store_wrapped(HK, u, r, J, [NK[u, r, rows_of(L, j), :] * (keep[j] * inside) for j in range(J)])

    loop(lo - 1, hi + 1, halves, L.most)
    for r in range(R):
        for j in range(J):
            M["CX"][lo, r, j] = M["HK"][lo - 1, r, j + 1] + M["HK"][lo, r, j + 1]

    def couple(x, U):
        HK, CX = M["HK"].at[pl.ds(x - 1, U + 2)], M["CX"].at[pl.ds(x, U + 1)]
        CY, CM, CP, D, Q = (M[name].at[pl.ds(x, U)] for name in ("CY", "CM", "CP", "D", "Q"))
        for u in range(U):
            for j in range(J):
                mine = [HK[u + 1, r, j + 1] for r in range(R)]
                down, up = beside_z(L, mine)
                down[0] = jnp.where(lane < L.hold, 0.0, down[0])
                up[R - 1] = jnp.where(lane >= 128 - L.hold, 0.0, up[R - 1])
                for r in range(R):
                    h = mine[r]
                    xm, xp = HK[u, r, j + 1], HK[u + 2, r, j + 1]
                    ym, yp = HK[u + 1, r, j], HK[u + 1, r, j + 2]
                    diagonal = (xm + xp) + (ym + yp) + (down[r] + up[r]) + 6.0 * h
                    CX[u + 1, r, j] = h + xp
                    CY[u, r, j] = h + ym
                    if j == J - 1:
                        CY[u, r, J] = h + yp
                    low, high = h + down[r], h + up[r]
                    if r == 0:
                        low = jnp.where(lane < L.hold, 0.0, low)
                    if r == R - 1:
                        high = jnp.where(lane >= 128 - L.hold, 0.0, high)
                    CM[u, r, j] = low
                    CP[u, r, j] = high
                    D[u, r, j] = diagonal
                    Q[u, r, j] = jnp.where(h > 0.0, 1.0 / diagonal, 0.0)

    loop(lo, hi, couple, L.most)


def scale_source(L, M, lo, hi, start):
    J = L.J

    def body(x, U):
        Q, NS, G, VA = (M[name].at[pl.ds(x, U)] for name in ("Q", "NS", "G", "VA"))
        for u in range(U):
            for r in range(L.R):
                values = []
                for j in range(J):
                    g = Q[u, r, j] * NS[u, r, rows_of(L, j), :]
                    G[u, r, j] = g
                    values.append(g * (1.0 / THETA))
                if start:
                    store_wrapped(VA, u, r, J, values)

    loop(lo, hi, body, L.most)


def sweep(L, M, src, dst, lo, hi, kind, step=None, keep_rows=None, emit=None):
    J, R = L.J, L.R

    def body(x, U):
        V, CX = M[src].at[pl.ds(x - 1, U + 2)], M["CX"].at[pl.ds(x, U + 1)]
        CY, CM, CP, D, Q, G, DIR = (M[name].at[pl.ds(x, U)] for name in ("CY", "CM", "CP", "D", "Q", "G", "DIR"))
        if dst is not None:
            W = M[dst].at[pl.ds(x, U)]
        if kind == "residual":
            RN = M["RN"].at[pl.ds(x - L.x0, U)]
        if keep_rows is not None:
            kept = keep_rows.at[pl.ds(x - L.x0 + 1, U)]
        for u in range(U):
            new = [[None] * J for _ in range(R)]
            for j in range(J):
                mine = [V[u + 1, r, j + 1] for r in range(R)]
                down, up = beside_z(L, mine)
                for r in range(R):
                    c = mine[r]
                    near = CX[u, r, j] * V[u, r, j + 1] + CX[u + 1, r, j] * V[u + 2, r, j + 1]
                    near = near + (CY[u, r, j] * V[u + 1, r, j] + CY[u, r, j + 1] * V[u + 1, r, j + 2])
                    near = near + (CM[u, r, j] * down[r] + CP[u, r, j] * up[r])
                    update = (G[u, r, j] - c) + Q[u, r, j] * near
                    if kind == "residual":
                        RN[u, r, rows_of(L, j), :] = D[u, r, j] * update
                        continue
                    if kind == "first":
                        direction = update * (1.0 / THETA)
                    elif kind == "from_zero":
                        direction = step[0] * c + step[1] * update
                    else:
                        direction = step[0] * DIR[u, r, j] + step[1] * update
                    if kind != "last":
                        DIR[u, r, j] = direction
                    new[r][j] = c + direction
            if kind == "residual":
                continue
            for r in range(R):
                if dst is not None:
                    store_wrapped(W, u, r, J, new[r])
                if keep_rows is not None:
                    for j in range(J):
                        kept[u, r, rows_of(L, j), :] = new[r][j]
            if emit is not None:
                emit(x + u, new)

    loop(lo, hi, body, L.most)


def descend(L, M):
    lo, hi = L.x0, L.x0 + L.nx
    sweep(L, M, "VA", "VB", lo - 2, hi + 2, "from_zero", STEP_1)
    sweep(L, M, "VB", "VA", lo - 1, hi + 1, "last", STEP_2, keep_rows=M["SV"])
    sweep(L, M, "VA", None, lo, hi, "residual")


def ascend(L, M, margin, emit):
    lo, hi = L.x0, L.x0 + L.nx

    def begin(x, U):
        NV, HK, VA = (M[name].at[pl.ds(x, U)] for name in ("NV", "HK", "VA"))
        for u in range(U):
            xc = lax.shift_right_logical(x + u, 1) + L.xc
            for r in range(L.R):
                values = []
                for j in range(L.J):
                    added = M["E"][xc, r, pl.ds(L.erow + j, 8, stride=L.J), :]
                    total = NV[u, r, rows_of(L, j), :] + added
                    values.append(jnp.where(HK[u, r, j + 1] > 0.0, total, 0.0))
                store_wrapped(VA, u, r, L.J, values)

    loop(lo - margin, hi + margin, begin, L.most)
    margin -= 1
    sweep(L, M, "VA", "VB", lo - margin, hi + margin, "first")
    margin -= 1
    sweep(L, M, "VB", "VA", lo - margin, hi + margin, "next", STEP_1)
    margin -= 1
    sweep(L, M, "VA", None, lo - margin, hi + margin, "last", STEP_2, emit=emit)


def coarsen(L, src, sx0, scale, put):
    lane = lanes()
    even = (lane * 2) & 127

    def body(x, U):
        pairs = src.at[pl.ds(sx0 + 2 * x, 2 * U)]
        for u, t in [(u, t) for u in range(U) for t in range(max(1, L.ny // 16))]:
            sums = []
            for r in range(L.R):
                rows = [pairs[2 * u + dx, r, pl.ds(8 + 16 * t + b, 8, stride=2), :] for dx in (0, 1) for b in (0, 1)]
                total = (rows[0] + rows[1]) + (rows[2] + rows[3])
                if L.R == 2:
                    sums.append(pick(total + turn(total, -1, 1), even))
                else:
                    other = jnp.where((lane & L.hold) == 0, turn(total, -L.hold, 1), turn(total, L.hold, 1))
                    sums.append(total + other)
            value = jnp.where(lane < 64, sums[0], sums[1]) if L.R == 2 else sums[0]
            put(x + u, t, value * scale)

    return body


def coarsen_into(L, src, sx0, scale, nxt, dst):
    def put(x, t, value):
        dst[nxt.x0 + x, 0, 8 + 8 * t : 16 + 8 * t, :] = value

    loop(0, L.nx // 2, coarsen(L, src, sx0, scale, put), 4)


def kernel(gx_size, gy_size, names, source, conductance, inverse, out, *refs):
    S = dict(zip(names, refs))
    M = [{k[1:]: v for k, v in S.items() if k[0] == str(l)} for l in range(3)]
    gx, gy = lax.axis_index("gx"), lax.axis_index("gy")
    L0, L1, L2 = LEVELS

    def device(a, b):
        return {"gx": lax.rem(gx + a + gx_size, gx_size), "gy": lax.rem(gy + b + gy_size, gy_size)}

    def remote(src, dst, name, n, a, b):
        return pltpu.make_async_remote_copy(
            src_ref=src,
            dst_ref=dst,
            send_sem=S["send_" + name].at[n],
            recv_sem=S["recv_" + name].at[n],
            device_id=device(a, b),
            device_id_type=MESH,
        )

    def exchange(L, src, sx0, dst, width, where, name):
        copies = []
        for n, (a, b) in enumerate(where):
            if a == 0:
                xs, xd, wx = sx0, L.x0, L.nx
            elif abs(a) == 2:
                xs, xd, wx = sx0, L.x0 - (a // 2) * 2 * L.nx, L.nx
            elif a == 1:
                xs, xd, wx = sx0 + L.nx - width, L.x0 - width, width
            else:
                xs, xd, wx = sx0, L.x0 + L.nx, width
            if b == 0:
                ys, yd, wy = 8, 8, L.ny
            elif b == 1:
                ys, yd, wy = L.ny, 0, 8
            else:
                ys, yd, wy = 8, 8 + L.ny, 8
            copies.append(
                remote(
                    src.at[pl.ds(xs, wx), :, pl.ds(ys, wy), :],
                    dst.at[pl.ds(xd, wx), :, pl.ds(yd, wy), :],
                    name,
                    n,
                    a,
                    b,
                )
            )
        for copy in copies:
            copy.start()
        return copies

    def arrive(copies):
        for copy in copies:
            copy.wait_recv()

    sent = []

    peers = list(WIDE) + [(0, b) for b in range(2, gy_size - 1)]
    barrier = pltpu.get_barrier_semaphore()
    for a, b in peers:
        pl.semaphore_signal(barrier, inc=1, device_id=device(a, b), device_id_type=MESH)

    loads = []
    for n, (src, dst) in enumerate(((conductance, M[0]["NK"]), (source, M[0]["NS"]))):
        for r in range(2):
            copy = pltpu.make_async_copy(
                src.at[:, :, pl.ds(128 * r, 128)],
                dst.at[pl.ds(4, 16), r, pl.ds(8, 32), :],
                S["local"].at[2 * n + r],
            )
            copy.start()
            loads.append(copy)
    for copy in loads:
        copy.wait()

    sub, lane = sublanes(), lanes()
    XP, YP, XR, YR = S["xp"], S["yp"], S["xr"], S["yr"]
    fields = (M[0]["NK"], M[0]["NS"])

    def pack_x(i, _):
        for a in range(2):
            for r in range(2):
                XP[0, a, i, r] = fields[a][4 + i, r, 8:40, :].astype(BF16)
                XP[1, a, i, r] = fields[a][16 + i, r, 8:40, :].astype(BF16)

    loop(0, 4, pack_x)

    def pack_y(i, _):
        for a in range(2):
            low, high = [], []
            for d in range(2):
                x = 4 + 2 * i + d
                near, far = fields[a][x, 0, 8:16, :], fields[a][x, 1, 8:16, :]
                low.append(jnp.where(sub < 4, near, turn(far, 4, 0)))
                near, far = fields[a][x, 0, 32:40, :], fields[a][x, 1, 32:40, :]
                high.append(jnp.where(sub < 4, turn(near, 4, 0), far))
            YP[0, a, i] = jnp.concatenate(low, axis=0).astype(BF16)
            YP[1, a, i] = jnp.concatenate(high, axis=0).astype(BF16)

    loop(0, 8, pack_y)

    pl.semaphore_wait(barrier, len(peers))

    fine = []
    for n, (a, b) in enumerate(AROUND):
        if b == 0:
            fine.append(remote(XP.at[(a + 1) // 2], XR.at[(1 - a) // 2], "fine", n, a, b))
        else:
            xs, xd, wx = {0: (0, 2, 8), 1: (6, 0, 2), -1: (0, 10, 2)}[a]
            fine.append(
                remote(
                    YP.at[(b + 1) // 2, :, pl.ds(xs, wx)],
                    YR.at[(1 - b) // 2, :, pl.ds(xd, wx)],
                    "fine",
                    n,
                    a,
                    b,
                )
            )
    for copy in fine:
        copy.start()
    sent += fine

    coarsen_into(L0, M[0]["NK"], 4, 0.125, L1, M[1]["NK"])
    kappa_1 = exchange(L1, M[1]["NK"], 8, M[1]["NK"], 6, AROUND, "kappa_1")
    coarsen_into(L1, M[1]["NK"], 8, 0.125, L2, M[2]["NK"])
    kappa_2 = exchange(L2, M[2]["NK"], 8, M[2]["NK"], 4, WIDE, "kappa_2")
    sent += kappa_1 + kappa_2

    one = lambda mask: jnp.where(mask, 1.0, 0.0).astype(BF16)
    row = lax.broadcasted_iota(jnp.int32, (128, 128), 0)
    column = lax.broadcasted_iota(jnp.int32, (128, 128), 1)
    order = one(row == ((column >> 2) & 1) * 64 + (column >> 3) * 4 + (column & 3))
    for k in range(2):
        S["mp"][128 * k : 128 * (k + 1), :] = jnp.dot(
            inverse[0, k], order, preferred_element_type=F32
        ).astype(BF16)

    row = lax.broadcasted_iota(jnp.int32, (48, 256), 0)
    column = lax.broadcasted_iota(jnp.int32, (48, 256), 1)
    layer = jnp.where(row >= 24, 1, 0)
    row = row - 24 * layer
    half = jnp.where(row >= 12, 1, 0)
    row = row - 12 * half
    base = layer * 128 + half * 64

    def share(d, _):
        chosen = one(column == base + ((row + (4 * d + 60)) & 63))
        S["ms"][d] = jnp.dot(chosen, S["mp"][...], preferred_element_type=F32).astype(BF16)

    loop(0, gy_size, share)
    matrices = []
    for n in range(gy_size - 1):
        there = lax.rem(gy + n + 1, gy_size)
        matrices.append(remote(S["ms"].at[there], S["mm"].at[gy], "matrix", n, 0, n + 1))
    for copy in matrices:
        copy.start()
    sent += matrices
    S["mm"][gy] = S["ms"][gy]

    arrive(fine)

    def unpack_x(i, _):
        for a in range(2):
            for r in range(2):
                fields[a][i, r, 8:40, :] = XR[0, a, i, r].astype(F32)
                fields[a][20 + i, r, 8:40, :] = XR[1, a, i, r].astype(F32)

    loop(0, 4, unpack_x)

    def unpack_y(i, _):
        for a in range(2):
            low, high = YR[0, a, i].astype(F32), YR[1, a, i].astype(F32)
            for d in range(2):
                x = 2 * i + d
                part = low[8 * d : 8 * d + 8]
                fields[a][x, 0, 0:8, :] = turn(part, 4, 0)
                fields[a][x, 1, 0:8, :] = part
                part = high[8 * d : 8 * d + 8]
                fields[a][x, 0, 40:48, :] = part
                fields[a][x, 1, 40:48, :] = turn(part, 4, 0)

    loop(0, 12, unpack_y)

    place = (gx, gy, gx_size, gy_size)
    prepare(L0, M[0], 1, 23, *place)
    scale_source(L0, M[0], 1, 23, True)
    descend(L0, M[0])
    coarsen_into(L0, M[0]["RN"], 0, 0.5, L1, M[1]["NS"])
    source_1 = exchange(L1, M[1]["NS"], 8, M[1]["NS"], 4, AROUND, "source_1")
    smooth_0 = exchange(L0, M[0]["SV"], 1, M[0]["NV"], 3, AROUND, "smooth_0")
    sent += source_1 + smooth_0

    arrive(kappa_1)
    prepare(L1, M[1], 3, 21, *place)
    arrive(source_1)
    scale_source(L1, M[1], 4, 20, True)
    descend(L1, M[1])
    coarsen_into(L1, M[1]["RN"], 0, 0.5, L2, M[2]["NS"])
    source_2 = exchange(L2, M[2]["NS"], 8, M[2]["NS"], 4, WIDE, "source_2")
    smooth_1 = exchange(L1, M[1]["SV"], 1, M[1]["NV"], 5, AROUND, "smooth_1")
    sent += source_2 + smooth_1

    arrive(kappa_2)
    prepare(L2, M[2], 3, 17, *place)
    arrive(source_2)
    scale_source(L2, M[2], 3, 17, True)
    descend(L2, M[2])
    tiles = []
    make = coarsen(L2, M[2]["RN"], 0, 1.0 / 128.0, lambda x, t, value: tiles.append(value))
    make(0, 2)
    rounded = jnp.where(sub < 4, tiles[0], turn(tiles[1], 4, 0)).astype(BF16).astype(F32)
    S["mine"][...] = rounded
    gathered = []
    for n in range(gy_size - 1):
        gathered.append(remote(S["mine"], S["all"].at[gy], "gather", n, 0, n + 1))
    for copy in gathered:
        copy.start()
    smooth_2 = exchange(L2, M[2]["SV"], 1, M[2]["NV"], 4, WIDE, "smooth_2")
    sent += gathered + smooth_2
    S["all"][gy] = rounded

    kept = []
    for l, L in enumerate(LEVELS):
        copy = pltpu.make_async_copy(
            M[l]["SV"].at[pl.ds(1, L.nx), :, pl.ds(8, L.ny), :],
            M[l]["NV"].at[pl.ds(L.x0, L.nx), :, pl.ds(8, L.ny), :],
            S["local"].at[l],
        )
        copy.start()
        kept.append(copy)
    for copy in kept:
        copy.wait()

    arrive(matrices)
    arrive(gathered)
    right = S["all"][...].reshape(gy_size * 8, 128).astype(BF16)
    layer_of = lax.broadcasted_iota(jnp.int32, (24, 128), 1) >> 2

    def solve(d, total):
        product = jnp.dot(S["mm"][d], right, preferred_element_type=F32)
        total = total + jnp.where(layer_of == 2 * d, product[:24], 0.0)
        return total + jnp.where(layer_of == 2 * d + 1, product[24:], 0.0)

    S["corr"][2] = lax.fori_loop(0, gy_size, solve, jnp.zeros((24, 128), F32))
    coarse = []
    for n, a in enumerate((-2, -1, 1, 2)):
        coarse.append(remote(S["corr"].at[2], S["corr"].at[2 - a], "coarse", n, a, 0))
    for copy in coarse:
        copy.start()
    sent += coarse
    arrive(smooth_2)
    arrive(coarse)

    for slab in range(5):
        for d in range(2):
            for b in range(2):
                M[2]["E"][2 * slab + d, 0, pl.ds(b, 8, stride=2), :] = S["corr"][slab, 12 * d : 12 * d + 8, :]
                M[2]["E"][2 * slab + d, 0, pl.ds(16 + b, 4, stride=2), :] = S["corr"][slab, 12 * d + 8 : 12 * d + 12, :]

    def emit_2(x, new):
        for j in range(L2.J):
            for b in range(2):
                M[1]["E"][x, 0, pl.ds(2 * j + b, 8, stride=2 * L2.J), :] = new[0][j]

    def emit_1(x, new):
        for j in range(L1.J):
            for r in range(2):
                value = pick(new[0][j], (lane >> 1) + 64 * r)
                for b in range(2):
                    M[0]["E"][x, r, pl.ds(2 * j + b, 8, stride=2 * L1.J), :] = value

    def emit_0(x, new):
        for r in range(2):
            for j in range(L0.J):
                S["result"][x - L0.x0, r, rows_of(L0, j), :] = new[r][j]

    ascend(L2, M[2], 6, emit_2)
    arrive(smooth_1)
    ascend(L1, M[1], 5, emit_1)
    arrive(smooth_0)
    ascend(L0, M[0], 3, emit_0)

    stores = []
    for r in range(2):
        copy = pltpu.make_async_copy(
            S["result"].at[:, r, pl.ds(8, 32), :], out.at[:, :, pl.ds(128 * r, 128)], S["local"].at[r]
        )
        copy.start()
        stores.append(copy)
    for copy in sent:
        copy.wait_send()
    for copy in stores:
        copy.wait()


def solution(mesh):
    gx_size, gy_size = mesh.shape["gx"], mesh.shape["gy"]
    scratch = {}
    for l, L in enumerate(LEVELS):
        for name, shape in L.scratch(COARSE_X[l]).items():
            scratch[str(l) + name] = shape
    scratch["xp"] = pltpu.VMEM((2, 2, 4, 2, 32, 128), BF16)
    scratch["xr"] = pltpu.VMEM((2, 2, 4, 2, 32, 128), BF16)
    scratch["yp"] = pltpu.VMEM((2, 2, 8, 16, 128), BF16)
    scratch["yr"] = pltpu.VMEM((2, 2, 12, 16, 128), BF16)
    scratch["mp"] = pltpu.VMEM((256, 128), BF16)
    scratch["ms"] = pltpu.VMEM((gy_size, 48, 128), BF16)
    scratch["mm"] = pltpu.VMEM((gy_size, 48, 128), BF16)
    scratch["mine"] = pltpu.VMEM((8, 128), F32)
    scratch["all"] = pltpu.VMEM((gy_size, 8, 128), F32)
    scratch["corr"] = pltpu.VMEM((5, 24, 128), F32)
    scratch["result"] = pltpu.VMEM((16, 2, 48, 128), F32)
    scratch["local"] = pltpu.SemaphoreType.DMA((4,))
    line = gy_size - 1
    counts = dict(
        fine=8, kappa_1=8, kappa_2=14, matrix=line, source_1=8, smooth_0=8, source_2=14, smooth_1=8,
        gather=line, smooth_2=14, coarse=4,
    )
    for name, count in counts.items():
        scratch["send_" + name] = pltpu.SemaphoreType.DMA((count,))
        scratch["recv_" + name] = pltpu.SemaphoreType.DMA((count,))

    def local(pressure_source, conductance, coarse_inverse):
        return pl.pallas_call(
            functools.partial(kernel, gx_size, gy_size, tuple(scratch)),
            out_shape=jax.ShapeDtypeStruct(pressure_source.shape, F32),
            in_specs=[
                pl.BlockSpec(memory_space=pl.ANY),
                pl.BlockSpec(memory_space=pl.ANY),
                pl.BlockSpec(memory_space=pltpu.VMEM),
            ],
            out_specs=pl.BlockSpec(memory_space=pl.ANY),
            scratch_shapes=list(scratch.values()),
            compiler_params=pltpu.CompilerParams(
                collective_id=0, has_side_effects=True, vmem_limit_bytes=56 * 2**20
            ),
        )(pressure_source, conductance, coarse_inverse)

    in_specs = (P("gx", "gy", None), P("gx", "gy", None), P("gx", "gy", None, None))
    return jax.shard_map(local, mesh=mesh, in_specs=in_specs, out_specs=P("gx", "gy", None), check_vma=False)
```

```python
import functools
import math

import jax
import jax.numpy as jnp
from jax import lax
from jax.experimental import pallas as pl
from jax.experimental.pallas import tpu as pltpu
from jax.sharding import PartitionSpec as P

MESH = pl.DeviceIdType.MESH

LMAX = 2.0
LMIN = 0.25
THETA = 0.5 * (LMAX + LMIN)
DELTA = 0.5 * (LMAX - LMIN)
SIGMA = THETA / DELTA
RATIO_0 = 1.0 / SIGMA
RATIO_1 = 1.0 / (2.0 * SIGMA - RATIO_0)
RATIO_2 = 1.0 / (2.0 * SIGMA - RATIO_1)
STEP_1 = (RATIO_1 * RATIO_0, 2.0 * RATIO_1 / DELTA)
STEP_2 = (RATIO_2 * RATIO_1, 2.0 * RATIO_2 / DELTA)

F32 = jnp.float32
BF16 = jnp.bfloat16

EXCHANGES = (
    "fine", "kappa_1", "kappa_2", "matrix", "source_1", "smooth_0", "source_2", "gather", "smooth_2", "coarse",
)
AROUND = [(a, b) for a in (-1, 0, 1) for b in (-1, 0, 1) if (a, b) != (0, 0)]
WIDE = [(a, b) for a in (-2, -1, 0, 1, 2) for b in (-1, 0, 1) if (a, b) != (0, 0)]


class Level:
    def __init__(self, nx, ny, x0, side, R, J, hold, row0, erow, xc, coarse, most):
        self.nx, self.ny, self.X, self.x0, self.side = nx, ny, nx + 2 * x0, x0, side
        self.R, self.J, self.hold, self.row0, self.most = R, J, hold, row0, most
        self.erow, self.xc, self.coarse = erow, xc, coarse
        self.rows = ny + 2 * side

    def scratch(self):
        X, R, J = self.X, self.R, self.J
        vm = lambda *shape: pltpu.VMEM(shape + (128,), F32)
        blocked = {name: vm(X, R, J, 8) for name in ("CM", "CP", "Q", "G", "D", "DIR")}
        natural = {name: vm(X, R, self.rows) for name in ("NS", "NK", "RN")}
        return dict(
            E=vm(self.coarse[0], R, self.coarse[1]),
            HK=vm(X, R, J + 2, 8),
            CX=vm(X + 1, R, J, 8),
            CY=vm(X, R, J + 1, 8),
            VA=vm(X, R, J + 2, 8),
            VB=vm(X, R, J + 2, 8),
            **blocked,
            **natural,
        )


LEVELS = (
    Level(16, 32, 4, 8, 2, 5, 1, 4, 20, 8, (28, 80), 6),
    Level(8, 16, 10, 16, 1, 5, 1, 4, 4, 3, (20, 48), 12),
    Level(4, 8, 8, 8, 1, 3, 2, 0, 0, 0, (10, 24), 16),
)


def lanes(*lead):
    return lax.broadcasted_iota(jnp.int32, lead + (8, 128), len(lead) + 1)


def sublanes():
    return lax.broadcasted_iota(jnp.int32, (8, 128), 0)


def turn(value, shift, axis):
    return pltpu.roll(value, shift % value.shape[axis], axis)


def pick(value, index):
    return jnp.take_along_axis(value, index, axis=1, mode="promise_in_bounds")


def rows_of(L, j):
    return pl.ds(L.row0 + j, 8, stride=L.J)


def beside_z(L, parts):
    h = L.hold
    down = [turn(p, h, 2) for p in parts]
    up = [turn(p, -h, 2) for p in parts]
    if L.R == 2:
        lane = lanes(L.J)
        down[1] = jnp.where(lane == 0, down[0], down[1])
        up[0] = jnp.where(lane == 127, up[1], up[0])
    return down, up


def store_wrapped(ref, x, r, J, values):
    ref[x, r, 1 : J + 1] = values
    ref[x, r, 0] = turn(values[J - 1], 1, 0)
    ref[x, r, J + 1] = turn(values[0], -1, 0)


def rows_from(L, ref, x, r):
    return jnp.stack([ref[x, r, rows_of(L, j), :] for j in range(L.J)])


def rows_to(L, ref, x, r, values):
    for j in range(L.J):
        ref[x, r, rows_of(L, j), :] = values[j]


def loop(lo, hi, body, most=1):
    count = hi - lo
    steps = -(-count // most)
    U = -(-count // steps)
    whole = count // U
    if whole > 1:

        def step(i, carry):
            body(lo + i * U, U)
            return carry

        lax.fori_loop(0, whole, step, 0)
    elif whole == 1:
        body(lo, U)
    if count > whole * U:
        body(lo + whole * U, count - whole * U)


def prepare(L, M, lo, hi, gx, gy, count_x, count_y):
    J, R, h = L.J, L.R, L.hold
    shape = (J, 8, 128)
    lane = lanes(J)
    place = lax.broadcasted_iota(jnp.int32, shape, 0) + J * lax.broadcasted_iota(jnp.int32, shape, 1)
    place = place + (gy * L.ny - L.side + L.row0)
    keep = jnp.where((place >= 0) & (place < L.ny * count_y), 0.5, 0.0).astype(F32)

    def halves(x, U):
        NK, HK = M["NK"].at[pl.ds(x, U)], M["HK"].at[pl.ds(x, U)]
        for u in range(U):
            place = gx * L.nx + x + u - L.x0
            inside = jnp.where((place >= 0) & (place < L.nx * count_x), 1.0, 0.0).astype(F32)
            mask = keep * inside
            for r in range(R):
                store_wrapped(HK, u, r, J, rows_from(L, NK, u, r) * mask)

    loop(lo - 1, hi + 1, halves, L.most)
    for r in range(R):
        M["CX"][lo, r] = M["HK"][lo - 1, r, 1 : J + 1] + M["HK"][lo, r, 1 : J + 1]

    def couple(x, U):
        HK, CX = M["HK"].at[pl.ds(x - 1, U + 2)], M["CX"].at[pl.ds(x, U + 1)]
        CY, CM, CP, D, Q = (M[name].at[pl.ds(x, U)] for name in ("CY", "CM", "CP", "D", "Q"))
        for u in range(U):
            mine = [HK[u + 1, r, 1 : J + 1] for r in range(R)]
            down, up = beside_z(L, mine)
            down[0] = jnp.where(lane < h, 0.0, down[0])
            up[R - 1] = jnp.where(lane >= 128 - h, 0.0, up[R - 1])
            for r in range(R):
                c = mine[r]
                xm, xp = HK[u, r, 1 : J + 1], HK[u + 2, r, 1 : J + 1]
                ym, yp = HK[u + 1, r, 0:J], HK[u + 1, r, 2 : J + 2]
                diagonal = (xm + xp) + (ym + yp) + (down[r] + up[r]) + 6.0 * c
                CX[u + 1, r] = c + xp
                CY[u, r, 0:J] = c + ym
                CY[u, r, J] = c[J - 1] + yp[J - 1]
                low, high = c + down[r], c + up[r]
                if r == 0:
                    low = jnp.where(lane < h, 0.0, low)
                if r == R - 1:
                    high = jnp.where(lane >= 128 - h, 0.0, high)
                CM[u, r] = low
                CP[u, r] = high
                D[u, r] = diagonal
                Q[u, r] = jnp.where(c > 0.0, 1.0 / diagonal, 0.0)

    loop(lo, hi, couple, L.most)


def scale_source(L, M, name, lo, hi, start):
    J, field = L.J, M[name]

    def body(x, U):
        Q, G, VA, NS = (ref.at[pl.ds(x, U)] for ref in (M["Q"], M["G"], M["VA"], field))
        for u in range(U):
            for r in range(L.R):
                g = Q[u, r] * rows_from(L, NS, u, r)
                G[u, r] = g
                if start:
                    store_wrapped(VA, u, r, J, g * (1.0 / THETA))

    loop(lo, hi, body, L.most)


def sweep(L, M, src, dst, lo, hi, kind, step=None, keep_rows=None, emit=None):
    J, R = L.J, L.R

    def body(x, U):
        V, CX = M[src].at[pl.ds(x - 1, U + 2)], M["CX"].at[pl.ds(x, U + 1)]
        CY, CM, CP, D, Q, G, DIR = (M[name].at[pl.ds(x, U)] for name in ("CY", "CM", "CP", "D", "Q", "G", "DIR"))
        if dst is not None:
            W = M[dst].at[pl.ds(x, U)]
        if kind == "residual":
            RN = M["RN"].at[pl.ds(x, U)]
        if keep_rows is not None:
            kept = keep_rows.at[pl.ds(x - L.x0 + 1, U)]
        for u in range(U):
            mine = [V[u + 1, r, 1 : J + 1] for r in range(R)]
            down, up = beside_z(L, mine)
            new = []
            for r in range(R):
                c = mine[r]
                near = CX[u, r] * V[u, r, 1 : J + 1] + CX[u + 1, r] * V[u + 2, r, 1 : J + 1]
                near = near + (CY[u, r, 0:J] * V[u + 1, r, 0:J] + CY[u, r, 1 : J + 1] * V[u + 1, r, 2 : J + 2])
                near = near + (CM[u, r] * down[r] + CP[u, r] * up[r])
                update = (G[u, r] - c) + Q[u, r] * near
                if kind == "residual":
                    rows_to(L, RN, u, r, D[u, r] * update)
                    continue
                if kind == "first":
                    direction = update * (1.0 / THETA)
                elif kind == "from_zero":
                    direction = step[0] * c + step[1] * update
                else:
                    direction = step[0] * DIR[u, r] + step[1] * update
                if kind != "last":
                    DIR[u, r] = direction
                value = c + direction
                if dst is not None:
                    store_wrapped(W, u, r, J, value)
                if keep_rows is not None:
                    rows_to(L, kept, u, r, value)
                new.append(value)
            if emit is not None:
                emit(x + u, new)

    loop(lo, hi, body, L.most)


def descend(L, M, margin, keep_rows=None):
    lo, hi = L.x0 - margin, L.x0 + L.nx + margin
    sweep(L, M, "VA", "VB", lo - 2, hi + 2, "from_zero", STEP_1)
    sweep(L, M, "VB", "VA", lo - 1, hi + 1, "last", STEP_2, keep_rows=keep_rows)
    sweep(L, M, "VA", None, lo, hi, "residual")


def ascend(L, M, margin, emit, smoothed=None):
    lo, hi = L.x0, L.x0 + L.nx

    def begin(x, U):
        HK, VA = (M[name].at[pl.ds(x, U)] for name in ("HK", "VA"))
        if smoothed is not None:
            NV = smoothed.at[pl.ds(x, U)]
        for u in range(U):
            xc = lax.shift_right_logical(x + u, 1) + L.xc
            for r in range(L.R):
                added = [M["E"][xc, r, pl.ds(L.erow + j, 8, stride=L.J), :] for j in range(L.J)]
                base = VA[u, r, 1 : L.J + 1] if smoothed is None else rows_from(L, NV, u, r)
                inside = HK[u, r, 1 : L.J + 1] > 0.0
                store_wrapped(VA, u, r, L.J, jnp.where(inside, jnp.stack(added) + base, 0.0))

    loop(lo - margin, hi + margin, begin, L.most)
    margin -= 1
    sweep(L, M, "VA", "VB", lo - margin, hi + margin, "first")
    margin -= 1
    sweep(L, M, "VB", "VA", lo - margin, hi + margin, "next", STEP_1)
    margin -= 1
    sweep(L, M, "VA", None, lo - margin, hi + margin, "last", STEP_2, emit=emit)


def coarsen(L, src, row, tiles, scale, put):
    lane = lanes()
    even = (lane * 2) & 127

    def body(x, U):
        pairs = src.at[pl.ds(2 * x, 2 * U)]
        for u, t in [(u, t) for u in range(U) for t in range(tiles)]:
            sums = []
            for r in range(L.R):
                rows = [pairs[2 * u + dx, r, pl.ds(row + 16 * t + b, 8, stride=2), :] for dx in (0, 1) for b in (0, 1)]
                total = (rows[0] + rows[1]) + (rows[2] + rows[3])
                if L.R == 2:
                    sums.append(pick(total + turn(total, -1, 1), even))
                else:
                    other = jnp.where((lane & L.hold) == 0, turn(total, -L.hold, 1), turn(total, L.hold, 1))
                    sums.append(total + other)
            value = jnp.where(lane < 64, sums[0], sums[1]) if L.R == 2 else sums[0]
            put(x + u, t, value * scale)

    return body


def put_rows(dst, dx, row):
    def put(x, t, value):
        dst[dx + x, 0, row + 8 * t : row + 8 * t + 8, :] = value

    return put


def kernel(gx_size, gy_size, names, source, conductance, inverse, out, *refs):
    S = dict(zip(names, refs))
    M = [{k[1:]: v for k, v in S.items() if k[0] == str(l)} for l in range(3)]
    M[2]["s2"] = S["s2"]
    gx, gy = lax.axis_index("gx"), lax.axis_index("gy")
    L0, L1, L2 = LEVELS

    def device(a, b):
        return {"gx": lax.rem(gx + a + gx_size, gx_size), "gy": lax.rem(gy + b + gy_size, gy_size)}

    class Exchange:
        def __init__(self, name):
            self.out, self.back, self.rows, self.copies = S["send_" + name], S["recv_" + name], 0, []

        def add(self, src, dst, a, b):
            copy = pltpu.make_async_remote_copy(
                src_ref=src, dst_ref=dst, send_sem=self.out, recv_sem=self.back, device_id=device(a, b), device_id_type=MESH
            )
            self.copies.append(copy)
            rows = math.prod(src.shape[:-1])
            self.rows += rows if src.dtype == F32 else rows // 2

        def start(self):
            for copy in self.copies:
                copy.start()
            return self

        def wait(self, semaphore):
            size = S["size"].at[pl.ds(0, self.rows)]
            pltpu.make_async_copy(size, size, semaphore).wait()

        def arrive(self):
            self.wait(self.back)

        def left(self):
            self.wait(self.out)

    def exchange(L, src, sx0, dst, near, far, name):
        both = Exchange(name)
        h = L.side
        for a, b in WIDE if far else AROUND:
            w = {0: L.nx, 1: near, 2: far}[abs(a)]
            xs = sx0 + (L.nx - w if a > 0 else 0)
            xd = {0: L.x0, 1: L.x0 - w, 2: L.x0 - L.nx - w, -1: L.x0 + L.nx, -2: L.x0 + 2 * L.nx}[a]
            ys = h + (L.ny - h if b > 0 else 0)
            yd, wy = {0: (h, L.ny), 1: (0, h), -1: (h + L.ny, h)}[b]
            both.add(src.at[pl.ds(xs, w), :, pl.ds(ys, wy), :], dst.at[pl.ds(xd, w), :, pl.ds(yd, wy), :], a, b)
        return both.start()

    peers = list(WIDE) + [(0, b) for b in range(2, gy_size - 1)]
    barrier = pltpu.get_barrier_semaphore()
    for a, b in peers:
        pl.semaphore_signal(barrier, inc=1, device_id=device(a, b), device_id_type=MESH)

    loads = []
    for n, (src, dst) in enumerate(((conductance, M[0]["NK"]), (source, M[0]["NS"]))):
        for r in range(2):
            copy = pltpu.make_async_copy(
                src.at[:, :, pl.ds(128 * r, 128)],
                dst.at[pl.ds(4, 16), r, pl.ds(8, 32), :],
                S["local"].at[2 * n + r],
            )
            copy.start()
            loads.append(copy)
    for copy in loads:
        copy.wait()

    sub, lane = sublanes(), lanes()
    XP, YP, XR, YR = S["xp"], S["yp"], S["xr"], S["yr"]
    fields = (M[0]["NK"], M[0]["NS"])

    def pack_x(i, _):
        for a in range(2):
            for r in range(2):
                XP[0, a, i, r] = fields[a][4 + i, r, 8:40, :].astype(BF16)
                XP[1, a, i, r] = fields[a][16 + i, r, 8:40, :].astype(BF16)

    loop(0, 4, pack_x)

    def pack_y(i, _):
        for a in range(2):
            low, high = [], []
            for d in range(2):
                x = 4 + 2 * i + d
                near, far = fields[a][x, 0, 8:16, :], fields[a][x, 1, 8:16, :]
                low.append(jnp.where(sub < 4, near, turn(far, 4, 0)))
                near, far = fields[a][x, 0, 32:40, :], fields[a][x, 1, 32:40, :]
                high.append(jnp.where(sub < 4, turn(near, 4, 0), far))
            YP[0, a, i] = jnp.concatenate(low, axis=0).astype(BF16)
            YP[1, a, i] = jnp.concatenate(high, axis=0).astype(BF16)

    loop(0, 8, pack_y)

    pl.semaphore_wait(barrier, len(peers))

    fine = Exchange("fine")
    for a, b in AROUND:
        if b == 0:
            fine.add(XP.at[(a + 1) // 2], XR.at[(1 - a) // 2], a, b)
        else:
            xs, xd, wx = {0: (0, 2, 8), 1: (6, 0, 2), -1: (0, 10, 2)}[a]
            fine.add(YP.at[(b + 1) // 2, :, pl.ds(xs, wx)], YR.at[(1 - b) // 2, :, pl.ds(xd, wx)], a, b)
    fine.start()

    def halve(field, packed):
        packed[10:18, 0, 16:32, :] = field[10:18, 0, 16:32, :].astype(BF16)

    def widen(packed, field):
        def whole(x, U):
            for u in range(U):
                field[x + u, 0] = packed[x + u, 0].astype(F32)

        def ends(x, U):
            for u in range(U):
                for rows in (pl.ds(0, 16), pl.ds(32, 16)):
                    field[x + u, 0, rows, :] = packed[x + u, 0, rows, :].astype(F32)

        loop(0, 10, whole, 5)
        loop(10, 18, ends, 8)
        loop(18, 28, whole, 5)

    loop(0, 8, coarsen(L0, M[0]["NK"].at[pl.ds(4, 16)], 8, 2, 0.125, put_rows(M[1]["NK"], 10, 16)), 4)
    halve(M[1]["NK"], S["k1"])
    kappa_1 = exchange(L1, S["k1"], 10, S["k1"], 8, 2, "kappa_1")
    loop(0, 4, coarsen(L1, M[1]["NK"].at[pl.ds(10, 8)], 16, 1, 0.125, put_rows(M[2]["NK"], 8, 8)), 4)
    kappa_2 = exchange(L2, M[2]["NK"], 8, M[2]["NK"], 4, 4, "kappa_2")

    one = lambda mask: jnp.where(mask, 1.0, 0.0).astype(BF16)
    row = lax.broadcasted_iota(jnp.int32, (128, 128), 0)
    column = lax.broadcasted_iota(jnp.int32, (128, 128), 1)
    order = one(row == ((column >> 2) & 1) * 64 + (column >> 3) * 4 + (column & 3))
    for k in range(2):
        S["mp"][128 * k : 128 * (k + 1), :] = jnp.dot(
            inverse[0, k], order, preferred_element_type=F32
        ).astype(BF16)

    row = lax.broadcasted_iota(jnp.int32, (48, 256), 0)
    column = lax.broadcasted_iota(jnp.int32, (48, 256), 1)
    layer = jnp.where(row >= 24, 1, 0)
    row = row - 24 * layer
    half = jnp.where(row >= 12, 1, 0)
    row = row - 12 * half
    base = layer * 128 + half * 64

    def share(d, _):
        chosen = one(column == base + ((row + (4 * d + 60)) & 63))
        S["ms"][d] = jnp.dot(chosen, S["mp"][...], preferred_element_type=F32).astype(BF16)

    loop(0, gy_size, share)
    matrices = Exchange("matrix")
    for n in range(1, gy_size):
        matrices.add(S["ms"].at[lax.rem(gy + n, gy_size)], S["mm"].at[gy], 0, n)
    matrices.start()
    S["mm"][gy] = S["ms"][gy]

    fine.arrive()

    def unpack_x(i, _):
        for a in range(2):
            for r in range(2):
                fields[a][i, r, 8:40, :] = XR[0, a, i, r].astype(F32)
                fields[a][20 + i, r, 8:40, :] = XR[1, a, i, r].astype(F32)

    loop(0, 4, unpack_x)

    def unpack_y(i, _):
        for a in range(2):
            low, high = YR[0, a, i].astype(F32), YR[1, a, i].astype(F32)
            for d in range(2):
                x = 2 * i + d
                part = low[8 * d : 8 * d + 8]
                fields[a][x, 0, 0:8, :] = turn(part, 4, 0)
                fields[a][x, 1, 0:8, :] = part
                part = high[8 * d : 8 * d + 8]
                fields[a][x, 0, 40:48, :] = part
                fields[a][x, 1, 40:48, :] = turn(part, 4, 0)

    loop(0, 12, unpack_y)

    place = (gx, gy, gx_size, gy_size)
    prepare(L0, M[0], 1, 23, *place)
    scale_source(L0, M[0], "NS", 1, 23, True)
    descend(L0, M[0], 0, S["keep0"])
    residual = M[0]["RN"].at[pl.ds(4, 16)]
    loop(0, 8, coarsen(L0, residual, 8, 2, 0.5, put_rows(M[1]["NS"], 10, 16)), 4)
    halve(M[1]["NS"], S["s1"])
    source_1 = exchange(L1, S["s1"], 10, S["s1"], 8, 2, "source_1")
    smooth_0 = exchange(L0, S["keep0"], 1, S["smooth0"], 3, 0, "smooth_0")

    kappa_1.arrive()
    widen(S["k1"], M[1]["NK"])
    prepare(L1, M[1], 1, 27, *place)
    kappa_2.arrive()
    prepare(L2, M[2], 3, 17, *place)
    source_1.arrive()
    widen(S["s1"], M[1]["NS"])
    scale_source(L1, M[1], "NS", 1, 27, True)
    descend(L1, M[1], 6)

    residual = M[1]["RN"].at[pl.ds(4, 20)]
    loop(0, 10, coarsen(L1, residual, 0, 3, 0.5, put_rows(S["s2"], 5, 0)), 5)
    M[2]["NS"][8:12, :, 8:16, :] = S["s2"][8:12, :, 8:16, :]
    source_2 = exchange(L2, M[2]["NS"], 8, M[2]["NS"], 4, 4, "source_2")
    scale_source(L2, M[2], "s2", 5, 15, True)
    descend(L2, M[2], 0, S["keep2"])
    tiles = []
    residual = M[2]["RN"].at[pl.ds(8, 4)]
    loop(0, 2, coarsen(L2, residual, 8, 1, 1.0 / 128.0, lambda x, t, value: tiles.append(value)), 2)
    rounded = jnp.where(sub < 4, tiles[0], turn(tiles[1], 4, 0)).astype(BF16).astype(F32)
    S["mine"][...] = rounded
    gathered = Exchange("gather")
    for n in range(1, gy_size):
        gathered.add(S["mine"], S["all"].at[gy], 0, n)
    gathered.start()
    smooth_2 = exchange(L2, S["keep2"], 1, S["smooth2"], 4, 4, "smooth_2")
    S["all"][gy] = rounded

    kept = []
    for n, (L, src, dst) in enumerate(((L0, S["keep0"], S["smooth0"]), (L2, S["keep2"], S["smooth2"]))):
        copy = pltpu.make_async_copy(
            src.at[pl.ds(1, L.nx), :, pl.ds(8, L.ny), :],
            dst.at[pl.ds(L.x0, L.nx), :, pl.ds(8, L.ny), :],
            S["local"].at[n],
        )
        copy.start()
        kept.append(copy)
    for old in (fine, kappa_1, kappa_2, matrices, source_1, smooth_0, source_2):
        old.left()
    for copy in kept:
        copy.wait()

    source_2.arrive()
    scale_source(L2, M[2], "NS", 3, 17, False)
    matrices.arrive()
    gathered.arrive()
    right = S["all"][...].reshape(gy_size * 8, 128).astype(BF16)
    layer_of = lax.broadcasted_iota(jnp.int32, (24, 128), 1) >> 2

    def solve(d, total):
        product = jnp.dot(S["mm"][d], right, preferred_element_type=F32)
        total = total + jnp.where(layer_of == 2 * d, product[:24], 0.0)
        return total + jnp.where(layer_of == 2 * d + 1, product[24:], 0.0)

    S["corr"][2] = lax.fori_loop(0, gy_size, solve, jnp.zeros((24, 128), F32))
    coarse = Exchange("coarse")
    for a in (-2, -1, 1, 2):
        coarse.add(S["corr"].at[2], S["corr"].at[2 - a], a, 0)
    coarse.start()
    gathered.left()
    smooth_2.left()
    smooth_2.arrive()
    smooth_0.arrive()
    coarse.arrive()

    for slab in range(5):
        for d in range(2):
            for b in range(2):
                M[2]["E"][2 * slab + d, 0, pl.ds(b, 8, stride=2), :] = S["corr"][slab, 12 * d : 12 * d + 8, :]
                M[2]["E"][2 * slab + d, 0, pl.ds(16 + b, 4, stride=2), :] = S["corr"][slab, 12 * d + 8 : 12 * d + 12, :]

    def emit_2(x, new):
        for j in range(L2.J):
            for b in range(2):
                M[1]["E"][x, 0, pl.ds(2 * j + b, 8, stride=2 * L2.J), :] = new[0][j]

    def emit_1(x, new):
        for j in range(L1.J):
            for r in range(2):
                value = pick(new[0][j], (lane >> 1) + 64 * r)
                for b in range(2):
                    M[0]["E"][x, r, pl.ds(2 * j + b, 8, stride=2 * L1.J), :] = value

    def emit_0(x, new):
        for r in range(2):
            for j in range(L0.J):
                S["result"][x - L0.x0, r, rows_of(L0, j), :] = new[r][j]

    ascend(L2, M[2], 6, emit_2, S["smooth2"])
    ascend(L1, M[1], 5, emit_1)
    ascend(L0, M[0], 3, emit_0, S["smooth0"])

    stores = []
    for r in range(2):
        copy = pltpu.make_async_copy(
            S["result"].at[:, r, pl.ds(8, 32), :], out.at[:, :, pl.ds(128 * r, 128)], S["local"].at[r]
        )
        copy.start()
        stores.append(copy)
    coarse.left()
    for copy in stores:
        copy.wait()


def solution(mesh):
    gx_size, gy_size = mesh.shape["gx"], mesh.shape["gy"]
    scratch = {}
    for l, L in enumerate(LEVELS):
        for name, shape in L.scratch().items():
            scratch[str(l) + name] = shape
    scratch["xp"] = pltpu.VMEM((2, 2, 4, 2, 32, 128), BF16)
    scratch["xr"] = pltpu.VMEM((2, 2, 4, 2, 32, 128), BF16)
    scratch["yp"] = pltpu.VMEM((2, 2, 8, 16, 128), BF16)
    scratch["yr"] = pltpu.VMEM((2, 2, 12, 16, 128), BF16)
    scratch["k1"] = pltpu.VMEM((28, 1, 48, 128), BF16)
    scratch["s1"] = pltpu.VMEM((28, 1, 48, 128), BF16)
    scratch["s2"] = pltpu.VMEM((20, 1, 24, 128), F32)
    scratch["keep0"] = pltpu.VMEM((18, 2, 48, 128), F32)
    scratch["smooth0"] = pltpu.VMEM((24, 2, 48, 128), F32)
    scratch["keep2"] = pltpu.VMEM((6, 1, 24, 128), F32)
    scratch["smooth2"] = pltpu.VMEM((20, 1, 24, 128), F32)
    scratch["size"] = pltpu.VMEM((1280, 128), F32)
    scratch["mp"] = pltpu.VMEM((256, 128), BF16)
    scratch["ms"] = pltpu.VMEM((gy_size, 48, 128), BF16)
    scratch["mm"] = pltpu.VMEM((gy_size, 48, 128), BF16)
    scratch["mine"] = pltpu.VMEM((8, 128), F32)
    scratch["all"] = pltpu.VMEM((gy_size, 8, 128), F32)
    scratch["corr"] = pltpu.VMEM((5, 24, 128), F32)
    scratch["result"] = pltpu.VMEM((16, 2, 48, 128), F32)
    scratch["local"] = pltpu.SemaphoreType.DMA((4,))
    for name in EXCHANGES:
        scratch["send_" + name] = pltpu.SemaphoreType.DMA
        scratch["recv_" + name] = pltpu.SemaphoreType.DMA

    def local(pressure_source, conductance, coarse_inverse):
        return pl.pallas_call(
            functools.partial(kernel, gx_size, gy_size, tuple(scratch)),
            out_shape=jax.ShapeDtypeStruct(pressure_source.shape, F32),
            in_specs=[
                pl.BlockSpec(memory_space=pl.ANY),
                pl.BlockSpec(memory_space=pl.ANY),
                pl.BlockSpec(memory_space=pltpu.VMEM),
            ],
            out_specs=pl.BlockSpec(memory_space=pl.ANY),
            scratch_shapes=list(scratch.values()),
            compiler_params=pltpu.CompilerParams(
                collective_id=0, has_side_effects=True, vmem_limit_bytes=56 * 2**20
            ),
        )(pressure_source, conductance, coarse_inverse)

    in_specs = (P("gx", "gy", None), P("gx", "gy", None), P("gx", "gy", None, None))
    return jax.shard_map(local, mesh=mesh, in_specs=in_specs, out_specs=P("gx", "gy", None), check_vma=False)
```

```python
import functools
import math

import jax
import jax.numpy as jnp
from jax import lax
from jax.experimental import pallas as pl
from jax.experimental.pallas import tpu as pltpu
from jax.sharding import PartitionSpec as P

MESH = pl.DeviceIdType.MESH

LMAX = 2.0
LMIN = 0.25
THETA = 0.5 * (LMAX + LMIN)
DELTA = 0.5 * (LMAX - LMIN)
SIGMA = THETA / DELTA
RATIO_0 = 1.0 / SIGMA
RATIO_1 = 1.0 / (2.0 * SIGMA - RATIO_0)
RATIO_2 = 1.0 / (2.0 * SIGMA - RATIO_1)
STEP_1 = (RATIO_1 * RATIO_0, 2.0 * RATIO_1 / DELTA)
STEP_2 = (RATIO_2 * RATIO_1, 2.0 * RATIO_2 / DELTA)

F32 = jnp.float32
BF16 = jnp.bfloat16

EXCHANGES = ("side_k", "side_s", "side_v", "kappa_1", "matrix", "source_1", "gather", "level_2", "coarse")
AROUND = [(a, b) for a in (-1, 0, 1) for b in (-1, 0, 1) if (a, b) != (0, 0)]
WIDE = [(a, b) for a in (-2, -1, 0, 1, 2) for b in (-1, 0, 1) if (a, b) != (0, 0)]


class Level:
    def __init__(self, nx, ny, x0, side, R, J, hold, row0, erow, xc, coarse, most):
        self.nx, self.ny, self.X, self.x0, self.side = nx, ny, nx + 2 * x0, x0, side
        self.R, self.J, self.hold, self.row0, self.most = R, J, hold, row0, most
        self.erow, self.xc, self.coarse = erow, xc, coarse
        self.rows = ny + 2 * side

    def scratch(self):
        X, R, J = self.X, self.R, self.J
        vm = lambda *shape: pltpu.VMEM(shape + (128,), F32)
        blocked = {name: vm(X, R, J, 8) for name in ("CM", "CP", "Q", "G", "D", "DIR")}
        natural = {name: vm(X, R, self.rows) for name in ("NS", "NK", "RN")}
        return dict(
            E=vm(self.coarse[0], R, self.coarse[1]),
            HK=vm(X, R, J + 2, 8),
            CX=vm(X + 1, R, J, 8),
            CY=vm(X, R, J + 1, 8),
            VA=vm(X, R, J + 2, 8),
            VB=vm(X, R, J + 2, 8),
            **blocked,
            **natural,
        )


LEVELS = (
    Level(16, 32, 4, 8, 2, 5, 1, 4, 20, 10, (32, 80), 10),
    Level(8, 16, 12, 16, 1, 5, 1, 4, 4, 2, (20, 48), 12),
    Level(4, 8, 8, 8, 1, 3, 2, 0, 0, 0, (10, 24), 16),
)


def lanes(*lead):
    return lax.broadcasted_iota(jnp.int32, lead + (8, 128), len(lead) + 1)


def sublanes():
    return lax.broadcasted_iota(jnp.int32, (8, 128), 0)


def turn(value, shift, axis):
    return pltpu.roll(value, shift % value.shape[axis], axis)


def pick(value, index):
    return jnp.take_along_axis(value, index, axis=1, mode="promise_in_bounds")


def rows_of(L, j):
    return pl.ds(L.row0 + j, 8, stride=L.J)


def beside_z(L, parts):
    h = L.hold
    down = [turn(p, h, 2) for p in parts]
    up = [turn(p, -h, 2) for p in parts]
    if L.R == 2:
        lane = lanes(L.J)
        down[1] = jnp.where(lane == 0, down[0], down[1])
        up[0] = jnp.where(lane == 127, up[1], up[0])
    return down, up


def store_wrapped(ref, x, r, J, values):
    ref[x, r, 1 : J + 1] = values
    ref[x, r, 0] = turn(values[J - 1], 1, 0)
    ref[x, r, J + 1] = turn(values[0], -1, 0)


def rows_from(L, ref, x, r):
    return jnp.stack([ref[x, r, rows_of(L, j), :] for j in range(L.J)])


def rows_to(L, ref, x, r, values):
    for j in range(L.J):
        ref[x, r, rows_of(L, j), :] = values[j]


def loop(lo, hi, body, most=1):
    count = hi - lo
    steps = -(-count // most)
    U = -(-count // steps)
    whole = count // U
    if whole > 1:

        def step(i, carry):
            body(lo + i * U, U)
            return carry

        lax.fori_loop(0, whole, step, 0)
    elif whole == 1:
        body(lo, U)
    if count > whole * U:
        body(lo + whole * U, count - whole * U)


def prepare(L, M, lo, hi, gx, gy, count_x, count_y):
    J, R, h = L.J, L.R, L.hold
    shape = (J, 8, 128)
    lane = lanes(J)
    place = lax.broadcasted_iota(jnp.int32, shape, 0) + J * lax.broadcasted_iota(jnp.int32, shape, 1)
    place = place + (gy * L.ny - L.side + L.row0)
    keep = jnp.where((place >= 0) & (place < L.ny * count_y), 0.5, 0.0).astype(F32)

    def halves(x, U):
        NK, HK = M["NK"].at[pl.ds(x, U)], M["HK"].at[pl.ds(x, U)]
        for u in range(U):
            place = gx * L.nx + x + u - L.x0
            inside = jnp.where((place >= 0) & (place < L.nx * count_x), 1.0, 0.0).astype(F32)
            mask = keep * inside
            for r in range(R):
                store_wrapped(HK, u, r, J, rows_from(L, NK, u, r) * mask)

    loop(lo - 1, hi + 1, halves, L.most)
    for r in range(R):
        M["CX"][lo, r] = M["HK"][lo - 1, r, 1 : J + 1] + M["HK"][lo, r, 1 : J + 1]

    def couple(x, U):
        HK, CX = M["HK"].at[pl.ds(x - 1, U + 2)], M["CX"].at[pl.ds(x, U + 1)]
        CY, CM, CP, D, Q = (M[name].at[pl.ds(x, U)] for name in ("CY", "CM", "CP", "D", "Q"))
        for u in range(U):
            mine = [HK[u + 1, r, 1 : J + 1] for r in range(R)]
            down, up = beside_z(L, mine)
            down[0] = jnp.where(lane < h, 0.0, down[0])
            up[R - 1] = jnp.where(lane >= 128 - h, 0.0, up[R - 1])
            for r in range(R):
                c = mine[r]
                xm, xp = HK[u, r, 1 : J + 1], HK[u + 2, r, 1 : J + 1]
                ym, yp = HK[u + 1, r, 0:J], HK[u + 1, r, 2 : J + 2]
                diagonal = (xm + xp) + (ym + yp) + (down[r] + up[r]) + 6.0 * c
                CX[u + 1, r] = c + xp
                CY[u, r, 0:J] = c + ym
                CY[u, r, J] = c[J - 1] + yp[J - 1]
                low, high = c + down[r], c + up[r]
                if r == 0:
                    low = jnp.where(lane < h, 0.0, low)
                if r == R - 1:
                    high = jnp.where(lane >= 128 - h, 0.0, high)
                CM[u, r] = low
                CP[u, r] = high
                D[u, r] = diagonal
                Q[u, r] = jnp.where(c > 0.0, 1.0 / diagonal, 0.0)

    loop(lo, hi, couple, L.most)


def scale_source(L, M, name, lo, hi, start):
    J, field = L.J, M[name]

    def body(x, U):
        Q, G, VA, NS = (ref.at[pl.ds(x, U)] for ref in (M["Q"], M["G"], M["VA"], field))
        for u in range(U):
            for r in range(L.R):
                g = Q[u, r] * rows_from(L, NS, u, r)
                G[u, r] = g
                if start:
                    store_wrapped(VA, u, r, J, g * (1.0 / THETA))

    loop(lo, hi, body, L.most)


def sweep(L, M, src, dst, lo, hi, kind, step=None, keep_rows=None, emit=None):
    J, R = L.J, L.R

    def body(x, U):
        V, CX = M[src].at[pl.ds(x - 1, U + 2)], M["CX"].at[pl.ds(x, U + 1)]
        CY, CM, CP, D, Q, G, DIR = (M[name].at[pl.ds(x, U)] for name in ("CY", "CM", "CP", "D", "Q", "G", "DIR"))
        if dst is not None:
            W = M[dst].at[pl.ds(x, U)]
        if kind == "residual":
            RN = M["RN"].at[pl.ds(x, U)]
        if keep_rows is not None:
            kept = keep_rows.at[pl.ds(x - L.x0 + 1, U)]
        for u in range(U):
            mine = [V[u + 1, r, 1 : J + 1] for r in range(R)]
            down, up = beside_z(L, mine)
            new = []
            for r in range(R):
                c = mine[r]
                near = CX[u, r] * V[u, r, 1 : J + 1] + CX[u + 1, r] * V[u + 2, r, 1 : J + 1]
                near = near + (CY[u, r, 0:J] * V[u + 1, r, 0:J] + CY[u, r, 1 : J + 1] * V[u + 1, r, 2 : J + 2])
                near = near + (CM[u, r] * down[r] + CP[u, r] * up[r])
                update = (G[u, r] - c) + Q[u, r] * near
                if kind == "residual":
                    rows_to(L, RN, u, r, D[u, r] * update)
                    continue
                if kind == "first":
                    direction = update * (1.0 / THETA)
                elif kind == "from_zero":
                    direction = step[0] * c + step[1] * update
                else:
                    direction = step[0] * DIR[u, r] + step[1] * update
                if kind != "last":
                    DIR[u, r] = direction
                value = c + direction
                if dst is not None:
                    store_wrapped(W, u, r, J, value)
                if keep_rows is not None:
                    rows_to(L, kept, u, r, value)
                new.append(value)
            if emit is not None:
                emit(x + u, new)

    loop(lo, hi, body, L.most)


def descend(L, M, margin, keep_rows=None):
    lo, hi = L.x0 - margin, L.x0 + L.nx + margin
    sweep(L, M, "VA", "VB", lo - 2, hi + 2, "from_zero", STEP_1)
    sweep(L, M, "VB", "VA", lo - 1, hi + 1, "last", STEP_2, keep_rows=keep_rows)
    sweep(L, M, "VA", None, lo, hi, "residual")


def ascend(L, M, margin, emit, smoothed=None, pieces=1, after=lambda n: None):
    lo, hi = L.x0, L.x0 + L.nx

    def begin(x, U):
        HK, VA = (M[name].at[pl.ds(x, U)] for name in ("HK", "VA"))
        if smoothed is not None:
            NV = smoothed.at[pl.ds(x, U)]
        for u in range(U):
            xc = lax.shift_right_logical(x + u, 1) + L.xc
            for r in range(L.R):
                added = [M["E"][xc, r, pl.ds(L.erow + j, 8, stride=L.J), :] for j in range(L.J)]
                base = VA[u, r, 1 : L.J + 1] if smoothed is None else rows_from(L, NV, u, r)
                inside = HK[u, r, 1 : L.J + 1] > 0.0
                store_wrapped(VA, u, r, L.J, jnp.where(inside, jnp.stack(added) + base, 0.0))

    loop(lo - margin, hi + margin, begin, L.most)
    margin -= 1
    sweep(L, M, "VA", "VB", lo - margin, hi + margin, "first")
    margin -= 1
    sweep(L, M, "VB", "VA", lo - margin, hi + margin, "next", STEP_1)
    margin -= 1
    width = (hi - lo + 2 * margin) // pieces
    for n in range(pieces):
        first = lo - margin + n * width
        sweep(L, M, "VA", None, first, first + width, "last", STEP_2, emit=emit)
        after(n)


def coarsen(L, src, row, tiles, scale, put):
    lane = lanes()
    even = (lane * 2) & 127

    def body(x, U):
        pairs = src.at[pl.ds(2 * x, 2 * U)]
        for u, t in [(u, t) for u in range(U) for t in range(tiles)]:
            sums = []
            for r in range(L.R):
                rows = [pairs[2 * u + dx, r, pl.ds(row + 16 * t + b, 8, stride=2), :] for dx in (0, 1) for b in (0, 1)]
                total = (rows[0] + rows[1]) + (rows[2] + rows[3])
                if L.R == 2:
                    sums.append(pick(total + turn(total, -1, 1), even))
                else:
                    other = jnp.where((lane & L.hold) == 0, turn(total, -L.hold, 1), turn(total, L.hold, 1))
                    sums.append(total + other)
            value = jnp.where(lane < 64, sums[0], sums[1]) if L.R == 2 else sums[0]
            put(x + u, t, value * scale)

    return body


def put_rows(dst, dx, row):
    def put(x, t, value):
        dst[dx + x, 0, row + 8 * t : row + 8 * t + 8, :] = value

    return put


def kernel(gx_size, gy_size, names, source, conductance, inverse, out, *refs):
    S = dict(zip(names, refs))
    M = [{k[1:]: v for k, v in S.items() if k[0] == str(l)} for l in range(3)]
    M[2]["s2"] = S["s2"]
    gx, gy = lax.axis_index("gx"), lax.axis_index("gy")
    L0, L1, L2 = LEVELS

    def device(a, b):
        return {"gx": lax.rem(gx + a + gx_size, gx_size), "gy": lax.rem(gy + b + gy_size, gy_size)}

    class Exchange:
        def __init__(self, name):
            self.out, self.back, self.rows, self.copies = S["send_" + name], S["recv_" + name], 0, []

        def add(self, src, dst, a, b):
            copy = pltpu.make_async_remote_copy(
                src_ref=src, dst_ref=dst, send_sem=self.out, recv_sem=self.back, device_id=device(a, b), device_id_type=MESH
            )
            self.copies.append(copy)
            rows = math.prod(src.shape[:-1])
            self.rows += rows if src.dtype == F32 else rows // 2

        def start(self):
            for copy in self.copies:
                copy.start()
            return self

        def wait(self, semaphore):
            size = S["size"].at[pl.ds(0, self.rows)]
            pltpu.make_async_copy(size, size, semaphore).wait()

        def arrive(self):
            self.wait(self.back)

        def left(self):
            self.wait(self.out)

    def exchange(L, src, sx0, dst, near, far, name):
        both = Exchange(name)
        h = L.side
        for a, b in WIDE if far else AROUND:
            w = {0: L.nx, 1: near, 2: far}[abs(a)]
            xs = sx0 + (L.nx - w if a > 0 else 0)
            xd = {0: L.x0, 1: L.x0 - w, 2: L.x0 - L.nx - w, -1: L.x0 + L.nx, -2: L.x0 + 2 * L.nx}[a]
            ys = h + (L.ny - h if b > 0 else 0)
            yd, wy = {0: (h, L.ny), 1: (0, h), -1: (h + L.ny, h)}[b]
            both.add(src.at[pl.ds(xs, w), :, pl.ds(ys, wy), :], dst.at[pl.ds(xd, w), :, pl.ds(yd, wy), :], a, b)
        return both.start()

    peers = list(WIDE) + [(0, b) for b in range(2, gy_size - 1)]
    barrier = pltpu.get_barrier_semaphore()
    for a, b in peers:
        pl.semaphore_signal(barrier, inc=1, device_id=device(a, b), device_id_type=MESH)

    fields = (M[0]["NK"], M[0]["NS"], S["smooth0"])
    XP, YP, XR, YR = S["xp"], S["yp"], S["xr"], S["yr"]
    sub, lane = sublanes(), lanes()

    loads = [pltpu.make_async_copy(inverse, S["inverse"], S["local"].at[4])]
    for n, src in enumerate((conductance, source)):
        for r in range(2):
            loads.append(
                pltpu.make_async_copy(
                    src.at[:, :, pl.ds(128 * r, 128)],
                    fields[n].at[pl.ds(4, 16), r, pl.ds(8, 32), :],
                    S["local"].at[2 * n + r],
                )
            )
    for copy in loads:
        copy.start()

    def pack(a, field, first):
        def pack_x(i, _):
            for r in range(2):
                XP[a, 0, i, r] = field[first + i, r, 8:40, :].astype(BF16)
                XP[a, 1, i, r] = field[first + 12 + i, r, 8:40, :].astype(BF16)

        def pack_y(i, _):
            low, high = [], []
            for d in range(2):
                x = first + 2 * i + d
                near, far = field[x, 0, 8:16, :], field[x, 1, 8:16, :]
                low.append(jnp.where(sub < 4, near, turn(far, 4, 0)))
                near, far = field[x, 0, 32:40, :], field[x, 1, 32:40, :]
                high.append(jnp.where(sub < 4, turn(near, 4, 0), far))
            YP[a, 0, i] = jnp.concatenate(low, axis=0).astype(BF16)
            YP[a, 1, i] = jnp.concatenate(high, axis=0).astype(BF16)

        loop(0, 4, pack_x)
        loop(0, 8, pack_y)

    def sides(a, name):
        both = Exchange(name)
        for x, y in AROUND:
            if y == 0:
                both.add(XP.at[a, (x + 1) // 2], XR.at[a, (1 - x) // 2], x, y)
            else:
                xs, xd, wx = {0: (0, 2, 8), 1: (6, 0, 2), -1: (0, 10, 2)}[x]
                both.add(YP.at[a, (y + 1) // 2, pl.ds(xs, wx)], YR.at[a, (1 - y) // 2, pl.ds(xd, wx)], x, y)
        return both.start()

    def unpack(a):
        field = fields[a]

        def unpack_x(i, _):
            for r in range(2):
                field[i, r, 8:40, :] = XR[a, 0, i, r].astype(F32)
                field[20 + i, r, 8:40, :] = XR[a, 1, i, r].astype(F32)

        def unpack_y(i, _):
            low, high = YR[a, 0, i].astype(F32), YR[a, 1, i].astype(F32)
            for d in range(2):
                x = 2 * i + d
                part = low[8 * d : 8 * d + 8]
                field[x, 0, 0:8, :] = turn(part, 4, 0)
                field[x, 1, 0:8, :] = part
                part = high[8 * d : 8 * d + 8]
                field[x, 0, 40:48, :] = part
                field[x, 1, 40:48, :] = turn(part, 4, 0)

        loop(0, 4, unpack_x)
        loop(0, 12, unpack_y)

    for a in range(2):
        loads[1 + 2 * a].wait()
        loads[2 + 2 * a].wait()
        pack(a, fields[a], 4)

    pl.semaphore_wait(barrier, len(peers))
    side_k = sides(0, "side_k")
    side_s = sides(1, "side_s")

    def halve(field, packed):
        packed[12:20, 0, 16:32, :] = field[12:20, 0, 16:32, :].astype(BF16)

    def widen(packed, field, margin):
        def whole(x, U):
            for u in range(U):
                field[x + u, 0] = packed[x + u, 0].astype(F32)

        def ends(x, U):
            for u in range(U):
                for rows in (pl.ds(0, 16), pl.ds(32, 16)):
                    field[x + u, 0, rows, :] = packed[x + u, 0, rows, :].astype(F32)

        loop(12 - margin, 12, whole, 6)
        loop(12, 20, ends, 8)
        loop(20, 20 + margin, whole, 6)

    loop(0, 8, coarsen(L0, M[0]["NK"].at[pl.ds(4, 16)], 8, 2, 0.125, put_rows(M[1]["NK"], 12, 16)), 4)
    halve(M[1]["NK"], S["k1"])

    loads[0].wait()
    one = lambda mask: jnp.where(mask, 1.0, 0.0).astype(BF16)
    row = lax.broadcasted_iota(jnp.int32, (128, 128), 0)
    column = lax.broadcasted_iota(jnp.int32, (128, 128), 1)
    order = one(row == ((column >> 2) & 1) * 64 + (column >> 3) * 4 + (column & 3))
    for k in range(2):
        S["mp"][128 * k : 128 * (k + 1), :] = jnp.dot(
            S["inverse"][0, k], order, preferred_element_type=F32
        ).astype(BF16)

    row = lax.broadcasted_iota(jnp.int32, (48, 256), 0)
    column = lax.broadcasted_iota(jnp.int32, (48, 256), 1)
    layer = jnp.where(row >= 24, 1, 0)
    row = row - 24 * layer
    half = jnp.where(row >= 12, 1, 0)
    row = row - 12 * half
    base = layer * 128 + half * 64

    def share(d, _):
        chosen = one(column == base + ((row + (4 * d + 60)) & 63))
        S["ms"][d] = jnp.dot(chosen, S["mp"][...], preferred_element_type=F32).astype(BF16)

    loop(0, gy_size, share)
    kappa_1 = exchange(L1, S["k1"], 12, S["k1"], 8, 4, "kappa_1")

    place = (gx, gy, gx_size, gy_size)
    side_k.arrive()
    unpack(0)
    prepare(L0, M[0], 1, 23, *place)
    side_s.arrive()
    unpack(1)
    scale_source(L0, M[0], "NS", 1, 23, True)
    descend(L0, M[0], 0, S["keep0"])
    residual = M[0]["RN"].at[pl.ds(4, 16)]
    loop(0, 8, coarsen(L0, residual, 8, 2, 0.5, put_rows(M[1]["NS"], 12, 16)), 4)
    halve(M[1]["NS"], S["s1"])
    source_1 = exchange(L1, S["s1"], 12, S["s1"], 8, 2, "source_1")

    kappa_1.arrive()
    widen(S["k1"], M[1]["NK"], 12)
    prepare(L1, M[1], 3, 29, *place)
    loop(0, 16, coarsen(L1, M[1]["NK"], 0, 3, 0.125, put_rows(M[2]["NK"], 2, 0)), 8)
    prepare(L2, M[2], 3, 17, *place)
    matrices = Exchange("matrix")
    for n in range(1, gy_size):
        matrices.add(S["ms"].at[lax.rem(gy + n, gy_size)], S["mm"].at[gy], 0, n)
    matrices.start()
    S["mm"][gy] = S["ms"][gy]
    pack(2, S["keep0"], 1)
    side_v = sides(2, "side_v")

    source_1.arrive()
    widen(S["s1"], M[1]["NS"], 10)
    scale_source(L1, M[1], "NS", 3, 29, True)
    descend(L1, M[1], 6)

    residual = M[1]["RN"].at[pl.ds(6, 20)]
    loop(0, 10, coarsen(L1, residual, 0, 3, 0.5, put_rows(S["s2"], 5, 0)), 5)
    scale_source(L2, M[2], "s2", 5, 15, True)
    descend(L2, M[2], 0, S["keep2"])
    tiles = []
    residual = M[2]["RN"].at[pl.ds(8, 4)]
    loop(0, 2, coarsen(L2, residual, 8, 1, 1.0 / 128.0, lambda x, t, value: tiles.append(value)), 2)
    rounded = jnp.where(sub < 4, tiles[0], turn(tiles[1], 4, 0)).astype(BF16).astype(F32)
    S["mine"][...] = rounded
    gathered = Exchange("gather")
    for n in range(1, gy_size):
        gathered.add(S["mine"], S["all"].at[gy], 0, n)
    gathered.start()
    odd = (lanes(4) & 1) == 1
    pair = S["pair"]
    pair[8:12, 0, 8:16, :] = jnp.where(odd, S["keep2"][1:5, 0, 8:16, :], S["s2"][8:12, 0, 8:16, :])
    level_2 = exchange(L2, pair, 8, pair, 4, 4, "level_2")
    S["all"][gy] = rounded

    kept = pltpu.make_async_copy(
        S["keep0"].at[pl.ds(1, 16), :, pl.ds(8, 32), :],
        S["smooth0"].at[pl.ds(4, 16), :, pl.ds(8, 32), :],
        S["local"].at[0],
    )
    kept.start()
    for old in (side_k, side_s, kappa_1, source_1, matrices, side_v):
        old.left()
    side_v.arrive()
    unpack(2)
    kept.wait()
    matrices.arrive()
    gathered.arrive()
    right = S["all"][...].reshape(gy_size * 8, 128).astype(BF16)
    layer_of = lax.broadcasted_iota(jnp.int32, (24, 128), 1) >> 2

    def solve(d, total):
        product = jnp.dot(S["mm"][d], right, preferred_element_type=F32)
        total = total + jnp.where(layer_of == 2 * d, product[:24], 0.0)
        return total + jnp.where(layer_of == 2 * d + 1, product[24:], 0.0)

    S["corr"][2] = lax.fori_loop(0, gy_size, solve, jnp.zeros((24, 128), F32))
    coarse = Exchange("coarse")
    for a in (-2, -1, 1, 2):
        coarse.add(S["corr"].at[2], S["corr"].at[2 - a], a, 0)
    coarse.start()
    gathered.left()
    level_2.left()
    level_2.arrive()

    def part(x, U):
        for u in range(U):
            for t in range(3):
                rows = pl.ds(8 * t, 8)
                both = pair[x + u, 0, rows, :]
                second = (lane & 1) == 1
                M[2]["NS"][x + u, 0, rows, :] = jnp.where(second, turn(both, 1, 1), both)
                S["smooth2"][x + u, 0, rows, :] = jnp.where(second, both, turn(both, -1, 1))

    loop(2, 18, part, 8)
    scale_source(L2, M[2], "NS", 3, 17, False)
    coarse.arrive()

    for slab in range(5):
        for d in range(2):
            for b in range(2):
                M[2]["E"][2 * slab + d, 0, pl.ds(b, 8, stride=2), :] = S["corr"][slab, 12 * d : 12 * d + 8, :]
                M[2]["E"][2 * slab + d, 0, pl.ds(16 + b, 4, stride=2), :] = S["corr"][slab, 12 * d + 8 : 12 * d + 12, :]

    def emit_2(x, new):
        for j in range(L2.J):
            for b in range(2):
                M[1]["E"][x, 0, pl.ds(2 * j + b, 8, stride=2 * L2.J), :] = new[0][j]

    def emit_1(x, new):
        for j in range(L1.J):
            for r in range(2):
                value = pick(new[0][j], (lane >> 1) + 64 * r)
                for b in range(2):
                    M[0]["E"][x, r, pl.ds(2 * j + b, 8, stride=2 * L1.J), :] = value

    def emit_0(x, new):
        for r in range(2):
            for j in range(L0.J):
                S["result"][x - L0.x0, r, rows_of(L0, j), :] = new[r][j]

    ascend(L2, M[2], 6, emit_2, S["smooth2"])
    ascend(L1, M[1], 5, emit_1)
    stores = []

    def store(n):
        for r in range(2):
            copy = pltpu.make_async_copy(
                S["result"].at[pl.ds(8 * n, 8), r, pl.ds(8, 32), :],
                out.at[pl.ds(8 * n, 8), :, pl.ds(128 * r, 128)],
                S["local"].at[2 * n + r],
            )
            copy.start()
            stores.append(copy)

    ascend(L0, M[0], 3, emit_0, S["smooth0"], 2, store)
    coarse.left()
    for copy in stores:
        copy.wait()


def solution(mesh):
    gx_size, gy_size = mesh.shape["gx"], mesh.shape["gy"]
    scratch = {}
    for l, L in enumerate(LEVELS):
        for name, shape in L.scratch().items():
            scratch[str(l) + name] = shape
    scratch["xp"] = pltpu.VMEM((3, 2, 4, 2, 32, 128), BF16)
    scratch["xr"] = pltpu.VMEM((3, 2, 4, 2, 32, 128), BF16)
    scratch["yp"] = pltpu.VMEM((3, 2, 8, 16, 128), BF16)
    scratch["yr"] = pltpu.VMEM((3, 2, 12, 16, 128), BF16)
    scratch["k1"] = pltpu.VMEM((32, 1, 48, 128), BF16)
    scratch["s1"] = pltpu.VMEM((32, 1, 48, 128), BF16)
    scratch["s2"] = pltpu.VMEM((20, 1, 24, 128), F32)
    scratch["keep0"] = pltpu.VMEM((18, 2, 48, 128), F32)
    scratch["smooth0"] = pltpu.VMEM((24, 2, 48, 128), F32)
    scratch["keep2"] = pltpu.VMEM((6, 1, 24, 128), F32)
    scratch["pair"] = pltpu.VMEM((20, 1, 24, 128), F32)
    scratch["smooth2"] = pltpu.VMEM((20, 1, 24, 128), F32)
    scratch["size"] = pltpu.VMEM((768, 128), F32)
    scratch["inverse"] = pltpu.VMEM((1, 2, 128, 128), BF16)
    scratch["mp"] = pltpu.VMEM((256, 128), BF16)
    scratch["ms"] = pltpu.VMEM((gy_size, 48, 128), BF16)
    scratch["mm"] = pltpu.VMEM((gy_size, 48, 128), BF16)
    scratch["mine"] = pltpu.VMEM((8, 128), F32)
    scratch["all"] = pltpu.VMEM((gy_size, 8, 128), F32)
    scratch["corr"] = pltpu.VMEM((5, 24, 128), F32)
    scratch["result"] = pltpu.VMEM((16, 2, 48, 128), F32)
    scratch["local"] = pltpu.SemaphoreType.DMA((5,))
    for name in EXCHANGES:
        scratch["send_" + name] = pltpu.SemaphoreType.DMA
        scratch["recv_" + name] = pltpu.SemaphoreType.DMA

    def local(pressure_source, conductance, coarse_inverse):
        return pl.pallas_call(
            functools.partial(kernel, gx_size, gy_size, tuple(scratch)),
            out_shape=jax.ShapeDtypeStruct(pressure_source.shape, F32),
            in_specs=[
                pl.BlockSpec(memory_space=pl.ANY),
                pl.BlockSpec(memory_space=pl.ANY),
                pl.BlockSpec(memory_space=pl.ANY),
            ],
            out_specs=pl.BlockSpec(memory_space=pl.ANY),
            scratch_shapes=list(scratch.values()),
            compiler_params=pltpu.CompilerParams(
                collective_id=0, has_side_effects=True, vmem_limit_bytes=56 * 2**20
            ),
        )(pressure_source, conductance, coarse_inverse)

    in_specs = (P("gx", "gy", None), P("gx", "gy", None), P("gx", "gy", None, None))
    return jax.shard_map(local, mesh=mesh, in_specs=in_specs, out_specs=P("gx", "gy", None), check_vma=False)
```

```python
import functools
import math

import jax
import jax.numpy as jnp
from jax import lax
from jax.experimental import pallas as pl
from jax.experimental.pallas import tpu as pltpu
from jax.sharding import PartitionSpec as P

MESH = pl.DeviceIdType.MESH

LMAX = 2.0
LMIN = 0.25
THETA = 0.5 * (LMAX + LMIN)
DELTA = 0.5 * (LMAX - LMIN)
SIGMA = THETA / DELTA
RATIO_0 = 1.0 / SIGMA
RATIO_1 = 1.0 / (2.0 * SIGMA - RATIO_0)
RATIO_2 = 1.0 / (2.0 * SIGMA - RATIO_1)
STEP_1 = (RATIO_1 * RATIO_0, 2.0 * RATIO_1 / DELTA)
STEP_2 = (RATIO_2 * RATIO_1, 2.0 * RATIO_2 / DELTA)

F32 = jnp.float32
BF16 = jnp.bfloat16

EXCHANGES = ("side_k", "side_s", "side_v", "kappa_1", "matrix", "source_1", "gather", "level_2", "coarse")
AROUND = [(a, b) for a in (-1, 0, 1) for b in (-1, 0, 1) if (a, b) != (0, 0)]
WIDE = [(a, b) for a in (-2, -1, 0, 1, 2) for b in (-1, 0, 1) if (a, b) != (0, 0)]
AROUND.sort(key=lambda o: -abs(o[0]) - 2 * abs(o[1]))
WIDE.sort(key=lambda o: -abs(o[0]) - 2 * abs(o[1]))
LINE = sorted(range(1, 16), key=lambda n: -min(n // 4, 4 - n // 4) - min(n % 4, 4 - n % 4))


class Level:
    def __init__(self, nx, ny, x0, side, R, J, hold, row0, erow, xc, coarse, most):
        self.nx, self.ny, self.X, self.x0, self.side = nx, ny, nx + 2 * x0, x0, side
        self.R, self.J, self.hold, self.row0, self.most = R, J, hold, row0, most
        self.erow, self.xc, self.coarse = erow, xc, coarse
        self.rows = ny + 2 * side

    def scratch(self):
        X, R, J = self.X, self.R, self.J
        vm = lambda *shape: pltpu.VMEM(shape + (128,), F32)
        blocked = {name: vm(X, R, J, 8) for name in ("CM", "CP", "Q", "G", "D", "DIR")}
        natural = {name: vm(X, R, self.rows) for name in ("NS", "NK", "RN")}
        return dict(
            E=vm(self.coarse[0], R, self.coarse[1]),
            HK=vm(X, R, J + 2, 8),
            CX=vm(X + 1, R, J, 8),
            CY=vm(X, R, J + 1, 8),
            VA=vm(X, R, J + 2, 8),
            VB=vm(X, R, J + 2, 8),
            **blocked,
            **natural,
        )


LEVELS = (
    Level(16, 32, 4, 8, 2, 5, 1, 4, 20, 10, (32, 80), 10),
    Level(8, 16, 12, 16, 1, 5, 1, 4, 4, 2, (20, 48), 12),
    Level(4, 8, 8, 8, 1, 3, 2, 0, 0, 0, (10, 24), 16),
)


def lanes(*lead):
    return lax.broadcasted_iota(jnp.int32, lead + (8, 128), len(lead) + 1)


def sublanes():
    return lax.broadcasted_iota(jnp.int32, (8, 128), 0)


def turn(value, shift, axis):
    return pltpu.roll(value, shift % value.shape[axis], axis)


def pick(value, index):
    return jnp.take_along_axis(value, index, axis=1, mode="promise_in_bounds")


def rows_of(L, j):
    return pl.ds(L.row0 + j, 8, stride=L.J)


def beside_z(L, parts):
    h = L.hold
    down = [turn(p, h, 2) for p in parts]
    up = [turn(p, -h, 2) for p in parts]
    if L.R == 2:
        lane = lanes(L.J)
        down[1] = jnp.where(lane == 0, down[0], down[1])
        up[0] = jnp.where(lane == 127, up[1], up[0])
    return down, up


def store_wrapped(ref, x, r, J, values):
    ref[x, r, 1 : J + 1] = values
    ref[x, r, 0] = turn(values[J - 1], 1, 0)
    ref[x, r, J + 1] = turn(values[0], -1, 0)


def rows_from(L, ref, x, r):
    return jnp.stack([ref[x, r, rows_of(L, j), :] for j in range(L.J)])


def rows_to(L, ref, x, r, values):
    for j in range(L.J):
        ref[x, r, rows_of(L, j), :] = values[j]


def loop(lo, hi, body, most=1):
    count = hi - lo
    steps = -(-count // most)
    U = -(-count // steps)
    whole = count // U
    if whole > 1:

        def step(i, carry):
            body(lo + i * U, U)
            return carry

        lax.fori_loop(0, whole, step, 0)
    elif whole == 1:
        body(lo, U)
    if count > whole * U:
        body(lo + whole * U, count - whole * U)


def prepare(L, M, lo, hi, gx, gy, count_x, count_y):
    J, R, h = L.J, L.R, L.hold
    shape = (J, 8, 128)
    lane = lanes(J)
    place = lax.broadcasted_iota(jnp.int32, shape, 0) + J * lax.broadcasted_iota(jnp.int32, shape, 1)
    place = place + (gy * L.ny - L.side + L.row0)
    keep = jnp.where((place >= 0) & (place < L.ny * count_y), 0.5, 0.0).astype(F32)

    def halves(x, U):
        NK, HK = M["NK"].at[pl.ds(x, U)], M["HK"].at[pl.ds(x, U)]
        for u in range(U):
            place = gx * L.nx + x + u - L.x0
            inside = jnp.where((place >= 0) & (place < L.nx * count_x), 1.0, 0.0).astype(F32)
            mask = keep * inside
            for r in range(R):
                store_wrapped(HK, u, r, J, rows_from(L, NK, u, r) * mask)

    loop(lo - 1, hi + 1, halves, L.most)
    for r in range(R):
        M["CX"][lo, r] = M["HK"][lo - 1, r, 1 : J + 1] + M["HK"][lo, r, 1 : J + 1]

    def couple(x, U):
        HK, CX = M["HK"].at[pl.ds(x - 1, U + 2)], M["CX"].at[pl.ds(x, U + 1)]
        CY, CM, CP, D, Q = (M[name].at[pl.ds(x, U)] for name in ("CY", "CM", "CP", "D", "Q"))
        for u in range(U):
            mine = [HK[u + 1, r, 1 : J + 1] for r in range(R)]
            down, up = beside_z(L, mine)
            down[0] = jnp.where(lane < h, 0.0, down[0])
            up[R - 1] = jnp.where(lane >= 128 - h, 0.0, up[R - 1])
            for r in range(R):
                c = mine[r]
                xm, xp = HK[u, r, 1 : J + 1], HK[u + 2, r, 1 : J + 1]
                ym, yp = HK[u + 1, r, 0:J], HK[u + 1, r, 2 : J + 2]
                diagonal = (xm + xp) + (ym + yp) + (down[r] + up[r]) + 6.0 * c
                CX[u + 1, r] = c + xp
                CY[u, r, 0:J] = c + ym
                CY[u, r, J] = c[J - 1] + yp[J - 1]
                low, high = c + down[r], c + up[r]
                if r == 0:
                    low = jnp.where(lane < h, 0.0, low)
                if r == R - 1:
                    high = jnp.where(lane >= 128 - h, 0.0, high)
                CM[u, r] = low
                CP[u, r] = high
                D[u, r] = diagonal
                Q[u, r] = jnp.where(c > 0.0, 1.0 / diagonal, 0.0)

    loop(lo, hi, couple, L.most)


def scale_source(L, M, name, lo, hi, start):
    J, field = L.J, M[name]

    def body(x, U):
        Q, G, VA, NS = (ref.at[pl.ds(x, U)] for ref in (M["Q"], M["G"], M["VA"], field))
        for u in range(U):
            for r in range(L.R):
                g = Q[u, r] * rows_from(L, NS, u, r)
                G[u, r] = g
                if start:
                    store_wrapped(VA, u, r, J, g * (1.0 / THETA))

    loop(lo, hi, body, L.most)


def sweep(L, M, src, dst, lo, hi, kind, step=None, keep_rows=None, emit=None):
    J, R = L.J, L.R

    def body(x, U):
        V, CX = M[src].at[pl.ds(x - 1, U + 2)], M["CX"].at[pl.ds(x, U + 1)]
        CY, CM, CP, D, Q, G, DIR = (M[name].at[pl.ds(x, U)] for name in ("CY", "CM", "CP", "D", "Q", "G", "DIR"))
        if dst is not None:
            W = M[dst].at[pl.ds(x, U)]
        if kind == "residual":
            RN = M["RN"].at[pl.ds(x, U)]
        if keep_rows is not None:
            kept = keep_rows.at[pl.ds(x - L.x0 + 1, U)]
        for u in range(U):
            mine = [V[u + 1, r, 1 : J + 1] for r in range(R)]
            down, up = beside_z(L, mine)
            new = []
            for r in range(R):
                c = mine[r]
                near = CX[u, r] * V[u, r, 1 : J + 1] + CX[u + 1, r] * V[u + 2, r, 1 : J + 1]
                near = near + (CY[u, r, 0:J] * V[u + 1, r, 0:J] + CY[u, r, 1 : J + 1] * V[u + 1, r, 2 : J + 2])
                near = near + (CM[u, r] * down[r] + CP[u, r] * up[r])
                update = (G[u, r] - c) + Q[u, r] * near
                if kind == "residual":
                    rows_to(L, RN, u, r, D[u, r] * update)
                    continue
                if kind == "first":
                    direction = update * (1.0 / THETA)
                elif kind == "from_zero":
                    direction = step[0] * c + step[1] * update
                else:
                    direction = step[0] * DIR[u, r] + step[1] * update
                if kind != "last":
                    DIR[u, r] = direction
                value = c + direction
                if dst is not None:
                    store_wrapped(W, u, r, J, value)
                if keep_rows is not None:
                    rows_to(L, kept, u, r, value)
                new.append(value)
            if emit is not None:
                emit(x + u, new)

    loop(lo, hi, body, L.most)


def descend(L, M, margin, keep_rows=None):
    lo, hi = L.x0 - margin, L.x0 + L.nx + margin
    sweep(L, M, "VA", "VB", lo - 2, hi + 2, "from_zero", STEP_1)
    sweep(L, M, "VB", "VA", lo - 1, hi + 1, "last", STEP_2, keep_rows=keep_rows)
    sweep(L, M, "VA", None, lo, hi, "residual")


def ascend(L, M, margin, emit, smoothed=None, pieces=1, after=lambda n: None):
    lo, hi = L.x0, L.x0 + L.nx

    def begin(x, U):
        HK, VA = (M[name].at[pl.ds(x, U)] for name in ("HK", "VA"))
        if smoothed is not None:
            NV = smoothed.at[pl.ds(x, U)]
        for u in range(U):
            xc = lax.shift_right_logical(x + u, 1) + L.xc
            for r in range(L.R):
                added = [M["E"][xc, r, pl.ds(L.erow + j, 8, stride=L.J), :] for j in range(L.J)]
                base = VA[u, r, 1 : L.J + 1] if smoothed is None else rows_from(L, NV, u, r)
                inside = HK[u, r, 1 : L.J + 1] > 0.0
                store_wrapped(VA, u, r, L.J, jnp.where(inside, jnp.stack(added) + base, 0.0))

    loop(lo - margin, hi + margin, begin, L.most)
    margin -= 1
    sweep(L, M, "VA", "VB", lo - margin, hi + margin, "first")
    margin -= 1
    sweep(L, M, "VB", "VA", lo - margin, hi + margin, "next", STEP_1)
    margin -= 1
    width = (hi - lo + 2 * margin) // pieces
    for n in range(pieces):
        first = lo - margin + n * width
        sweep(L, M, "VA", None, first, first + width, "last", STEP_2, emit=emit)
        after(n)


def coarsen(L, src, row, tiles, scale, put):
    lane = lanes()
    even = (lane * 2) & 127

    def body(x, U):
        pairs = src.at[pl.ds(2 * x, 2 * U)]
        for u, t in [(u, t) for u in range(U) for t in range(tiles)]:
            sums = []
            for r in range(L.R):
                rows = [pairs[2 * u + dx, r, pl.ds(row + 16 * t + b, 8, stride=2), :] for dx in (0, 1) for b in (0, 1)]
                total = (rows[0] + rows[1]) + (rows[2] + rows[3])
                if L.R == 2:
                    sums.append(pick(total + turn(total, -1, 1), even))
                else:
                    other = jnp.where((lane & L.hold) == 0, turn(total, -L.hold, 1), turn(total, L.hold, 1))
                    sums.append(total + other)
            value = jnp.where(lane < 64, sums[0], sums[1]) if L.R == 2 else sums[0]
            put(x + u, t, value * scale)

    return body


def put_rows(dst, dx, row):
    def put(x, t, value):
        dst[dx + x, 0, row + 8 * t : row + 8 * t + 8, :] = value

    return put


def kernel(gx_size, gy_size, names, source, conductance, inverse, out, *refs):
    S = dict(zip(names, refs))
    M = [{k[1:]: v for k, v in S.items() if k[0] == str(l)} for l in range(3)]
    M[2]["s2"] = S["s2"]
    gx, gy = lax.axis_index("gx"), lax.axis_index("gy")
    L0, L1, L2 = LEVELS

    def device(a, b):
        return {"gx": lax.rem(gx + a + gx_size, gx_size), "gy": lax.rem(gy + b + gy_size, gy_size)}

    class Exchange:
        def __init__(self, name):
            self.out, self.back, self.rows, self.copies = S["send_" + name], S["recv_" + name], 0, []

        def add(self, src, dst, a, b):
            copy = pltpu.make_async_remote_copy(
                src_ref=src, dst_ref=dst, send_sem=self.out, recv_sem=self.back, device_id=device(a, b), device_id_type=MESH
            )
            self.copies.append(copy)
            rows = math.prod(src.shape[:-1])
            self.rows += rows if src.dtype == F32 else rows // 2

        def start(self):
            for copy in self.copies:
                copy.start()
            return self

        def wait(self, semaphore):
            size = S["size"].at[pl.ds(0, self.rows)]
            pltpu.make_async_copy(size, size, semaphore).wait()

        def arrive(self):
            self.wait(self.back)

        def left(self):
            self.wait(self.out)

    def exchange(L, src, sx0, dst, near, far, name):
        both = Exchange(name)
        h = L.side
        for a, b in WIDE if far else AROUND:
            w = {0: L.nx, 1: near, 2: far}[abs(a)]
            xs = sx0 + (L.nx - w if a > 0 else 0)
            xd = {0: L.x0, 1: L.x0 - w, 2: L.x0 - L.nx - w, -1: L.x0 + L.nx, -2: L.x0 + 2 * L.nx}[a]
            ys = h + (L.ny - h if b > 0 else 0)
            yd, wy = {0: (h, L.ny), 1: (0, h), -1: (h + L.ny, h)}[b]
            both.add(src.at[pl.ds(xs, w), :, pl.ds(ys, wy), :], dst.at[pl.ds(xd, w), :, pl.ds(yd, wy), :], a, b)
        return both.start()

    peers = [(0, b) for b in LINE if 1 < b < gy_size - 1] + WIDE
    barrier = pltpu.get_barrier_semaphore()
    for a, b in peers:
        pl.semaphore_signal(barrier, inc=1, device_id=device(a, b), device_id_type=MESH)

    fields = (M[0]["NK"], M[0]["NS"], S["smooth0"])
    XP, YP, XR, YR = S["xp"], S["yp"], S["xr"], S["yr"]
    sub, lane = sublanes(), lanes()

    loads = [pltpu.make_async_copy(inverse, S["inverse"], S["local"].at[4])]
    for n, src in enumerate((conductance, source)):
        for r in range(2):
            loads.append(
                pltpu.make_async_copy(
                    src.at[:, :, pl.ds(128 * r, 128)],
                    fields[n].at[pl.ds(4, 16), r, pl.ds(8, 32), :],
                    S["local"].at[2 * n + r],
                )
            )
    for copy in loads:
        copy.start()

    def pack(a, field, first):
        def pack_x(i, _):
            for r in range(2):
                XP[a, 0, i, r] = field[first + i, r, 8:40, :].astype(BF16)
                XP[a, 1, i, r] = field[first + 12 + i, r, 8:40, :].astype(BF16)

        def pack_y(i, _):
            low, high = [], []
            for d in range(2):
                x = first + 2 * i + d
                near, far = field[x, 0, 8:16, :], field[x, 1, 8:16, :]
                low.append(jnp.where(sub < 4, near, turn(far, 4, 0)))
                near, far = field[x, 0, 32:40, :], field[x, 1, 32:40, :]
                high.append(jnp.where(sub < 4, turn(near, 4, 0), far))
            YP[a, 0, i] = jnp.concatenate(low, axis=0).astype(BF16)
            YP[a, 1, i] = jnp.concatenate(high, axis=0).astype(BF16)

        loop(0, 4, pack_x)
        loop(0, 8, pack_y)

    def sides(a, name):
        both = Exchange(name)
        for x, y in AROUND:
            if y == 0:
                both.add(XP.at[a, (x + 1) // 2], XR.at[a, (1 - x) // 2], x, y)
            else:
                wx = 8 if x == 0 else 2 if a == 0 else 1
                xs, xd = {0: (0, 2), 1: (8 - wx, 2 - wx), -1: (0, 10)}[x]
                both.add(YP.at[a, (y + 1) // 2, pl.ds(xs, wx)], YR.at[a, (1 - y) // 2, pl.ds(xd, wx)], x, y)
        return both.start()

    def unpack(a):
        field = fields[a]

        def unpack_x(i, _):
            for r in range(2):
                field[i, r, 8:40, :] = XR[a, 0, i, r].astype(F32)
                field[20 + i, r, 8:40, :] = XR[a, 1, i, r].astype(F32)

        def unpack_y(i, _):
            low, high = YR[a, 0, i].astype(F32), YR[a, 1, i].astype(F32)
            for d in range(2):
                x = 2 * i + d
                part = low[8 * d : 8 * d + 8]
                field[x, 0, 0:8, :] = turn(part, 4, 0)
                field[x, 1, 0:8, :] = part
                part = high[8 * d : 8 * d + 8]
                field[x, 0, 40:48, :] = part
                field[x, 1, 40:48, :] = turn(part, 4, 0)

        loop(0, 4, unpack_x)
        loop(0, 12, unpack_y)

    for a in range(2):
        loads[1 + 2 * a].wait()
        loads[2 + 2 * a].wait()
        pack(a, fields[a], 4)

    pl.semaphore_wait(barrier, len(peers))
    side_k = sides(0, "side_k")
    side_s = sides(1, "side_s")

    def halve(field, packed):
        packed[12:20, 0, 16:32, :] = field[12:20, 0, 16:32, :].astype(BF16)

    def widen(packed, field, margin, beside):
        def take(parts):
            def body(x, U):
                for u in range(U):
                    for rows in parts:
                        field[x + u, 0, rows, :] = packed[x + u, 0, rows, :].astype(F32)

            return body

        loop(12 - margin, 12, take(beside), 12)
        loop(12, 20, take((pl.ds(0, 16), pl.ds(32, 16))), 8)
        loop(20, 20 + margin, take(beside), 12)

    loop(0, 8, coarsen(L0, M[0]["NK"].at[pl.ds(4, 16)], 8, 2, 0.125, put_rows(M[1]["NK"], 12, 16)), 4)
    halve(M[1]["NK"], S["k1"])

    loads[0].wait()
    one = lambda mask: jnp.where(mask, 1.0, 0.0).astype(BF16)
    row = lax.broadcasted_iota(jnp.int32, (128, 128), 0)
    column = lax.broadcasted_iota(jnp.int32, (128, 128), 1)
    order = one(row == ((column >> 2) & 1) * 64 + (column >> 3) * 4 + (column & 3))
    for k in range(2):
        S["mp"][128 * k : 128 * (k + 1), :] = jnp.dot(
            S["inverse"][0, k], order, preferred_element_type=F32
        ).astype(BF16)

    row = lax.broadcasted_iota(jnp.int32, (4, 48, 256), 1)
    column = lax.broadcasted_iota(jnp.int32, (4, 48, 256), 2)
    layer = jnp.where(row >= 24, 1, 0)
    row = row - 24 * layer
    half = jnp.where(row >= 12, 1, 0)
    row = row - 12 * half + 4 * lax.broadcasted_iota(jnp.int32, (4, 48, 256), 0)
    base = layer * 128 + half * 64

    def share(d, _):
        chosen = one(column == base + ((row + (16 * d + 60)) & 63)).reshape(192, 256)
        rows = jnp.dot(chosen, S["mp"][...], preferred_element_type=F32)
        S["ms"][pl.ds(4 * d, 4)] = rows.astype(BF16).reshape(4, 48, 128)

    loop(0, gy_size // 4, share)
    kappa_1 = exchange(L1, S["k1"], 12, S["k1"], 8, 4, "kappa_1")

    place = (gx, gy, gx_size, gy_size)
    side_k.arrive()
    unpack(0)
    prepare(L0, M[0], 1, 23, *place)
    side_s.arrive()
    unpack(1)
    scale_source(L0, M[0], "NS", 1, 23, True)
    descend(L0, M[0], 0, S["keep0"])
    residual = M[0]["RN"].at[pl.ds(4, 16)]
    loop(0, 8, coarsen(L0, residual, 8, 2, 0.5, put_rows(M[1]["NS"], 12, 16)), 4)
    halve(M[1]["NS"], S["s1"])
    for i in range(4):
        for side in range(2):
            rows = pl.ds(16 + 8 * side, 8)
            both = [M[1]["NS"][12 + 2 * i + d, 0, rows, :] for d in range(2)]
            S["cp"][side, i] = jnp.concatenate(both, axis=0).astype(BF16)
    source_1 = Exchange("source_1")
    for a in (-1, 1):
        for b in (-1, 1):
            source_1.add(S["cp"].at[(b + 1) // 2], S["cr"].at[(1 - b) // 2, (1 - a) // 2], a, b)
    own = pl.ds(16, 16)
    for a, xs, xd, w in ((-2, 12, 28, 1), (2, 19, 3, 1), (-1, 12, 20, 8), (1, 12, 4, 8)):
        source_1.add(S["s1"].at[pl.ds(xs, w), :, own, :], S["s1"].at[pl.ds(xd, w), :, own, :], a, 0)
    own = S["s1"].at[pl.ds(12, 8), :, pl.ds(16, 16), :]
    for b in (-1, 1):
        source_1.add(own, S["s1"].at[pl.ds(12, 8), :, pl.ds(16 - 16 * b, 16), :], 0, b)
    source_1.start()

    kappa_1.arrive()
    widen(S["k1"], M[1]["NK"], 12, (pl.ds(0, 48),))
    prepare(L1, M[1], 3, 29, *place)
    loop(0, 16, coarsen(L1, M[1]["NK"], 0, 3, 0.125, put_rows(M[2]["NK"], 2, 0)), 8)
    prepare(L2, M[2], 3, 17, *place)
    matrices = Exchange("matrix")
    for n in LINE:
        matrices.add(S["ms"].at[lax.rem(gy + n, gy_size)], S["mm"].at[gy], 0, n)
    matrices.start()
    S["mm"][gy] = S["ms"][gy]
    pack(2, S["keep0"], 1)
    side_v = sides(2, "side_v")

    source_1.arrive()
    widen(S["s1"], M[1]["NS"], 9, (pl.ds(16, 16),))
    for i in range(4):
        for ys in range(2):
            for xs in range(2):
                both = S["cr"][ys, xs, i].astype(F32)
                for d in range(2):
                    M[1]["NS"][4 + 16 * xs + 2 * i + d, 0, pl.ds(8 + 24 * ys, 8), :] = both[8 * d : 8 * d + 8]
    scale_source(L1, M[1], "NS", 3, 29, True)
    descend(L1, M[1], 6)

    residual = M[1]["RN"].at[pl.ds(6, 20)]
    loop(0, 10, coarsen(L1, residual, 0, 3, 0.5, put_rows(S["s2"], 5, 0)), 5)
    scale_source(L2, M[2], "s2", 5, 15, True)
    descend(L2, M[2], 0, S["keep2"])
    tiles = []
    residual = M[2]["RN"].at[pl.ds(8, 4)]
    loop(0, 2, coarsen(L2, residual, 8, 1, 1.0 / 128.0, lambda x, t, value: tiles.append(value)), 2)
    rounded = jnp.where(sub < 4, tiles[0], turn(tiles[1], 4, 0)).astype(BF16).astype(F32)
    S["mine"][...] = rounded
    gathered = Exchange("gather")
    for n in LINE:
        gathered.add(S["mine"], S["all"].at[gy], 0, n)
    gathered.start()
    odd = (lanes(4) & 1) == 1
    pair = S["pair"]
    pair[8:12, 0, 8:16, :] = jnp.where(odd, S["keep2"][1:5, 0, 8:16, :], S["s2"][8:12, 0, 8:16, :])
    level_2 = exchange(L2, pair, 8, pair, 4, 4, "level_2")
    S["all"][gy] = rounded

    kept = pltpu.make_async_copy(
        S["keep0"].at[pl.ds(1, 16), :, pl.ds(8, 32), :],
        S["smooth0"].at[pl.ds(4, 16), :, pl.ds(8, 32), :],
        S["local"].at[0],
    )
    kept.start()
    for old in (side_k, side_s, kappa_1, source_1, matrices, side_v):
        old.left()
    side_v.arrive()
    unpack(2)
    kept.wait()
    matrices.arrive()
    gathered.arrive()
    right = S["all"][...].reshape(gy_size * 8, 128).astype(BF16)
    product = jnp.dot(S["mm"][...].reshape(gy_size * 48, 128), right, preferred_element_type=F32)
    layer_of = lax.broadcasted_iota(jnp.int32, (24, 128), 1) >> 2
    terms = [jnp.where(layer_of == k, product[24 * k : 24 * k + 24], 0.0) for k in range(2 * gy_size)]
    while len(terms) > 1:
        terms = [terms[i] + terms[i + 1] for i in range(0, len(terms), 2)]
    S["corr"][2] = terms[0]
    coarse = Exchange("coarse")
    for a in (-2, -1, 1, 2):
        coarse.add(S["corr"].at[2], S["corr"].at[2 - a], a, 0)
    coarse.start()
    gathered.left()
    level_2.left()
    level_2.arrive()

    def part(x, U):
        for u in range(U):
            for t in range(3):
                rows = pl.ds(8 * t, 8)
                both = pair[x + u, 0, rows, :]
                second = (lane & 1) == 1
                M[2]["NS"][x + u, 0, rows, :] = jnp.where(second, turn(both, 1, 1), both)
                S["smooth2"][x + u, 0, rows, :] = jnp.where(second, both, turn(both, -1, 1))

    loop(2, 18, part, 8)
    scale_source(L2, M[2], "NS", 3, 17, False)
    coarse.arrive()

    for slab in range(5):
        for d in range(2):
            for b in range(2):
                M[2]["E"][2 * slab + d, 0, pl.ds(b, 8, stride=2), :] = S["corr"][slab, 12 * d : 12 * d + 8, :]
                M[2]["E"][2 * slab + d, 0, pl.ds(16 + b, 4, stride=2), :] = S["corr"][slab, 12 * d + 8 : 12 * d + 12, :]

    def emit_2(x, new):
        for j in range(L2.J):
            for b in range(2):
                M[1]["E"][x, 0, pl.ds(2 * j + b, 8, stride=2 * L2.J), :] = new[0][j]

    def emit_1(x, new):
        for j in range(L1.J):
            for r in range(2):
                value = pick(new[0][j], (lane >> 1) + 64 * r)
                for b in range(2):
                    M[0]["E"][x, r, pl.ds(2 * j + b, 8, stride=2 * L1.J), :] = value

    def emit_0(x, new):
        for r in range(2):
            for j in range(L0.J):
                S["result"][x - L0.x0, r, rows_of(L0, j), :] = new[r][j]

    ascend(L2, M[2], 6, emit_2, S["smooth2"])
    ascend(L1, M[1], 5, emit_1)
    stores = []

    def store(n):
        for r in range(2):
            copy = pltpu.make_async_copy(
                S["result"].at[pl.ds(8 * n, 8), r, pl.ds(8, 32), :],
                out.at[pl.ds(8 * n, 8), :, pl.ds(128 * r, 128)],
                S["local"].at[2 * n + r],
            )
            copy.start()
            stores.append(copy)

    ascend(L0, M[0], 3, emit_0, S["smooth0"], 2, store)
    coarse.left()
    for copy in stores:
        copy.wait()


def solution(mesh):
    gx_size, gy_size = mesh.shape["gx"], mesh.shape["gy"]
    scratch = {}
    for l, L in enumerate(LEVELS):
        for name, shape in L.scratch().items():
            scratch[str(l) + name] = shape
    scratch["xp"] = pltpu.VMEM((3, 2, 4, 2, 32, 128), BF16)
    scratch["xr"] = pltpu.VMEM((3, 2, 4, 2, 32, 128), BF16)
    scratch["yp"] = pltpu.VMEM((3, 2, 8, 16, 128), BF16)
    scratch["yr"] = pltpu.VMEM((3, 2, 12, 16, 128), BF16)
    scratch["k1"] = pltpu.VMEM((32, 1, 48, 128), BF16)
    scratch["s1"] = pltpu.VMEM((32, 1, 48, 128), BF16)
    scratch["cp"] = pltpu.VMEM((2, 4, 16, 128), BF16)
    scratch["cr"] = pltpu.VMEM((2, 2, 4, 16, 128), BF16)
    scratch["s2"] = pltpu.VMEM((20, 1, 24, 128), F32)
    scratch["keep0"] = pltpu.VMEM((18, 2, 48, 128), F32)
    scratch["smooth0"] = pltpu.VMEM((24, 2, 48, 128), F32)
    scratch["keep2"] = pltpu.VMEM((6, 1, 24, 128), F32)
    scratch["pair"] = pltpu.VMEM((20, 1, 24, 128), F32)
    scratch["smooth2"] = pltpu.VMEM((20, 1, 24, 128), F32)
    scratch["size"] = pltpu.VMEM((768, 128), F32)
    scratch["inverse"] = pltpu.VMEM((1, 2, 128, 128), BF16)
    scratch["mp"] = pltpu.VMEM((256, 128), BF16)
    scratch["ms"] = pltpu.VMEM((gy_size, 48, 128), BF16)
    scratch["mm"] = pltpu.VMEM((gy_size, 48, 128), BF16)
    scratch["mine"] = pltpu.VMEM((8, 128), F32)
    scratch["all"] = pltpu.VMEM((gy_size, 8, 128), F32)
    scratch["corr"] = pltpu.VMEM((5, 24, 128), F32)
    scratch["result"] = pltpu.VMEM((16, 2, 48, 128), F32)
    scratch["local"] = pltpu.SemaphoreType.DMA((5,))
    for name in EXCHANGES:
        scratch["send_" + name] = pltpu.SemaphoreType.DMA
        scratch["recv_" + name] = pltpu.SemaphoreType.DMA

    def local(pressure_source, conductance, coarse_inverse):
        return pl.pallas_call(
            functools.partial(kernel, gx_size, gy_size, tuple(scratch)),
            out_shape=pltpu.VMEM(pressure_source.shape, F32),
            in_specs=[
                pl.BlockSpec(memory_space=pl.ANY),
                pl.BlockSpec(memory_space=pl.ANY),
                pl.BlockSpec(memory_space=pl.ANY),
            ],
            out_specs=pl.BlockSpec(memory_space=pl.ANY),
            scratch_shapes=list(scratch.values()),
            compiler_params=pltpu.CompilerParams(
                collective_id=0, has_side_effects=True, vmem_limit_bytes=40 * 2**20
            ),
        )(*(pltpu.with_memory_space_constraint(x, pltpu.HBM) for x in (pressure_source, conductance, coarse_inverse)))

    in_specs = (P("gx", "gy", None), P("gx", "gy", None), P("gx", "gy", None, None))
    return jax.shard_map(local, mesh=mesh, in_specs=in_specs, out_specs=P("gx", "gy", None), check_vma=False)
```

```python
import functools
import math

import jax
import jax.numpy as jnp
from jax import lax
from jax.experimental import pallas as pl
from jax.experimental.pallas import tpu as pltpu
from jax.sharding import PartitionSpec as P

MESH = pl.DeviceIdType.MESH

LMAX = 2.0
LMIN = 0.25
THETA = 0.5 * (LMAX + LMIN)
DELTA = 0.5 * (LMAX - LMIN)
SIGMA = THETA / DELTA
RATIO_0 = 1.0 / SIGMA
RATIO_1 = 1.0 / (2.0 * SIGMA - RATIO_0)
RATIO_2 = 1.0 / (2.0 * SIGMA - RATIO_1)
STEP_1 = (RATIO_1 * RATIO_0, 2.0 * RATIO_1 / DELTA)
STEP_2 = (RATIO_2 * RATIO_1, 2.0 * RATIO_2 / DELTA)

F32 = jnp.float32
BF16 = jnp.bfloat16

EXCHANGES = ("side_k", "side_s", "side_v", "kappa_1", "matrix", "source_1", "gather", "level_2", "coarse")
AROUND = [(a, b) for a in (-1, 0, 1) for b in (-1, 0, 1) if (a, b) != (0, 0)]
WIDE = [(a, b) for a in (-2, -1, 0, 1, 2) for b in (-1, 0, 1) if (a, b) != (0, 0)]
AROUND.sort(key=lambda o: -abs(o[0]) - 2 * abs(o[1]))
WIDE.sort(key=lambda o: -abs(o[0]) - 2 * abs(o[1]))
LINE = sorted(range(1, 16), key=lambda n: -min(n // 4, 4 - n // 4) - min(n % 4, 4 - n % 4))


class Level:
    def __init__(self, nx, ny, x0, side, R, J, hold, row0, erow, xc, coarse, most):
        self.nx, self.ny, self.X, self.x0, self.side = nx, ny, nx + 2 * x0, x0, side
        self.R, self.J, self.hold, self.row0, self.most = R, J, hold, row0, most
        self.erow, self.xc, self.coarse = erow, xc, coarse
        self.rows = ny + 2 * side

    def scratch(self):
        X, R, J = self.X, self.R, self.J
        vm = lambda *shape: pltpu.VMEM(shape + (128,), F32)
        blocked = {name: vm(X, R, J, 8) for name in ("CM", "CP", "Q", "G", "D", "DIR")}
        natural = {name: vm(X, R, self.rows) for name in ("NS", "NK", "RN")}
        return dict(
            E=vm(self.coarse[0], R, self.coarse[1]),
            HK=vm(X, R, J + 2, 8),
            CX=vm(X + 1, R, J, 8),
            CY=vm(X, R, J + 1, 8),
            VA=vm(X, R, J + 2, 8),
            VB=vm(X, R, J + 2, 8),
            **blocked,
            **natural,
        )


LEVELS = (
    Level(16, 32, 4, 8, 2, 5, 1, 4, 20, 10, (32, 80), 10),
    Level(8, 16, 12, 16, 1, 5, 1, 4, 4, 2, (20, 48), 12),
    Level(4, 8, 8, 8, 1, 3, 2, 0, 0, 0, (10, 24), 16),
)


def lanes(*lead):
    return lax.broadcasted_iota(jnp.int32, lead + (8, 128), len(lead) + 1)


def sublanes():
    return lax.broadcasted_iota(jnp.int32, (8, 128), 0)


def turn(value, shift, axis):
    return pltpu.roll(value, shift % value.shape[axis], axis)


def pick(value, index):
    return jnp.take_along_axis(value, index, axis=1, mode="promise_in_bounds")


def rows_of(L, j):
    return pl.ds(L.row0 + j, 8, stride=L.J)


def beside_z(L, parts):
    h = L.hold
    down = [turn(p, h, 2) for p in parts]
    up = [turn(p, -h, 2) for p in parts]
    if L.R == 2:
        lane = lanes(L.J)
        down[1] = jnp.where(lane == 0, down[0], down[1])
        up[0] = jnp.where(lane == 127, up[1], up[0])
    return down, up


def store_wrapped(ref, x, r, J, values):
    ref[x, r, 1 : J + 1] = values
    ref[x, r, 0] = turn(values[J - 1], 1, 0)
    ref[x, r, J + 1] = turn(values[0], -1, 0)


def rows_from(L, ref, x, r):
    return jnp.stack([ref[x, r, rows_of(L, j), :] for j in range(L.J)])


def rows_to(L, ref, x, r, values):
    for j in range(L.J):
        ref[x, r, rows_of(L, j), :] = values[j]


def loop(lo, hi, body, most=1):
    count = hi - lo
    steps = -(-count // most)
    U = -(-count // steps)
    whole = count // U
    if whole > 1:

        def step(i, carry):
            body(lo + i * U, U)
            return carry

        lax.fori_loop(0, whole, step, 0)
    elif whole == 1:
        body(lo, U)
    if count > whole * U:
        body(lo + whole * U, count - whole * U)


def prepare(L, M, lo, hi, gx, gy, count_x, count_y):
    J, R, h = L.J, L.R, L.hold
    shape = (J, 8, 128)
    lane = lanes(J)
    place = lax.broadcasted_iota(jnp.int32, shape, 0) + J * lax.broadcasted_iota(jnp.int32, shape, 1)
    place = place + (gy * L.ny - L.side + L.row0)
    keep = jnp.where((place >= 0) & (place < L.ny * count_y), 0.5, 0.0).astype(F32)

    def halves(x, U):
        NK, HK = M["NK"].at[pl.ds(x, U)], M["HK"].at[pl.ds(x, U)]
        for u in range(U):
            place = gx * L.nx + x + u - L.x0
            inside = jnp.where((place >= 0) & (place < L.nx * count_x), 1.0, 0.0).astype(F32)
            mask = keep * inside
            for r in range(R):
                store_wrapped(HK, u, r, J, rows_from(L, NK, u, r) * mask)

    loop(lo - 1, hi + 1, halves, L.most)
    for r in range(R):
        M["CX"][lo, r] = M["HK"][lo - 1, r, 1 : J + 1] + M["HK"][lo, r, 1 : J + 1]

    def couple(x, U):
        HK, CX = M["HK"].at[pl.ds(x - 1, U + 2)], M["CX"].at[pl.ds(x, U + 1)]
        CY, CM, CP, D, Q = (M[name].at[pl.ds(x, U)] for name in ("CY", "CM", "CP", "D", "Q"))
        for u in range(U):
            mine = [HK[u + 1, r, 1 : J + 1] for r in range(R)]
            down, up = beside_z(L, mine)
            down[0] = jnp.where(lane < h, 0.0, down[0])
            up[R - 1] = jnp.where(lane >= 128 - h, 0.0, up[R - 1])
            for r in range(R):
                c = mine[r]
                xm, xp = HK[u, r, 1 : J + 1], HK[u + 2, r, 1 : J + 1]
                ym, yp = HK[u + 1, r, 0:J], HK[u + 1, r, 2 : J + 2]
                diagonal = (xm + xp) + (ym + yp) + (down[r] + up[r]) + 6.0 * c
                CX[u + 1, r] = c + xp
                CY[u, r, 0:J] = c + ym
                CY[u, r, J] = c[J - 1] + yp[J - 1]
                low, high = c + down[r], c + up[r]
                if r == 0:
                    low = jnp.where(lane < h, 0.0, low)
                if r == R - 1:
                    high = jnp.where(lane >= 128 - h, 0.0, high)
                CM[u, r] = low
                CP[u, r] = high
                D[u, r] = diagonal
                Q[u, r] = jnp.where(c > 0.0, 1.0 / diagonal, 0.0)

    loop(lo, hi, couple, L.most)


def scale_source(L, M, name, lo, hi, start):
    J, field = L.J, M[name]

    def body(x, U):
        Q, G, VA, NS = (ref.at[pl.ds(x, U)] for ref in (M["Q"], M["G"], M["VA"], field))
        for u in range(U):
            for r in range(L.R):
                g = Q[u, r] * rows_from(L, NS, u, r)
                G[u, r] = g
                if start:
                    store_wrapped(VA, u, r, J, g * (1.0 / THETA))

    loop(lo, hi, body, L.most)


def sweep(L, M, src, dst, lo, hi, kind, step=None, keep_rows=None, emit=None):
    J, R = L.J, L.R

    def body(x, U):
        V, CX = M[src].at[pl.ds(x - 1, U + 2)], M["CX"].at[pl.ds(x, U + 1)]
        CY, CM, CP, D, Q, G, DIR = (M[name].at[pl.ds(x, U)] for name in ("CY", "CM", "CP", "D", "Q", "G", "DIR"))
        if dst is not None:
            W = M[dst].at[pl.ds(x, U)]
        if kind == "residual":
            RN = M["RN"].at[pl.ds(x, U)]
        if keep_rows is not None:
            kept = keep_rows.at[pl.ds(x - L.x0 + 1, U)]
        for u in range(U):
            mine = [V[u + 1, r, 1 : J + 1] for r in range(R)]
            down, up = beside_z(L, mine)
            new = []
            for r in range(R):
                c = mine[r]
                near = CX[u, r] * V[u, r, 1 : J + 1] + CX[u + 1, r] * V[u + 2, r, 1 : J + 1]
                near = near + (CY[u, r, 0:J] * V[u + 1, r, 0:J] + CY[u, r, 1 : J + 1] * V[u + 1, r, 2 : J + 2])
                near = near + (CM[u, r] * down[r] + CP[u, r] * up[r])
                update = (G[u, r] - c) + Q[u, r] * near
                if kind == "residual":
                    rows_to(L, RN, u, r, D[u, r] * update)
                    continue
                if kind == "first":
                    direction = update * (1.0 / THETA)
                elif kind == "from_zero":
                    direction = step[0] * c + step[1] * update
                else:
                    direction = step[0] * DIR[u, r] + step[1] * update
                if kind != "last":
                    DIR[u, r] = direction
                value = c + direction
                if dst is not None:
                    store_wrapped(W, u, r, J, value)
                if keep_rows is not None:
                    rows_to(L, kept, u, r, value)
                new.append(value)
            if emit is not None:
                emit(x + u, new)

    loop(lo, hi, body, L.most)


def descend(L, M, margin, keep_rows=None):
    lo, hi = L.x0 - margin, L.x0 + L.nx + margin
    sweep(L, M, "VA", "VB", lo - 2, hi + 2, "from_zero", STEP_1)
    sweep(L, M, "VB", "VA", lo - 1, hi + 1, "last", STEP_2, keep_rows=keep_rows)
    sweep(L, M, "VA", None, lo, hi, "residual")


def ascend(L, M, margin, emit, smoothed=None, pieces=1, after=lambda n: None):
    lo, hi = L.x0, L.x0 + L.nx

    def begin(x, U):
        HK, VA = (M[name].at[pl.ds(x, U)] for name in ("HK", "VA"))
        if smoothed is not None:
            NV = smoothed.at[pl.ds(x, U)]
        for u in range(U):
            xc = lax.shift_right_logical(x + u, 1) + L.xc
            for r in range(L.R):
                added = [M["E"][xc, r, pl.ds(L.erow + j, 8, stride=L.J), :] for j in range(L.J)]
                base = VA[u, r, 1 : L.J + 1] if smoothed is None else rows_from(L, NV, u, r)
                inside = HK[u, r, 1 : L.J + 1] > 0.0
                store_wrapped(VA, u, r, L.J, jnp.where(inside, jnp.stack(added) + base, 0.0))

    loop(lo - margin, hi + margin, begin, L.most)
    margin -= 1
    sweep(L, M, "VA", "VB", lo - margin, hi + margin, "first")
    margin -= 1
    sweep(L, M, "VB", "VA", lo - margin, hi + margin, "next", STEP_1)
    margin -= 1
    width = (hi - lo + 2 * margin) // pieces
    for n in range(pieces):
        first = lo - margin + n * width
        sweep(L, M, "VA", None, first, first + width, "last", STEP_2, emit=emit)
        after(n)


def coarsen(L, src, row, tiles, scale, put):
    lane = lanes()
    even = (lane * 2) & 127

    def body(x, U):
        pairs = src.at[pl.ds(2 * x, 2 * U)]
        for u, t in [(u, t) for u in range(U) for t in range(tiles)]:
            sums = []
            for r in range(L.R):
                rows = [pairs[2 * u + dx, r, pl.ds(row + 16 * t + b, 8, stride=2), :] for dx in (0, 1) for b in (0, 1)]
                total = (rows[0] + rows[1]) + (rows[2] + rows[3])
                if L.R == 2:
                    sums.append(pick(total + turn(total, -1, 1), even))
                else:
                    other = jnp.where((lane & L.hold) == 0, turn(total, -L.hold, 1), turn(total, L.hold, 1))
                    sums.append(total + other)
            value = jnp.where(lane < 64, sums[0], sums[1]) if L.R == 2 else sums[0]
            put(x + u, t, value * scale)

    return body


def put_rows(dst, dx, row):
    def put(x, t, value):
        dst[dx + x, 0, row + 8 * t : row + 8 * t + 8, :] = value

    return put


def kernel(gx_size, gy_size, names, source, conductance, inverse, out, *refs):
    S = dict(zip(names, refs))
    M = [{k[1:]: v for k, v in S.items() if k[0] == str(l)} for l in range(3)]
    M[2]["s2"] = S["s2"]
    gx, gy = lax.axis_index("gx"), lax.axis_index("gy")
    L0, L1, L2 = LEVELS

    def device(a, b):
        return {"gx": lax.rem(gx + a + gx_size, gx_size), "gy": lax.rem(gy + b + gy_size, gy_size)}

    class Exchange:
        def __init__(self, name):
            self.out, self.back, self.rows, self.copies = S["send_" + name], S["recv_" + name], 0, []

        def add(self, src, dst, a, b):
            copy = pltpu.make_async_remote_copy(
                src_ref=src, dst_ref=dst, send_sem=self.out, recv_sem=self.back, device_id=device(a, b), device_id_type=MESH
            )
            self.copies.append(copy)
            rows = math.prod(src.shape[:-1])
            self.rows += rows if src.dtype == F32 else rows // 2

        def start(self):
            for copy in self.copies:
                copy.start()
            return self

        def wait(self, semaphore):
            size = S["size"].at[pl.ds(0, self.rows)]
            pltpu.make_async_copy(size, size, semaphore).wait()

        def arrive(self):
            self.wait(self.back)

        def left(self):
            self.wait(self.out)

    def exchange(L, src, sx0, dst, near, far, name):
        both = Exchange(name)
        h = L.side
        for a, b in WIDE if far else AROUND:
            w = {0: L.nx, 1: near, 2: far}[abs(a)]
            xs = sx0 + (L.nx - w if a > 0 else 0)
            xd = {0: L.x0, 1: L.x0 - w, 2: L.x0 - L.nx - w, -1: L.x0 + L.nx, -2: L.x0 + 2 * L.nx}[a]
            ys = h + (L.ny - h if b > 0 else 0)
            yd, wy = {0: (h, L.ny), 1: (0, h), -1: (h + L.ny, h)}[b]
            both.add(src.at[pl.ds(xs, w), :, pl.ds(ys, wy), :], dst.at[pl.ds(xd, w), :, pl.ds(yd, wy), :], a, b)
        return both.start()

    peers = [(0, b) for b in LINE if 1 < b < gy_size - 1] + AROUND
    barrier = pltpu.get_barrier_semaphore()
    for a, b in peers:
        pl.semaphore_signal(barrier, inc=1, device_id=device(a, b), device_id_type=MESH)

    fields = (M[0]["NK"], M[0]["NS"], S["smooth0"])
    XP, YP, XR, YR = S["xp"], S["yp"], S["xr"], S["yr"]
    sub, lane = sublanes(), lanes()

    loads = [pltpu.make_async_copy(inverse, S["inverse"], S["local"].at[4])]
    for n, src in enumerate((conductance, source)):
        for r in range(2):
            loads.append(
                pltpu.make_async_copy(
                    src.at[:, :, pl.ds(128 * r, 128)],
                    fields[n].at[pl.ds(4, 16), r, pl.ds(8, 32), :],
                    S["local"].at[2 * n + r],
                )
            )
    for copy in loads:
        copy.start()

    def pack(a, field, first):
        def pack_x(i, _):
            for r in range(2):
                XP[a, 0, i, r] = field[first + i, r, 8:40, :].astype(BF16)
                XP[a, 1, i, r] = field[first + 12 + i, r, 8:40, :].astype(BF16)

        def pack_y(i, _):
            low, high = [], []
            for d in range(2):
                x = first + 2 * i + d
                near, far = field[x, 0, 8:16, :], field[x, 1, 8:16, :]
                low.append(jnp.where(sub < 4, near, turn(far, 4, 0)))
                near, far = field[x, 0, 32:40, :], field[x, 1, 32:40, :]
                high.append(jnp.where(sub < 4, turn(near, 4, 0), far))
            YP[a, 0, i] = jnp.concatenate(low, axis=0).astype(BF16)
            YP[a, 1, i] = jnp.concatenate(high, axis=0).astype(BF16)

        loop(0, 4, pack_x)
        loop(0, 8, pack_y)

    def sides(a, name):
        both = Exchange(name)
        for x, y in AROUND:
            if y == 0:
                both.add(XP.at[a, (x + 1) // 2], XR.at[a, (1 - x) // 2], x, y)
            else:
                wx = 8 if x == 0 else 2 if a == 0 else 1
                xs, xd = {0: (0, 2), 1: (8 - wx, 2 - wx), -1: (0, 10)}[x]
                both.add(YP.at[a, (y + 1) // 2, pl.ds(xs, wx)], YR.at[a, (1 - y) // 2, pl.ds(xd, wx)], x, y)
        return both.start()

    def unpack(a):
        field = fields[a]

        def unpack_x(i, _):
            for r in range(2):
                field[i, r, 8:40, :] = XR[a, 0, i, r].astype(F32)
                field[20 + i, r, 8:40, :] = XR[a, 1, i, r].astype(F32)

        def unpack_y(i, _):
            low, high = YR[a, 0, i].astype(F32), YR[a, 1, i].astype(F32)
            for d in range(2):
                x = 2 * i + d
                part = low[8 * d : 8 * d + 8]
                field[x, 0, 0:8, :] = turn(part, 4, 0)
                field[x, 1, 0:8, :] = part
                part = high[8 * d : 8 * d + 8]
                field[x, 0, 40:48, :] = part
                field[x, 1, 40:48, :] = turn(part, 4, 0)

        loop(0, 4, unpack_x)
        loop(0, 12, unpack_y)

    for a in range(2):
        loads[1 + 2 * a].wait()
        loads[2 + 2 * a].wait()
        pack(a, fields[a], 4)

    pl.semaphore_wait(barrier, len(peers))
    side_k = sides(0, "side_k")
    side_s = sides(1, "side_s")
    for a in (-1, 1):
        pl.semaphore_signal(S["ready"], inc=1, device_id=device(a, 0), device_id_type=MESH)

    def halve(field, packed):
        packed[12:20, 0, 16:32, :] = field[12:20, 0, 16:32, :].astype(BF16)

    def widen(packed, field, margin, beside):
        def take(parts):
            def body(x, U):
                for u in range(U):
                    for rows in parts:
                        field[x + u, 0, rows, :] = packed[x + u, 0, rows, :].astype(F32)

            return body

        loop(12 - margin, 12, take(beside), 12)
        loop(12, 20, take((pl.ds(0, 16), pl.ds(32, 16))), 8)
        loop(20, 20 + margin, take(beside), 12)

    loop(0, 8, coarsen(L0, M[0]["NK"].at[pl.ds(4, 16)], 8, 2, 0.125, put_rows(M[1]["NK"], 12, 16)), 4)
    halve(M[1]["NK"], S["k1"])

    loads[0].wait()
    one = lambda mask: jnp.where(mask, 1.0, 0.0).astype(BF16)
    row = lax.broadcasted_iota(jnp.int32, (128, 128), 0)
    column = lax.broadcasted_iota(jnp.int32, (128, 128), 1)
    order = one(row == ((column >> 2) & 1) * 64 + (column >> 3) * 4 + (column & 3))
    for k in range(2):
        S["mp"][128 * k : 128 * (k + 1), :] = jnp.dot(
            S["inverse"][0, k], order, preferred_element_type=F32
        ).astype(BF16)

    row = lax.broadcasted_iota(jnp.int32, (4, 48, 256), 1)
    column = lax.broadcasted_iota(jnp.int32, (4, 48, 256), 2)
    layer = jnp.where(row >= 24, 1, 0)
    row = row - 24 * layer
    half = jnp.where(row >= 12, 1, 0)
    row = row - 12 * half + 4 * lax.broadcasted_iota(jnp.int32, (4, 48, 256), 0)
    base = layer * 128 + half * 64

    def share(d, _):
        chosen = one(column == base + ((row + (16 * d + 60)) & 63)).reshape(192, 256)
        rows = jnp.dot(chosen, S["mp"][...], preferred_element_type=F32)
        S["ms"][pl.ds(4 * d, 4)] = rows.astype(BF16).reshape(4, 48, 128)

    loop(0, gy_size // 4, share)
    pl.semaphore_wait(S["ready"], 2)
    kappa_1 = exchange(L1, S["k1"], 12, S["k1"], 8, 4, "kappa_1")

    place = (gx, gy, gx_size, gy_size)
    side_k.arrive()
    unpack(0)
    prepare(L0, M[0], 1, 23, *place)
    side_s.arrive()
    unpack(1)
    scale_source(L0, M[0], "NS", 1, 23, True)
    descend(L0, M[0], 0, S["keep0"])
    residual = M[0]["RN"].at[pl.ds(4, 16)]
    loop(0, 8, coarsen(L0, residual, 8, 2, 0.5, put_rows(M[1]["NS"], 12, 16)), 4)
    halve(M[1]["NS"], S["s1"])
    for i in range(4):
        for side in range(2):
            rows = pl.ds(16 + 8 * side, 8)
            both = [M[1]["NS"][12 + 2 * i + d, 0, rows, :] for d in range(2)]
            S["cp"][side, i] = jnp.concatenate(both, axis=0).astype(BF16)
    source_1 = Exchange("source_1")
    for a in (-1, 1):
        for b in (-1, 1):
            source_1.add(S["cp"].at[(b + 1) // 2], S["cr"].at[(1 - b) // 2, (1 - a) // 2], a, b)
    own = pl.ds(16, 16)
    for a, xs, xd, w in ((-2, 12, 28, 1), (2, 19, 3, 1), (-1, 12, 20, 8), (1, 12, 4, 8)):
        source_1.add(S["s1"].at[pl.ds(xs, w), :, own, :], S["s1"].at[pl.ds(xd, w), :, own, :], a, 0)
    own = S["s1"].at[pl.ds(12, 8), :, pl.ds(16, 16), :]
    for b in (-1, 1):
        source_1.add(own, S["s1"].at[pl.ds(12, 8), :, pl.ds(16 - 16 * b, 16), :], 0, b)
    source_1.start()

    kappa_1.arrive()
    widen(S["k1"], M[1]["NK"], 12, (pl.ds(0, 48),))
    prepare(L1, M[1], 3, 29, *place)
    loop(0, 16, coarsen(L1, M[1]["NK"], 0, 3, 0.125, put_rows(M[2]["NK"], 2, 0)), 8)
    prepare(L2, M[2], 3, 17, *place)
    matrices = Exchange("matrix")
    for n in LINE:
        matrices.add(S["ms"].at[lax.rem(gy + n, gy_size)], S["mm"].at[gy], 0, n)
    matrices.start()
    S["mm"][gy] = S["ms"][gy]
    pack(2, S["keep0"], 1)
    side_v = sides(2, "side_v")

    source_1.arrive()
    widen(S["s1"], M[1]["NS"], 9, (pl.ds(16, 16),))
    for i in range(4):
        for ys in range(2):
            for xs in range(2):
                both = S["cr"][ys, xs, i].astype(F32)
                for d in range(2):
                    M[1]["NS"][4 + 16 * xs + 2 * i + d, 0, pl.ds(8 + 24 * ys, 8), :] = both[8 * d : 8 * d + 8]
    scale_source(L1, M[1], "NS", 3, 29, True)
    descend(L1, M[1], 6)

    residual = M[1]["RN"].at[pl.ds(6, 20)]
    loop(0, 10, coarsen(L1, residual, 0, 3, 0.5, put_rows(S["s2"], 5, 0)), 5)
    scale_source(L2, M[2], "s2", 5, 15, True)
    descend(L2, M[2], 0, S["keep2"])
    tiles = []
    residual = M[2]["RN"].at[pl.ds(8, 4)]
    loop(0, 2, coarsen(L2, residual, 8, 1, 1.0 / 128.0, lambda x, t, value: tiles.append(value)), 2)
    rounded = jnp.where(sub < 4, tiles[0], turn(tiles[1], 4, 0)).astype(BF16).astype(F32)
    S["mine"][...] = rounded
    gathered = Exchange("gather")
    for n in LINE:
        gathered.add(S["mine"], S["all"].at[gy], 0, n)
    gathered.start()
    odd = (lanes(4) & 1) == 1
    pair = S["pair"]
    pair[8:12, 0, 8:16, :] = jnp.where(odd, S["keep2"][1:5, 0, 8:16, :], S["s2"][8:12, 0, 8:16, :])
    level_2 = exchange(L2, pair, 8, pair, 4, 4, "level_2")
    S["all"][gy] = rounded

    kept = pltpu.make_async_copy(
        S["keep0"].at[pl.ds(1, 16), :, pl.ds(8, 32), :],
        S["smooth0"].at[pl.ds(4, 16), :, pl.ds(8, 32), :],
        S["local"].at[0],
    )
    kept.start()
    for old in (side_k, side_s, kappa_1, source_1, matrices, side_v):
        old.left()
    side_v.arrive()
    unpack(2)
    kept.wait()
    matrices.arrive()
    gathered.arrive()
    right = S["all"][...].reshape(gy_size * 8, 128).astype(BF16)
    product = jnp.dot(S["mm"][...].reshape(gy_size * 48, 128), right, preferred_element_type=F32)
    layer_of = lax.broadcasted_iota(jnp.int32, (24, 128), 1) >> 2
    terms = [jnp.where(layer_of == k, product[24 * k : 24 * k + 24], 0.0) for k in range(2 * gy_size)]
    while len(terms) > 1:
        terms = [terms[i] + terms[i + 1] for i in range(0, len(terms), 2)]
    S["corr"][2] = terms[0]
    coarse = Exchange("coarse")
    for a in (-2, -1, 1, 2):
        coarse.add(S["corr"].at[2], S["corr"].at[2 - a], a, 0)
    coarse.start()
    gathered.left()
    level_2.left()
    level_2.arrive()

    def part(x, U):
        for u in range(U):
            for t in range(3):
                rows = pl.ds(8 * t, 8)
                both = pair[x + u, 0, rows, :]
                second = (lane & 1) == 1
                M[2]["NS"][x + u, 0, rows, :] = jnp.where(second, turn(both, 1, 1), both)
                S["smooth2"][x + u, 0, rows, :] = jnp.where(second, both, turn(both, -1, 1))

    loop(2, 18, part, 8)
    scale_source(L2, M[2], "NS", 3, 17, False)
    coarse.arrive()

    for slab in range(5):
        for d in range(2):
            for b in range(2):
                M[2]["E"][2 * slab + d, 0, pl.ds(b, 8, stride=2), :] = S["corr"][slab, 12 * d : 12 * d + 8, :]
                M[2]["E"][2 * slab + d, 0, pl.ds(16 + b, 4, stride=2), :] = S["corr"][slab, 12 * d + 8 : 12 * d + 12, :]

    def emit_2(x, new):
        for j in range(L2.J):
            for b in range(2):
                M[1]["E"][x, 0, pl.ds(2 * j + b, 8, stride=2 * L2.J), :] = new[0][j]

    def emit_1(x, new):
        for j in range(L1.J):
            for r in range(2):
                value = pick(new[0][j], (lane >> 1) + 64 * r)
                for b in range(2):
                    M[0]["E"][x, r, pl.ds(2 * j + b, 8, stride=2 * L1.J), :] = value

    def emit_0(x, new):
        for r in range(2):
            for j in range(L0.J):
                S["result"][x - L0.x0, r, rows_of(L0, j), :] = new[r][j]

    ascend(L2, M[2], 6, emit_2, S["smooth2"])
    ascend(L1, M[1], 5, emit_1)
    stores = []

    def store(n):
        for r in range(2):
            copy = pltpu.make_async_copy(
                S["result"].at[pl.ds(8 * n, 8), r, pl.ds(8, 32), :],
                out.at[pl.ds(8 * n, 8), :, pl.ds(128 * r, 128)],
                S["local"].at[2 * n + r],
            )
            copy.start()
            stores.append(copy)

    ascend(L0, M[0], 3, emit_0, S["smooth0"], 2, store)
    coarse.left()
    for copy in stores:
        copy.wait()


def solution(mesh):
    gx_size, gy_size = mesh.shape["gx"], mesh.shape["gy"]
    scratch = {}
    for l, L in enumerate(LEVELS):
        for name, shape in L.scratch().items():
            scratch[str(l) + name] = shape
    scratch["xp"] = pltpu.VMEM((3, 2, 4, 2, 32, 128), BF16)
    scratch["xr"] = pltpu.VMEM((3, 2, 4, 2, 32, 128), BF16)
    scratch["yp"] = pltpu.VMEM((3, 2, 8, 16, 128), BF16)
    scratch["yr"] = pltpu.VMEM((3, 2, 12, 16, 128), BF16)
    scratch["k1"] = pltpu.VMEM((32, 1, 48, 128), BF16)
    scratch["s1"] = pltpu.VMEM((32, 1, 48, 128), BF16)
    scratch["cp"] = pltpu.VMEM((2, 4, 16, 128), BF16)
    scratch["cr"] = pltpu.VMEM((2, 2, 4, 16, 128), BF16)
    scratch["s2"] = pltpu.VMEM((20, 1, 24, 128), F32)
    scratch["keep0"] = pltpu.VMEM((18, 2, 48, 128), F32)
    scratch["smooth0"] = pltpu.VMEM((24, 2, 48, 128), F32)
    scratch["keep2"] = pltpu.VMEM((6, 1, 24, 128), F32)
    scratch["pair"] = pltpu.VMEM((20, 1, 24, 128), F32)
    scratch["smooth2"] = pltpu.VMEM((20, 1, 24, 128), F32)
    scratch["size"] = pltpu.VMEM((768, 128), F32)
    scratch["inverse"] = pltpu.VMEM((1, 2, 128, 128), BF16)
    scratch["mp"] = pltpu.VMEM((256, 128), BF16)
    scratch["ms"] = pltpu.VMEM((gy_size, 48, 128), BF16)
    scratch["mm"] = pltpu.VMEM((gy_size, 48, 128), BF16)
    scratch["mine"] = pltpu.VMEM((8, 128), F32)
    scratch["all"] = pltpu.VMEM((gy_size, 8, 128), F32)
    scratch["corr"] = pltpu.VMEM((5, 24, 128), F32)
    scratch["result"] = pltpu.VMEM((16, 2, 48, 128), F32)
    scratch["ready"] = pltpu.SemaphoreType.REGULAR
    scratch["local"] = pltpu.SemaphoreType.DMA((5,))
    for name in EXCHANGES:
        scratch["send_" + name] = pltpu.SemaphoreType.DMA
        scratch["recv_" + name] = pltpu.SemaphoreType.DMA

    def local(pressure_source, conductance, coarse_inverse):
        return pl.pallas_call(
            functools.partial(kernel, gx_size, gy_size, tuple(scratch)),
            out_shape=pltpu.VMEM(pressure_source.shape, F32),
            in_specs=[
                pl.BlockSpec(memory_space=pl.ANY),
                pl.BlockSpec(memory_space=pl.ANY),
                pl.BlockSpec(memory_space=pl.ANY),
            ],
            out_specs=pl.BlockSpec(memory_space=pl.ANY),
            scratch_shapes=list(scratch.values()),
            compiler_params=pltpu.CompilerParams(
                collective_id=0, has_side_effects=True, vmem_limit_bytes=40 * 2**20
            ),
        )(*(pltpu.with_memory_space_constraint(x, pltpu.HBM) for x in (pressure_source, conductance, coarse_inverse)))

    in_specs = (P("gx", "gy", None), P("gx", "gy", None), P("gx", "gy", None, None))
    return jax.shard_map(local, mesh=mesh, in_specs=in_specs, out_specs=P("gx", "gy", None), check_vma=False)
```

```python
import functools
import math

import jax
import jax.numpy as jnp
from jax import lax
from jax.experimental import pallas as pl
from jax.experimental.pallas import tpu as pltpu
from jax.sharding import PartitionSpec as P

MESH = pl.DeviceIdType.MESH

LMAX = 2.0
LMIN = 0.25
THETA = 0.5 * (LMAX + LMIN)
DELTA = 0.5 * (LMAX - LMIN)
SIGMA = THETA / DELTA
RATIO_0 = 1.0 / SIGMA
RATIO_1 = 1.0 / (2.0 * SIGMA - RATIO_0)
RATIO_2 = 1.0 / (2.0 * SIGMA - RATIO_1)
STEP_1 = (RATIO_1 * RATIO_0, 2.0 * RATIO_1 / DELTA)
STEP_2 = (RATIO_2 * RATIO_1, 2.0 * RATIO_2 / DELTA)

F32 = jnp.float32
BF16 = jnp.bfloat16

EXCHANGES = ("side_k", "side_s", "side_v", "kappa_1", "matrix", "source_1", "gather", "level_2", "coarse")
AROUND = [(a, b) for a in (-1, 0, 1) for b in (-1, 0, 1) if (a, b) != (0, 0)]
WIDE = [(a, b) for a in (-2, -1, 0, 1, 2) for b in (-1, 0, 1) if (a, b) != (0, 0)]
AROUND.sort(key=lambda o: -abs(o[0]) - 2 * abs(o[1]))
WIDE.sort(key=lambda o: -abs(o[0]) - 2 * abs(o[1]))
LINE = sorted(range(1, 16), key=lambda n: -min(n // 4, 4 - n // 4) - min(n % 4, 4 - n % 4))


class Level:
    def __init__(self, nx, ny, x0, side, R, J, hold, row0, erow, xc, coarse, most):
        self.nx, self.ny, self.X, self.x0, self.side = nx, ny, nx + 2 * x0, x0, side
        self.R, self.J, self.hold, self.row0, self.most = R, J, hold, row0, most
        self.erow, self.xc, self.coarse = erow, xc, coarse
        self.rows = ny + 2 * side

    def scratch(self):
        X, R, J = self.X, self.R, self.J
        vm = lambda *shape: pltpu.VMEM(shape + (128,), F32)
        blocked = {name: vm(X, R, J, 8) for name in ("CM", "CP", "Q", "G", "D")}
        natural = {name: vm(X, R, self.rows) for name in ("NS", "NK", "RN")}
        return dict(
            E=vm(self.coarse[0], R, self.coarse[1]),
            HK=vm(X, R, J + 2, 8),
            CX=vm(X + 1, R, J, 8),
            CY=vm(X, R, J + 1, 8),
            VA=vm(X, R, J + 2, 8),
            VB=vm(X, R, J + 2, 8),
            **blocked,
            **natural,
        )


LEVELS = (
    Level(16, 32, 4, 8, 2, 5, 1, 4, 20, 10, (32, 80), 22),
    Level(8, 16, 12, 16, 1, 5, 1, 4, 4, 2, (20, 48), 26),
    Level(4, 8, 8, 8, 1, 3, 2, 0, 0, 0, (10, 24), 16),
)


def lanes(*lead):
    return lax.broadcasted_iota(jnp.int32, lead + (8, 128), len(lead) + 1)


def sublanes():
    return lax.broadcasted_iota(jnp.int32, (8, 128), 0)


def turn(value, shift, axis):
    return pltpu.roll(value, shift % value.shape[axis], axis)


def pick(value, index):
    return jnp.take_along_axis(value, index, axis=1, mode="promise_in_bounds")


def rows_of(L, j):
    return pl.ds(L.row0 + j, 8, stride=L.J)


def beside_z(L, parts):
    h = L.hold
    down = [turn(p, h, 2) for p in parts]
    up = [turn(p, -h, 2) for p in parts]
    if L.R == 2:
        lane = lanes(L.J)
        down[1] = jnp.where(lane == 0, down[0], down[1])
        up[0] = jnp.where(lane == 127, up[1], up[0])
    return down, up


def store_wrapped(ref, x, r, J, values):
    ref[x, r, 1 : J + 1] = values
    ref[x, r, 0] = turn(values[J - 1], 1, 0)
    ref[x, r, J + 1] = turn(values[0], -1, 0)


def rows_from(L, ref, x, r):
    return jnp.stack([ref[x, r, rows_of(L, j), :] for j in range(L.J)])


def rows_to(L, ref, x, r, values):
    for j in range(L.J):
        ref[x, r, rows_of(L, j), :] = values[j]


def loop(lo, hi, body, most=1):
    count = hi - lo
    steps = -(-count // most)
    U = -(-count // steps)
    whole = count // U
    if whole > 1:

        def step(i, carry):
            body(lo + i * U, U)
            return carry

        lax.fori_loop(0, whole, step, 0)
    elif whole == 1:
        body(lo, U)
    if count > whole * U:
        body(lo + whole * U, count - whole * U)


def prepare(L, M, lo, hi, gx, gy, count_x, count_y):
    J, R, h = L.J, L.R, L.hold
    shape = (J, 8, 128)
    lane = lanes(J)
    place = lax.broadcasted_iota(jnp.int32, shape, 0) + J * lax.broadcasted_iota(jnp.int32, shape, 1)
    place = place + (gy * L.ny - L.side + L.row0)
    keep = jnp.where((place >= 0) & (place < L.ny * count_y), 0.5, 0.0).astype(F32)

    def halves(x, U):
        NK, HK = M["NK"].at[pl.ds(x, U)], M["HK"].at[pl.ds(x, U)]
        for u in range(U):
            place = gx * L.nx + x + u - L.x0
            inside = jnp.where((place >= 0) & (place < L.nx * count_x), 1.0, 0.0).astype(F32)
            mask = keep * inside
            for r in range(R):
                store_wrapped(HK, u, r, J, rows_from(L, NK, u, r) * mask)

    loop(lo - 1, hi + 1, halves, L.most)
    for r in range(R):
        M["CX"][lo, r] = M["HK"][lo - 1, r, 1 : J + 1] + M["HK"][lo, r, 1 : J + 1]

    def couple(x, U):
        HK, CX = M["HK"].at[pl.ds(x - 1, U + 2)], M["CX"].at[pl.ds(x, U + 1)]
        CY, CM, CP, D, Q = (M[name].at[pl.ds(x, U)] for name in ("CY", "CM", "CP", "D", "Q"))
        for u in range(U):
            slabs = [beside_y(L, HK, u + 1, r) for r in range(R)]
            down, up = beside_z(L, [slab[0] for slab in slabs])
            down[0] = jnp.where(lane < h, 0.0, down[0])
            up[R - 1] = jnp.where(lane >= 128 - h, 0.0, up[R - 1])
            for r in range(R):
                c, ym, yp = slabs[r]
                xm, xp = HK[u, r, 1 : J + 1], HK[u + 2, r, 1 : J + 1]
                diagonal = (xm + xp) + (ym + yp) + (down[r] + up[r]) + 6.0 * c
                CX[u + 1, r] = c + xp
                CY[u, r, 0:J] = c + ym
                CY[u, r, J] = c[J - 1] + yp[J - 1]
                low, high = c + down[r], c + up[r]
                if r == 0:
                    low = jnp.where(lane < h, 0.0, low)
                if r == R - 1:
                    high = jnp.where(lane >= 128 - h, 0.0, high)
                CM[u, r] = low
                CP[u, r] = high
                D[u, r] = diagonal
                Q[u, r] = jnp.where(c > 0.0, 1.0 / diagonal, 0.0)

    loop(lo, hi, couple, L.most)


def scale_source(L, M, name, lo, hi, start):
    J, field = L.J, M[name]

    def body(x, U):
        Q, G, VA, NS = (ref.at[pl.ds(x, U)] for ref in (M["Q"], M["G"], M["VA"], field))
        for u in range(U):
            for r in range(L.R):
                g = Q[u, r] * rows_from(L, NS, u, r)
                G[u, r] = g
                if start:
                    store_wrapped(VA, u, r, J, g * (1.0 / THETA))

    loop(lo, hi, body, L.most)


def beside_y(L, ref, x, r):
    c = ref[x, r, 1 : L.J + 1]
    low, high = ref[x, r, 0:1], ref[x, r, L.J + 1 : L.J + 2]
    return c, jnp.concatenate([low, c[:-1]], axis=0), jnp.concatenate([c[1:], high], axis=0)


def sweep(L, M, src, dst, lo, hi, step, keep_rows=None, emit=None):
    J, R = L.J, L.R

    def body(x, U):
        V, CX = M[src].at[pl.ds(x - 1, U + 2)], M["CX"].at[pl.ds(x, U + 1)]
        CY, CM, CP, D, Q, G = (M[name].at[pl.ds(x, U)] for name in ("CY", "CM", "CP", "D", "Q", "G"))
        W = M[dst].at[pl.ds(x, U)] if dst is not None else None
        if step is None:
            RN = M["RN"].at[pl.ds(x, U)]
        if keep_rows is not None:
            kept = keep_rows.at[pl.ds(x - L.x0 + 1, U)]
        for u in range(U):
            slabs = [beside_y(L, V, u + 1, r) for r in range(R)]
            down, up = beside_z(L, [slab[0] for slab in slabs])
            new = []
            for r in range(R):
                c, ym, yp = slabs[r]
                cy = CY[u, r]
                near = CX[u, r] * V[u, r, 1 : J + 1] + CX[u + 1, r] * V[u + 2, r, 1 : J + 1]
                near = near + (cy[:-1] * ym + cy[1:] * yp)
                near = near + (CM[u, r] * down[r] + CP[u, r] * up[r])
                z = G[u, r] + Q[u, r] * near
                if step is None:
                    rows_to(L, RN, u, r, D[u, r] * (z - c))
                    continue
                a, b, before = step
                value = (1.0 + a - b) * c + b * z
                if before:
                    value = value - a * W[u, r, 1 : J + 1]
                if emit is None:
                    store_wrapped(W, u, r, J, value)
                if keep_rows is not None:
                    rows_to(L, kept, u, r, value)
                new.append(value)
            if emit is not None:
                emit(x + u, new)

    loop(lo, hi, body, L.most)


def descend(L, M, margin, keep_rows=None):
    lo, hi = L.x0 - margin, L.x0 + L.nx + margin
    sweep(L, M, "VA", "VB", lo - 2, hi + 2, STEP_1 + (False,))
    sweep(L, M, "VB", "VA", lo - 1, hi + 1, STEP_2 + (True,), keep_rows=keep_rows)
    sweep(L, M, "VA", None, lo, hi, None)


def ascend(L, M, margin, emit, smoothed=None, pieces=1, after=lambda n: None):
    lo, hi = L.x0, L.x0 + L.nx

    def begin(x, U):
        HK, VA = (M[name].at[pl.ds(x, U)] for name in ("HK", "VA"))
        if smoothed is not None:
            NV = smoothed.at[pl.ds(x, U)]
        for u in range(U):
            xc = lax.shift_right_logical(x + u, 1) + L.xc
            for r in range(L.R):
                added = [M["E"][xc, r, pl.ds(L.erow + j, 8, stride=L.J), :] for j in range(L.J)]
                base = VA[u, r, 1 : L.J + 1] if smoothed is None else rows_from(L, NV, u, r)
                inside = HK[u, r, 1 : L.J + 1] > 0.0
                store_wrapped(VA, u, r, L.J, jnp.where(inside, jnp.stack(added) + base, 0.0))

    loop(lo - margin, hi + margin, begin, L.most)
    margin -= 1
    sweep(L, M, "VA", "VB", lo - margin, hi + margin, (0.0, 1.0 / THETA, False))
    margin -= 1
    sweep(L, M, "VB", "VA", lo - margin, hi + margin, STEP_1 + (True,))
    margin -= 1
    width = (hi - lo + 2 * margin) // pieces
    for n in range(pieces):
        first = lo - margin + n * width
        sweep(L, M, "VA", "VB", first, first + width, STEP_2 + (True,), emit=emit)
        after(n)


def coarsen(L, src, row, tiles, scale, put):
    lane = lanes()
    even = (lane * 2) & 127

    def body(x, U):
        pairs = src.at[pl.ds(2 * x, 2 * U)]
        for u, t in [(u, t) for u in range(U) for t in range(tiles)]:
            sums = []
            for r in range(L.R):
                rows = [pairs[2 * u + dx, r, pl.ds(row + 16 * t + b, 8, stride=2), :] for dx in (0, 1) for b in (0, 1)]
                total = (rows[0] + rows[1]) + (rows[2] + rows[3])
                if L.R == 2:
                    sums.append(pick(total + turn(total, -1, 1), even))
                else:
                    other = jnp.where((lane & L.hold) == 0, turn(total, -L.hold, 1), turn(total, L.hold, 1))
                    sums.append(total + other)
            value = jnp.where(lane < 64, sums[0], sums[1]) if L.R == 2 else sums[0]
            put(x + u, t, value * scale)

    return body


def put_rows(dst, dx, row):
    def put(x, t, value):
        dst[dx + x, 0, row + 8 * t : row + 8 * t + 8, :] = value

    return put


def kernel(gx_size, gy_size, names, source, conductance, inverse, out, *refs):
    S = dict(zip(names, refs))
    M = [{k[1:]: v for k, v in S.items() if k[0] == str(l)} for l in range(3)]
    M[2]["s2"] = S["s2"]
    gx, gy = lax.axis_index("gx"), lax.axis_index("gy")
    L0, L1, L2 = LEVELS

    def device(a, b):
        return {"gx": lax.rem(gx + a + gx_size, gx_size), "gy": lax.rem(gy + b + gy_size, gy_size)}

    class Exchange:
        def __init__(self, name):
            self.out, self.back, self.rows, self.copies = S["send_" + name], S["recv_" + name], 0, []

        def add(self, src, dst, a, b):
            copy = pltpu.make_async_remote_copy(
                src_ref=src, dst_ref=dst, send_sem=self.out, recv_sem=self.back, device_id=device(a, b), device_id_type=MESH
            )
            self.copies.append(copy)
            rows = math.prod(src.shape[:-1])
            self.rows += rows if src.dtype == F32 else rows // 2

        def start(self):
            for copy in self.copies:
                copy.start()
            return self

        def wait(self, semaphore):
            size = S["size"].at[pl.ds(0, self.rows)]
            pltpu.make_async_copy(size, size, semaphore).wait()

        def arrive(self):
            self.wait(self.back)

        def left(self):
            self.wait(self.out)

    def exchange(L, src, sx0, dst, near, far, name):
        both = Exchange(name)
        h = L.side
        for a, b in WIDE if far else AROUND:
            w = {0: L.nx, 1: near, 2: far}[abs(a)]
            xs = sx0 + (L.nx - w if a > 0 else 0)
            xd = {0: L.x0, 1: L.x0 - w, 2: L.x0 - L.nx - w, -1: L.x0 + L.nx, -2: L.x0 + 2 * L.nx}[a]
            ys = h + (L.ny - h if b > 0 else 0)
            yd, wy = {0: (h, L.ny), 1: (0, h), -1: (h + L.ny, h)}[b]
            both.add(src.at[pl.ds(xs, w), :, pl.ds(ys, wy), :], dst.at[pl.ds(xd, w), :, pl.ds(yd, wy), :], a, b)
        return both.start()

    peers = [(0, b) for b in LINE if 1 < b < gy_size - 1] + AROUND
    barrier = pltpu.get_barrier_semaphore()
    for a, b in peers:
        pl.semaphore_signal(barrier, inc=1, device_id=device(a, b), device_id_type=MESH)

    fields = (M[0]["NK"], M[0]["NS"], S["smooth0"])
    XP, YP, XR, YR = S["xp"], S["yp"], S["xr"], S["yr"]
    sub, lane = sublanes(), lanes()

    loads = [pltpu.make_async_copy(inverse, S["inverse"], S["local"].at[4])]
    for n, src in enumerate((conductance, source)):
        for r in range(2):
            loads.append(
                pltpu.make_async_copy(
                    src.at[:, :, pl.ds(128 * r, 128)],
                    fields[n].at[pl.ds(4, 16), r, pl.ds(8, 32), :],
                    S["local"].at[2 * n + r],
                )
            )
    for copy in loads:
        copy.start()

    def pack(a, field, first):
        def pack_x(i, _):
            for r in range(2):
                XP[a, 0, i, r] = field[first + i, r, 8:40, :].astype(BF16)
                XP[a, 1, i, r] = field[first + 12 + i, r, 8:40, :].astype(BF16)

        def pack_y(i, _):
            low, high = [], []
            for d in range(2):
                x = first + 2 * i + d
                near, far = field[x, 0, 8:16, :], field[x, 1, 8:16, :]
                low.append(jnp.where(sub < 4, near, turn(far, 4, 0)))
                near, far = field[x, 0, 32:40, :], field[x, 1, 32:40, :]
                high.append(jnp.where(sub < 4, turn(near, 4, 0), far))
            YP[a, 0, i] = jnp.concatenate(low, axis=0).astype(BF16)
            YP[a, 1, i] = jnp.concatenate(high, axis=0).astype(BF16)

        loop(0, 4, pack_x)
        loop(0, 8, pack_y)

    def sides(a, name):
        both = Exchange(name)
        for x, y in AROUND:
            if y == 0:
                both.add(XP.at[a, (x + 1) // 2], XR.at[a, (1 - x) // 2], x, y)
            else:
                wx = 8 if x == 0 else 2 if a == 0 else 1
                xs, xd = {0: (0, 2), 1: (8 - wx, 2 - wx), -1: (0, 10)}[x]
                both.add(YP.at[a, (y + 1) // 2, pl.ds(xs, wx)], YR.at[a, (1 - y) // 2, pl.ds(xd, wx)], x, y)
        return both.start()

    def unpack(a):
        field = fields[a]

        def unpack_x(i, _):
            for r in range(2):
                field[i, r, 8:40, :] = XR[a, 0, i, r].astype(F32)
                field[20 + i, r, 8:40, :] = XR[a, 1, i, r].astype(F32)

        def unpack_y(i, _):
            low, high = YR[a, 0, i].astype(F32), YR[a, 1, i].astype(F32)
            for d in range(2):
                x = 2 * i + d
                part = low[8 * d : 8 * d + 8]
                field[x, 0, 0:8, :] = turn(part, 4, 0)
                field[x, 1, 0:8, :] = part
                part = high[8 * d : 8 * d + 8]
                field[x, 0, 40:48, :] = part
                field[x, 1, 40:48, :] = turn(part, 4, 0)

        loop(0, 4, unpack_x)
        loop(0, 12, unpack_y)

    for a in range(2):
        loads[1 + 2 * a].wait()
        loads[2 + 2 * a].wait()
        pack(a, fields[a], 4)

    pl.semaphore_wait(barrier, len(peers))
    side_k = sides(0, "side_k")
    side_s = sides(1, "side_s")
    for a in (-1, 1):
        pl.semaphore_signal(S["ready"], inc=1, device_id=device(a, 0), device_id_type=MESH)

    def halve(field, packed):
        packed[12:20, 0, 16:32, :] = field[12:20, 0, 16:32, :].astype(BF16)

    def widen(packed, field, margin, beside):
        def take(parts):
            def body(x, U):
                for u in range(U):
                    for rows in parts:
                        field[x + u, 0, rows, :] = packed[x + u, 0, rows, :].astype(F32)

            return body

        loop(12 - margin, 12, take(beside), 12)
        loop(12, 20, take((pl.ds(0, 16), pl.ds(32, 16))), 8)
        loop(20, 20 + margin, take(beside), 12)

    loop(0, 8, coarsen(L0, M[0]["NK"].at[pl.ds(4, 16)], 8, 2, 0.125, put_rows(M[1]["NK"], 12, 16)), 4)
    halve(M[1]["NK"], S["k1"])

    loads[0].wait()
    one = lambda mask: jnp.where(mask, 1.0, 0.0).astype(BF16)
    row = lax.broadcasted_iota(jnp.int32, (128, 128), 0)
    column = lax.broadcasted_iota(jnp.int32, (128, 128), 1)
    order = one(row == ((column >> 2) & 1) * 64 + (column >> 3) * 4 + (column & 3))
    for k in range(2):
        S["mp"][128 * k : 128 * (k + 1), :] = jnp.dot(
            S["inverse"][0, k], order, preferred_element_type=F32
        ).astype(BF16)

    row = lax.broadcasted_iota(jnp.int32, (4, 48, 256), 1)
    column = lax.broadcasted_iota(jnp.int32, (4, 48, 256), 2)
    layer = jnp.where(row >= 24, 1, 0)
    row = row - 24 * layer
    half = jnp.where(row >= 12, 1, 0)
    row = row - 12 * half + 4 * lax.broadcasted_iota(jnp.int32, (4, 48, 256), 0)
    base = layer * 128 + half * 64

    def share(d, _):
        chosen = one(column == base + ((row + (16 * d + 60)) & 63)).reshape(192, 256)
        rows = jnp.dot(chosen, S["mp"][...], preferred_element_type=F32)
        S["ms"][pl.ds(4 * d, 4)] = rows.astype(BF16).reshape(4, 48, 128)

    loop(0, gy_size // 4, share)
    pl.semaphore_wait(S["ready"], 2)
    kappa_1 = exchange(L1, S["k1"], 12, S["k1"], 8, 4, "kappa_1")

    place = (gx, gy, gx_size, gy_size)
    side_k.arrive()
    unpack(0)
    prepare(L0, M[0], 1, 23, *place)
    side_s.arrive()
    unpack(1)
    scale_source(L0, M[0], "NS", 1, 23, True)
    descend(L0, M[0], 0, S["keep0"])
    residual = M[0]["RN"].at[pl.ds(4, 16)]
    loop(0, 8, coarsen(L0, residual, 8, 2, 0.5, put_rows(M[1]["NS"], 12, 16)), 8)
    halve(M[1]["NS"], S["s1"])
    for i in range(4):
        for side in range(2):
            rows = pl.ds(16 + 8 * side, 8)
            both = [M[1]["NS"][12 + 2 * i + d, 0, rows, :] for d in range(2)]
            S["cp"][side, i] = jnp.concatenate(both, axis=0).astype(BF16)
    source_1 = Exchange("source_1")
    for a in (-1, 1):
        for b in (-1, 1):
            source_1.add(S["cp"].at[(b + 1) // 2], S["cr"].at[(1 - b) // 2, (1 - a) // 2], a, b)
    own = pl.ds(16, 16)
    for a, xs, xd, w in ((-2, 12, 28, 1), (2, 19, 3, 1), (-1, 12, 20, 8), (1, 12, 4, 8)):
        source_1.add(S["s1"].at[pl.ds(xs, w), :, own, :], S["s1"].at[pl.ds(xd, w), :, own, :], a, 0)
    own = S["s1"].at[pl.ds(12, 8), :, pl.ds(16, 16), :]
    for b in (-1, 1):
        source_1.add(own, S["s1"].at[pl.ds(12, 8), :, pl.ds(16 - 16 * b, 16), :], 0, b)
    source_1.start()

    kappa_1.arrive()
    widen(S["k1"], M[1]["NK"], 12, (pl.ds(0, 48),))
    prepare(L1, M[1], 3, 29, *place)
    loop(0, 16, coarsen(L1, M[1]["NK"], 0, 3, 0.125, put_rows(M[2]["NK"], 2, 0)), 8)
    prepare(L2, M[2], 3, 17, *place)
    matrices = Exchange("matrix")
    for n in LINE:
        matrices.add(S["ms"].at[lax.rem(gy + n, gy_size)], S["mm"].at[gy], 0, n)
    matrices.start()
    S["mm"][gy] = S["ms"][gy]
    pack(2, S["keep0"], 1)
    side_v = sides(2, "side_v")

    source_1.arrive()
    widen(S["s1"], M[1]["NS"], 9, (pl.ds(16, 16),))
    for i in range(4):
        for ys in range(2):
            for xs in range(2):
                both = S["cr"][ys, xs, i].astype(F32)
                for d in range(2):
                    M[1]["NS"][4 + 16 * xs + 2 * i + d, 0, pl.ds(8 + 24 * ys, 8), :] = both[8 * d : 8 * d + 8]
    scale_source(L1, M[1], "NS", 3, 29, True)
    descend(L1, M[1], 6)

    residual = M[1]["RN"].at[pl.ds(6, 20)]
    loop(0, 10, coarsen(L1, residual, 0, 3, 0.5, put_rows(S["s2"], 5, 0)), 10)
    scale_source(L2, M[2], "s2", 5, 15, True)
    descend(L2, M[2], 0, S["keep2"])
    tiles = []
    residual = M[2]["RN"].at[pl.ds(8, 4)]
    loop(0, 2, coarsen(L2, residual, 8, 1, 1.0 / 128.0, lambda x, t, value: tiles.append(value)), 2)
    rounded = jnp.where(sub < 4, tiles[0], turn(tiles[1], 4, 0)).astype(BF16).astype(F32)
    S["mine"][...] = rounded
    gathered = Exchange("gather")
    for n in LINE:
        gathered.add(S["mine"], S["all"].at[gy], 0, n)
    gathered.start()
    odd = (lanes(4) & 1) == 1
    pair = S["pair"]
    pair[8:12, 0, 8:16, :] = jnp.where(odd, S["keep2"][1:5, 0, 8:16, :], S["s2"][8:12, 0, 8:16, :])
    level_2 = exchange(L2, pair, 8, pair, 4, 4, "level_2")
    S["all"][gy] = rounded

    kept = pltpu.make_async_copy(
        S["keep0"].at[pl.ds(1, 16), :, pl.ds(8, 32), :],
        S["smooth0"].at[pl.ds(4, 16), :, pl.ds(8, 32), :],
        S["local"].at[0],
    )
    kept.start()
    for old in (side_k, side_s, kappa_1, source_1, matrices, side_v):
        old.left()
    side_v.arrive()
    unpack(2)
    kept.wait()
    matrices.arrive()
    gathered.arrive()
    right = S["all"][...].reshape(gy_size * 8, 128).astype(BF16)
    product = jnp.dot(S["mm"][...].reshape(gy_size * 48, 128), right, preferred_element_type=F32)
    layer_of = lax.broadcasted_iota(jnp.int32, (24, 128), 1) >> 2
    terms = [jnp.where(layer_of == k, product[24 * k : 24 * k + 24], 0.0) for k in range(2 * gy_size)]
    while len(terms) > 1:
        terms = [terms[i] + terms[i + 1] for i in range(0, len(terms), 2)]
    S["corr"][2] = terms[0]
    coarse = Exchange("coarse")
    for a in (-2, -1, 1, 2):
        coarse.add(S["corr"].at[2], S["corr"].at[2 - a], a, 0)
    coarse.start()
    gathered.left()
    level_2.left()
    level_2.arrive()

    def part(x, U):
        for u in range(U):
            for t in range(3):
                rows = pl.ds(8 * t, 8)
                both = pair[x + u, 0, rows, :]
                second = (lane & 1) == 1
                M[2]["NS"][x + u, 0, rows, :] = jnp.where(second, turn(both, 1, 1), both)
                S["smooth2"][x + u, 0, rows, :] = jnp.where(second, both, turn(both, -1, 1))

    loop(2, 18, part, 8)
    scale_source(L2, M[2], "NS", 3, 17, False)
    coarse.arrive()

    for slab in range(5):
        for d in range(2):
            for b in range(2):
                M[2]["E"][2 * slab + d, 0, pl.ds(b, 8, stride=2), :] = S["corr"][slab, 12 * d : 12 * d + 8, :]
                M[2]["E"][2 * slab + d, 0, pl.ds(16 + b, 4, stride=2), :] = S["corr"][slab, 12 * d + 8 : 12 * d + 12, :]

    def emit_2(x, new):
        for j in range(L2.J):
            for b in range(2):
                M[1]["E"][x, 0, pl.ds(2 * j + b, 8, stride=2 * L2.J), :] = new[0][j]

    def emit_1(x, new):
        for j in range(L1.J):
            for r in range(2):
                value = pick(new[0][j], (lane >> 1) + 64 * r)
                for b in range(2):
                    M[0]["E"][x, r, pl.ds(2 * j + b, 8, stride=2 * L1.J), :] = value

    def emit_0(x, new):
        for r in range(2):
            for j in range(L0.J):
                S["result"][x - L0.x0, r, rows_of(L0, j), :] = new[r][j]

    ascend(L2, M[2], 6, emit_2, S["smooth2"])
    ascend(L1, M[1], 5, emit_1)
    stores = []

    def store(n):
        for r in range(2):
            copy = pltpu.make_async_copy(
                S["result"].at[pl.ds(8 * n, 8), r, pl.ds(8, 32), :],
                out.at[pl.ds(8 * n, 8), :, pl.ds(128 * r, 128)],
                S["local"].at[2 * n + r],
            )
            copy.start()
            stores.append(copy)

    ascend(L0, M[0], 3, emit_0, S["smooth0"], 2, store)
    coarse.left()
    for copy in stores:
        copy.wait()


def solution(mesh):
    gx_size, gy_size = mesh.shape["gx"], mesh.shape["gy"]
    scratch = {}
    for l, L in enumerate(LEVELS):
        for name, shape in L.scratch().items():
            scratch[str(l) + name] = shape
    scratch["xp"] = pltpu.VMEM((3, 2, 4, 2, 32, 128), BF16)
    scratch["xr"] = pltpu.VMEM((3, 2, 4, 2, 32, 128), BF16)
    scratch["yp"] = pltpu.VMEM((3, 2, 8, 16, 128), BF16)
    scratch["yr"] = pltpu.VMEM((3, 2, 12, 16, 128), BF16)
    scratch["k1"] = pltpu.VMEM((32, 1, 48, 128), BF16)
    scratch["s1"] = pltpu.VMEM((32, 1, 48, 128), BF16)
    scratch["cp"] = pltpu.VMEM((2, 4, 16, 128), BF16)
    scratch["cr"] = pltpu.VMEM((2, 2, 4, 16, 128), BF16)
    scratch["s2"] = pltpu.VMEM((20, 1, 24, 128), F32)
    scratch["keep0"] = pltpu.VMEM((18, 2, 48, 128), F32)
    scratch["smooth0"] = pltpu.VMEM((24, 2, 48, 128), F32)
    scratch["keep2"] = pltpu.VMEM((6, 1, 24, 128), F32)
    scratch["pair"] = pltpu.VMEM((20, 1, 24, 128), F32)
    scratch["smooth2"] = pltpu.VMEM((20, 1, 24, 128), F32)
    scratch["size"] = pltpu.VMEM((768, 128), F32)
    scratch["inverse"] = pltpu.VMEM((1, 2, 128, 128), BF16)
    scratch["mp"] = pltpu.VMEM((256, 128), BF16)
    scratch["ms"] = pltpu.VMEM((gy_size, 48, 128), BF16)
    scratch["mm"] = pltpu.VMEM((gy_size, 48, 128), BF16)
    scratch["mine"] = pltpu.VMEM((8, 128), F32)
    scratch["all"] = pltpu.VMEM((gy_size, 8, 128), F32)
    scratch["corr"] = pltpu.VMEM((5, 24, 128), F32)
    scratch["result"] = pltpu.VMEM((16, 2, 48, 128), F32)
    scratch["ready"] = pltpu.SemaphoreType.REGULAR
    scratch["local"] = pltpu.SemaphoreType.DMA((5,))
    for name in EXCHANGES:
        scratch["send_" + name] = pltpu.SemaphoreType.DMA
        scratch["recv_" + name] = pltpu.SemaphoreType.DMA

    def local(pressure_source, conductance, coarse_inverse):
        return pl.pallas_call(
            functools.partial(kernel, gx_size, gy_size, tuple(scratch)),
            out_shape=pltpu.VMEM(pressure_source.shape, F32),
            in_specs=[
                pl.BlockSpec(memory_space=pl.ANY),
                pl.BlockSpec(memory_space=pl.ANY),
                pl.BlockSpec(memory_space=pl.ANY),
            ],
            out_specs=pl.BlockSpec(memory_space=pl.ANY),
            scratch_shapes=list(scratch.values()),
            compiler_params=pltpu.CompilerParams(
                collective_id=0, has_side_effects=True, vmem_limit_bytes=40 * 2**20
            ),
        )(*(pltpu.with_memory_space_constraint(x, pltpu.HBM) for x in (pressure_source, conductance, coarse_inverse)))

    in_specs = (P("gx", "gy", None), P("gx", "gy", None), P("gx", "gy", None, None))
    return jax.shard_map(local, mesh=mesh, in_specs=in_specs, out_specs=P("gx", "gy", None), check_vma=False)
```

```python
import functools
import math

import jax
import jax.numpy as jnp
from jax import lax
from jax.experimental import pallas as pl
from jax.experimental.pallas import tpu as pltpu
from jax.sharding import PartitionSpec as P

MESH = pl.DeviceIdType.MESH

LMAX = 2.0
LMIN = 0.25
THETA = 0.5 * (LMAX + LMIN)
DELTA = 0.5 * (LMAX - LMIN)
SIGMA = THETA / DELTA
RATIO_0 = 1.0 / SIGMA
RATIO_1 = 1.0 / (2.0 * SIGMA - RATIO_0)
RATIO_2 = 1.0 / (2.0 * SIGMA - RATIO_1)
STEP_1 = (RATIO_1 * RATIO_0, 2.0 * RATIO_1 / DELTA)
STEP_2 = (RATIO_2 * RATIO_1, 2.0 * RATIO_2 / DELTA)

F32 = jnp.float32
BF16 = jnp.bfloat16

EXCHANGES = ("side_k", "side_s", "side_v", "kappa_1", "matrix", "source_1", "gather", "level_2", "coarse")
AROUND = [(a, b) for a in (-1, 0, 1) for b in (-1, 0, 1) if (a, b) != (0, 0)]
WIDE = [(a, b) for a in (-2, -1, 0, 1, 2) for b in (-1, 0, 1) if (a, b) != (0, 0)]
AROUND.sort(key=lambda o: -abs(o[0]) - 2 * abs(o[1]))
WIDE.sort(key=lambda o: -abs(o[0]) - 2 * abs(o[1]))
LINE = sorted(range(1, 16), key=lambda n: -min(n // 4, 4 - n // 4) - min(n % 4, 4 - n % 4))


class Level:
    def __init__(self, nx, ny, x0, side, R, J, hold, row0, erow, xc, coarse, most):
        self.nx, self.ny, self.X, self.x0, self.side = nx, ny, nx + 2 * x0, x0, side
        self.R, self.J, self.hold, self.row0, self.most = R, J, hold, row0, most
        self.erow, self.xc, self.coarse = erow, xc, coarse
        self.rows = ny + 2 * side

    def scratch(self):
        X, R, J = self.X, self.R, self.J
        vm = lambda *shape: pltpu.VMEM(shape + (128,), F32)
        blocked = {name: vm(X, R, J, 8) for name in ("CM", "CP", "Q", "G", "D")}
        natural = {name: vm(X, R, self.rows) for name in ("NS", "NK", "RN")}
        return dict(
            E=vm(self.coarse[0], R, self.coarse[1]),
            HK=vm(X, R, J + 2, 8),
            CX=vm(X + 1, R, J, 8),
            CY=vm(X, R, J + 1, 8),
            VA=vm(X, R, J + 2, 8),
            VB=vm(X, R, J + 2, 8),
            **blocked,
            **natural,
        )


LEVELS = (
    Level(16, 32, 4, 8, 2, 5, 1, 4, 20, 10, (32, 80), 22),
    Level(8, 16, 12, 16, 1, 5, 1, 4, 4, 2, (20, 48), 26),
    Level(4, 8, 8, 8, 1, 3, 2, 0, 0, 0, (10, 24), 16),
)


def lanes(*lead):
    return lax.broadcasted_iota(jnp.int32, lead + (8, 128), len(lead) + 1)


def sublanes():
    return lax.broadcasted_iota(jnp.int32, (8, 128), 0)


def turn(value, shift, axis):
    return pltpu.roll(value, shift % value.shape[axis], axis)


def pick(value, index):
    return jnp.take_along_axis(value, index, axis=1, mode="promise_in_bounds")


def rows_of(L, j):
    return pl.ds(L.row0 + j, 8, stride=L.J)


def beside_z(L, parts):
    h = L.hold
    down = [turn(p, h, 2) for p in parts]
    up = [turn(p, -h, 2) for p in parts]
    if L.R == 2:
        lane = lanes(L.J)
        down[1] = jnp.where(lane == 0, down[0], down[1])
        up[0] = jnp.where(lane == 127, up[1], up[0])
    return down, up


def store_wrapped(ref, x, r, J, values):
    ref[x, r, 1 : J + 1] = values
    ref[x, r, 0] = turn(values[J - 1], 1, 0)
    ref[x, r, J + 1] = turn(values[0], -1, 0)


def rows_from(L, ref, x, r):
    return jnp.stack([ref[x, r, rows_of(L, j), :] for j in range(L.J)])


def rows_to(L, ref, x, r, values):
    for j in range(L.J):
        ref[x, r, rows_of(L, j), :] = values[j]


def loop(lo, hi, body, most=1):
    count = hi - lo
    steps = -(-count // most)
    U = -(-count // steps)
    whole = count // U
    if whole > 1:

        def step(i, carry):
            body(lo + i * U, U)
            return carry

        lax.fori_loop(0, whole, step, 0)
    elif whole == 1:
        body(lo, U)
    if count > whole * U:
        body(lo + whole * U, count - whole * U)


def prepare(L, M, lo, hi, gx, gy, count_x, count_y):
    J, R, h = L.J, L.R, L.hold
    shape = (J, 8, 128)
    lane = lanes(J)
    place = lax.broadcasted_iota(jnp.int32, shape, 0) + J * lax.broadcasted_iota(jnp.int32, shape, 1)
    place = place + (gy * L.ny - L.side + L.row0)
    keep = jnp.where((place >= 0) & (place < L.ny * count_y), 0.5, 0.0).astype(F32)

    def halves(x, U):
        NK, HK = M["NK"].at[pl.ds(x, U)], M["HK"].at[pl.ds(x, U)]
        for u in range(U):
            place = gx * L.nx + x + u - L.x0
            inside = jnp.where((place >= 0) & (place < L.nx * count_x), 1.0, 0.0).astype(F32)
            mask = keep * inside
            for r in range(R):
                store_wrapped(HK, u, r, J, rows_from(L, NK, u, r) * mask)

    loop(lo - 1, hi + 1, halves, L.most)
    for r in range(R):
        M["CX"][lo, r] = M["HK"][lo - 1, r, 1 : J + 1] + M["HK"][lo, r, 1 : J + 1]

    def couple(x, U):
        HK, CX = M["HK"].at[pl.ds(x - 1, U + 2)], M["CX"].at[pl.ds(x, U + 1)]
        CY, CM, CP, D, Q = (M[name].at[pl.ds(x, U)] for name in ("CY", "CM", "CP", "D", "Q"))
        for u in range(U):
            slabs = [beside_y(L, HK, u + 1, r) for r in range(R)]
            down, up = beside_z(L, [slab[0] for slab in slabs])
            down[0] = jnp.where(lane < h, 0.0, down[0])
            up[R - 1] = jnp.where(lane >= 128 - h, 0.0, up[R - 1])
            for r in range(R):
                c, ym, yp = slabs[r]
                xm, xp = HK[u, r, 1 : J + 1], HK[u + 2, r, 1 : J + 1]
                diagonal = (xm + xp) + (ym + yp) + (down[r] + up[r]) + 6.0 * c
                CX[u + 1, r] = c + xp
                CY[u, r, 0:J] = c + ym
                CY[u, r, J] = c[J - 1] + yp[J - 1]
                low, high = c + down[r], c + up[r]
                if r == 0:
                    low = jnp.where(lane < h, 0.0, low)
                if r == R - 1:
                    high = jnp.where(lane >= 128 - h, 0.0, high)
                CM[u, r] = low
                CP[u, r] = high
                D[u, r] = diagonal
                Q[u, r] = jnp.where(c > 0.0, 1.0 / diagonal, 0.0)

    loop(lo, hi, couple, L.most)


def scale_source(L, M, name, lo, hi, start):
    J, field = L.J, M[name]

    def body(x, U):
        Q, G, VA, NS = (ref.at[pl.ds(x, U)] for ref in (M["Q"], M["G"], M["VA"], field))
        for u in range(U):
            for r in range(L.R):
                g = Q[u, r] * rows_from(L, NS, u, r)
                G[u, r] = g
                if start:
                    store_wrapped(VA, u, r, J, g * (1.0 / THETA))

    loop(lo, hi, body, L.most)


def beside_y(L, ref, x, r):
    c = ref[x, r, 1 : L.J + 1]
    low, high = ref[x, r, 0:1], ref[x, r, L.J + 1 : L.J + 2]
    return c, jnp.concatenate([low, c[:-1]], axis=0), jnp.concatenate([c[1:], high], axis=0)


def sweep(L, M, src, dst, lo, hi, step, keep_rows=None, emit=None):
    J, R = L.J, L.R

    def body(x, U):
        V, CX = M[src].at[pl.ds(x - 1, U + 2)], M["CX"].at[pl.ds(x, U + 1)]
        CY, CM, CP, D, Q, G = (M[name].at[pl.ds(x, U)] for name in ("CY", "CM", "CP", "D", "Q", "G"))
        W = M[dst].at[pl.ds(x, U)] if dst is not None else None
        if step is None:
            RN = M["RN"].at[pl.ds(x, U)]
        if keep_rows is not None:
            kept = keep_rows.at[pl.ds(x - L.x0 + 1, U)]
        for u in range(U):
            slabs = [beside_y(L, V, u + 1, r) for r in range(R)]
            down, up = beside_z(L, [slab[0] for slab in slabs])
            new = []
            for r in range(R):
                c, ym, yp = slabs[r]
                cy = CY[u, r]
                near = CX[u, r] * V[u, r, 1 : J + 1] + CX[u + 1, r] * V[u + 2, r, 1 : J + 1]
                near = near + (cy[:-1] * ym + cy[1:] * yp)
                near = near + (CM[u, r] * down[r] + CP[u, r] * up[r])
                z = G[u, r] + Q[u, r] * near
                if step is None:
                    rows_to(L, RN, u, r, D[u, r] * (z - c))
                    continue
                a, b, before = step
                value = (1.0 + a - b) * c + b * z
                if before:
                    value = value - a * W[u, r, 1 : J + 1]
                if emit is None:
                    store_wrapped(W, u, r, J, value)
                if keep_rows is not None:
                    rows_to(L, kept, u, r, value)
                new.append(value)
            if emit is not None:
                emit(x + u, new)

    loop(lo, hi, body, L.most)


def descend(L, M, margin, keep_rows=None):
    lo, hi = L.x0 - margin, L.x0 + L.nx + margin
    sweep(L, M, "VA", "VB", lo - 2, hi + 2, STEP_1 + (False,))
    sweep(L, M, "VB", "VA", lo - 1, hi + 1, STEP_2 + (True,), keep_rows=keep_rows)
    sweep(L, M, "VA", None, lo, hi, None)


def ascend(L, M, margin, emit, smoothed=None, pieces=1, after=lambda n: None):
    lo, hi = L.x0, L.x0 + L.nx

    def begin(x, U):
        HK, VA = (M[name].at[pl.ds(x, U)] for name in ("HK", "VA"))
        if smoothed is not None:
            NV = smoothed.at[pl.ds(x, U)]
        for u in range(U):
            xc = lax.shift_right_logical(x + u, 1) + L.xc
            for r in range(L.R):
                added = [M["E"][xc, r, pl.ds(L.erow + j, 8, stride=L.J), :] for j in range(L.J)]
                base = VA[u, r, 1 : L.J + 1] if smoothed is None else rows_from(L, NV, u, r)
                inside = HK[u, r, 1 : L.J + 1] > 0.0
                store_wrapped(VA, u, r, L.J, jnp.where(inside, jnp.stack(added) + base, 0.0))

    loop(lo - margin, hi + margin, begin, L.most)
    margin -= 1
    sweep(L, M, "VA", "VB", lo - margin, hi + margin, (0.0, 1.0 / THETA, False))
    margin -= 1
    sweep(L, M, "VB", "VA", lo - margin, hi + margin, STEP_1 + (True,))
    margin -= 1
    width = (hi - lo + 2 * margin) // pieces
    for n in range(pieces):
        first = lo - margin + n * width
        sweep(L, M, "VA", "VB", first, first + width, STEP_2 + (True,), emit=emit)
        after(n)


def coarsen(L, src, row, tiles, scale, put):
    lane = lanes()
    even = (lane * 2) & 127

    def body(x, U):
        pairs = src.at[pl.ds(2 * x, 2 * U)]
        for u, t in [(u, t) for u in range(U) for t in range(tiles)]:
            sums = []
            for r in range(L.R):
                rows = [pairs[2 * u + dx, r, pl.ds(row + 16 * t + b, 8, stride=2), :] for dx in (0, 1) for b in (0, 1)]
                total = (rows[0] + rows[1]) + (rows[2] + rows[3])
                if L.R == 2:
                    sums.append(pick(total + turn(total, -1, 1), even))
                else:
                    other = jnp.where((lane & L.hold) == 0, turn(total, -L.hold, 1), turn(total, L.hold, 1))
                    sums.append(total + other)
            value = jnp.where(lane < 64, sums[0], sums[1]) if L.R == 2 else sums[0]
            put(x + u, t, value * scale)

    return body


def put_rows(dst, dx, row):
    def put(x, t, value):
        dst[dx + x, 0, row + 8 * t : row + 8 * t + 8, :] = value

    return put


def kernel(gx_size, gy_size, names, source, conductance, inverse, out, *refs):
    S = dict(zip(names, refs))
    M = [{k[1:]: v for k, v in S.items() if k[0] == str(l)} for l in range(3)]
    M[2]["s2"] = S["s2"]
    gx, gy = lax.axis_index("gx"), lax.axis_index("gy")
    L0, L1, L2 = LEVELS

    def device(a, b):
        return {"gx": lax.rem(gx + a + gx_size, gx_size), "gy": lax.rem(gy + b + gy_size, gy_size)}

    class Exchange:
        def __init__(self, name):
            self.out, self.back, self.rows, self.copies = S["send_" + name], S["recv_" + name], 0, []

        def add(self, src, dst, a, b):
            copy = pltpu.make_async_remote_copy(
                src_ref=src, dst_ref=dst, send_sem=self.out, recv_sem=self.back, device_id=device(a, b), device_id_type=MESH
            )
            self.copies.append(copy)
            rows = math.prod(src.shape[:-1])
            self.rows += rows if src.dtype == F32 else rows // 2

        def start(self):
            for copy in self.copies:
                copy.start()
            return self

        def wait(self, semaphore):
            size = S["size"].at[pl.ds(0, self.rows)]
            pltpu.make_async_copy(size, size, semaphore).wait()

        def arrive(self):
            self.wait(self.back)

        def left(self):
            self.wait(self.out)

    def exchange(L, src, sx0, dst, near, far, name):
        both = Exchange(name)
        h = L.side
        for a, b in WIDE if far else AROUND:
            w = {0: L.nx, 1: near, 2: far}[abs(a)]
            xs = sx0 + (L.nx - w if a > 0 else 0)
            xd = {0: L.x0, 1: L.x0 - w, 2: L.x0 - L.nx - w, -1: L.x0 + L.nx, -2: L.x0 + 2 * L.nx}[a]
            ys = h + (L.ny - h if b > 0 else 0)
            yd, wy = {0: (h, L.ny), 1: (0, h), -1: (h + L.ny, h)}[b]
            both.add(src.at[pl.ds(xs, w), :, pl.ds(ys, wy), :], dst.at[pl.ds(xd, w), :, pl.ds(yd, wy), :], a, b)
        return both.start()

    peers = [(0, b) for b in LINE if 1 < b < gy_size - 1] + AROUND
    barrier = pltpu.get_barrier_semaphore()
    for a, b in peers:
        pl.semaphore_signal(barrier, inc=1, device_id=device(a, b), device_id_type=MESH)

    fields = (M[0]["NK"], M[0]["NS"], S["smooth0"])
    XP, YP, XR, YR = S["xp"], S["yp"], S["xr"], S["yr"]
    sub, lane = sublanes(), lanes()

    loads = [pltpu.make_async_copy(inverse, S["inverse"], S["local"].at[4])]
    for n, src in enumerate((conductance, source)):
        for r in range(2):
            loads.append(
                pltpu.make_async_copy(
                    src.at[:, :, pl.ds(128 * r, 128)],
                    fields[n].at[pl.ds(4, 16), r, pl.ds(8, 32), :],
                    S["local"].at[2 * n + r],
                )
            )
    for copy in loads:
        copy.start()

    def pack(a, field, first):
        def pack_x(i, _):
            for r in range(2):
                XP[a, 0, i, r] = field[first + i, r, 8:40, :].astype(BF16)
                XP[a, 1, i, r] = field[first + 12 + i, r, 8:40, :].astype(BF16)

        def pack_y(i, _):
            low, high = [], []
            for d in range(2):
                x = first + 2 * i + d
                near, far = field[x, 0, 8:16, :], field[x, 1, 8:16, :]
                low.append(jnp.where(sub < 4, near, turn(far, 4, 0)))
                near, far = field[x, 0, 32:40, :], field[x, 1, 32:40, :]
                high.append(jnp.where(sub < 4, turn(near, 4, 0), far))
            YP[a, 0, i] = jnp.concatenate(low, axis=0).astype(BF16)
            YP[a, 1, i] = jnp.concatenate(high, axis=0).astype(BF16)

        loop(0, 4, pack_x)
        loop(0, 8, pack_y)

    def sides(a, name):
        both = Exchange(name)
        for x, y in AROUND:
            if y == 0:
                both.add(XP.at[a, (x + 1) // 2], XR.at[a, (1 - x) // 2], x, y)
            else:
                wx = 8 if x == 0 else 2 if a == 0 else 1
                xs, xd = {0: (0, 2), 1: (8 - wx, 2 - wx), -1: (0, 10)}[x]
                both.add(YP.at[a, (y + 1) // 2, pl.ds(xs, wx)], YR.at[a, (1 - y) // 2, pl.ds(xd, wx)], x, y)
        return both.start()

    def unpack(a):
        field = fields[a]

        def unpack_x(i, _):
            for r in range(2):
                field[i, r, 8:40, :] = XR[a, 0, i, r].astype(F32)
                field[20 + i, r, 8:40, :] = XR[a, 1, i, r].astype(F32)

        def unpack_y(i, _):
            low, high = YR[a, 0, i].astype(F32), YR[a, 1, i].astype(F32)
            for d in range(2):
                x = 2 * i + d
                part = low[8 * d : 8 * d + 8]
                field[x, 0, 0:8, :] = turn(part, 4, 0)
                field[x, 1, 0:8, :] = part
                part = high[8 * d : 8 * d + 8]
                field[x, 0, 40:48, :] = part
                field[x, 1, 40:48, :] = turn(part, 4, 0)

        loop(0, 4, unpack_x)
        loop(0, 12, unpack_y)

    for a in range(2):
        loads[1 + 2 * a].wait()
        loads[2 + 2 * a].wait()
        pack(a, fields[a], 4)

    pl.semaphore_wait(barrier, len(peers))
    side_k = sides(0, "side_k")
    side_s = sides(1, "side_s")
    for a in (-1, 1):
        pl.semaphore_signal(S["ready"], inc=1, device_id=device(a, 0), device_id_type=MESH)

    def halve(field, packed):
        packed[12:20, 0, 16:32, :] = field[12:20, 0, 16:32, :].astype(BF16)

    def widen(packed, field, margin, beside):
        def take(parts):
            def body(x, U):
                for u in range(U):
                    for rows in parts:
                        field[x + u, 0, rows, :] = packed[x + u, 0, rows, :].astype(F32)

            return body

        loop(12 - margin, 12, take(beside), 12)
        loop(12, 20, take((pl.ds(0, 16), pl.ds(32, 16))), 8)
        loop(20, 20 + margin, take(beside), 12)

    loop(0, 8, coarsen(L0, M[0]["NK"].at[pl.ds(4, 16)], 8, 2, 0.125, put_rows(M[1]["NK"], 12, 16)), 4)
    halve(M[1]["NK"], S["k1"])

    loads[0].wait()
    one = lambda mask: jnp.where(mask, 1.0, 0.0).astype(BF16)
    row = lax.broadcasted_iota(jnp.int32, (128, 128), 0)
    column = lax.broadcasted_iota(jnp.int32, (128, 128), 1)
    order = one(row == ((column >> 2) & 1) * 64 + (column >> 3) * 4 + (column & 3))
    for k in range(2):
        S["mp"][128 * k : 128 * (k + 1), :] = jnp.dot(
            S["inverse"][0, k], order, preferred_element_type=F32
        ).astype(BF16)

    row = lax.broadcasted_iota(jnp.int32, (4, 48, 256), 1)
    column = lax.broadcasted_iota(jnp.int32, (4, 48, 256), 2)
    layer = jnp.where(row >= 24, 1, 0)
    row = row - 24 * layer
    half = jnp.where(row >= 12, 1, 0)
    row = row - 12 * half + 4 * lax.broadcasted_iota(jnp.int32, (4, 48, 256), 0)
    base = layer * 128 + half * 64

    def share(d, _):
        chosen = one(column == base + ((row + (16 * d + 60)) & 63)).reshape(192, 256)
        rows = jnp.dot(chosen, S["mp"][...], preferred_element_type=F32)
        S["ms"][pl.ds(4 * d, 4)] = rows.astype(BF16).reshape(4, 48, 128)

    loop(0, gy_size // 4, share)
    pl.semaphore_wait(S["ready"], 2)
    kappa_1 = exchange(L1, S["k1"], 12, S["k1"], 8, 4, "kappa_1")

    place = (gx, gy, gx_size, gy_size)
    side_k.arrive()
    unpack(0)
    prepare(L0, M[0], 1, 23, *place)
    side_s.arrive()
    unpack(1)
    scale_source(L0, M[0], "NS", 1, 23, True)
    descend(L0, M[0], 0, S["keep0"])
    residual = M[0]["RN"].at[pl.ds(4, 16)]
    loop(0, 8, coarsen(L0, residual, 8, 2, 0.5, put_rows(M[1]["NS"], 12, 16)), 8)
    halve(M[1]["NS"], S["s1"])
    for i in range(4):
        for side in range(2):
            rows = pl.ds(16 + 8 * side, 8)
            both = [M[1]["NS"][12 + 2 * i + d, 0, rows, :] for d in range(2)]
            S["cp"][side, i] = jnp.concatenate(both, axis=0).astype(BF16)
    source_1 = Exchange("source_1")
    for a in (-1, 1):
        for b in (-1, 1):
            source_1.add(S["cp"].at[(b + 1) // 2], S["cr"].at[(1 - b) // 2, (1 - a) // 2], a, b)
    own = pl.ds(16, 16)
    for a, xs, xd, w in ((-2, 12, 28, 1), (2, 19, 3, 1), (-1, 12, 20, 8), (1, 12, 4, 8)):
        source_1.add(S["s1"].at[pl.ds(xs, w), :, own, :], S["s1"].at[pl.ds(xd, w), :, own, :], a, 0)
    own = S["s1"].at[pl.ds(12, 8), :, pl.ds(16, 16), :]
    for b in (-1, 1):
        source_1.add(own, S["s1"].at[pl.ds(12, 8), :, pl.ds(16 - 16 * b, 16), :], 0, b)
    source_1.start()

    kappa_1.arrive()
    widen(S["k1"], M[1]["NK"], 12, (pl.ds(0, 48),))
    prepare(L1, M[1], 3, 29, *place)
    loop(0, 16, coarsen(L1, M[1]["NK"], 0, 3, 0.125, put_rows(M[2]["NK"], 2, 0)), 8)
    prepare(L2, M[2], 3, 17, *place)
    matrices = Exchange("matrix")
    for n in LINE:
        matrices.add(S["ms"].at[lax.rem(gy + n, gy_size)], S["mm"].at[gy], 0, n)
    matrices.start()
    S["mm"][gy] = S["ms"][gy]
    pack(2, S["keep0"], 1)
    side_v = sides(2, "side_v")

    source_1.arrive()
    widen(S["s1"], M[1]["NS"], 9, (pl.ds(16, 16),))
    for i in range(4):
        for ys in range(2):
            for xs in range(2):
                both = S["cr"][ys, xs, i].astype(F32)
                for d in range(2):
                    M[1]["NS"][4 + 16 * xs + 2 * i + d, 0, pl.ds(8 + 24 * ys, 8), :] = both[8 * d : 8 * d + 8]
    scale_source(L1, M[1], "NS", 3, 29, True)
    descend(L1, M[1], 6)

    residual = M[1]["RN"].at[pl.ds(6, 20)]
    loop(0, 10, coarsen(L1, residual, 0, 3, 0.5, put_rows(S["s2"], 5, 0)), 10)
    scale_source(L2, M[2], "s2", 5, 15, True)
    descend(L2, M[2], 0, S["keep2"])
    tiles = []
    residual = M[2]["RN"].at[pl.ds(8, 4)]
    loop(0, 2, coarsen(L2, residual, 8, 1, 1.0 / 128.0, lambda x, t, value: tiles.append(value)), 2)
    rounded = jnp.where(sub < 4, tiles[0], turn(tiles[1], 4, 0)).astype(BF16).astype(F32)
    S["mine"][...] = rounded
    gathered = Exchange("gather")
    for n in LINE:
        gathered.add(S["mine"], S["all"].at[gy], 0, n)
    gathered.start()
    odd = (lanes(4) & 1) == 1
    pair = S["pair"]
    pair[8:12, 0, 8:16, :] = jnp.where(odd, S["keep2"][1:5, 0, 8:16, :], S["s2"][8:12, 0, 8:16, :])
    level_2 = exchange(L2, pair, 8, pair, 4, 4, "level_2")
    S["all"][gy] = rounded

    kept = pltpu.make_async_copy(
        S["keep0"].at[pl.ds(1, 16), :, pl.ds(8, 32), :],
        S["smooth0"].at[pl.ds(4, 16), :, pl.ds(8, 32), :],
        S["local"].at[0],
    )
    kept.start()
    for old in (side_k, side_s, kappa_1, source_1, matrices, side_v):
        old.left()
    side_v.arrive()
    unpack(2)
    kept.wait()
    matrices.arrive()
    gathered.arrive()
    right = S["all"][...].reshape(gy_size * 8, 128).astype(BF16)
    product = jnp.dot(S["mm"][...].reshape(gy_size * 48, 128), right, preferred_element_type=F32)
    layer_of = lax.broadcasted_iota(jnp.int32, (24, 128), 1) >> 2
    terms = [jnp.where(layer_of == k, product[24 * k : 24 * k + 24], 0.0) for k in range(2 * gy_size)]
    while len(terms) > 1:
        terms = [terms[i] + terms[i + 1] for i in range(0, len(terms), 2)]
    S["corr"][2] = terms[0]
    coarse = Exchange("coarse")
    for a in (-2, -1, 1, 2):
        coarse.add(S["corr"].at[2], S["corr"].at[2 - a], a, 0)
    coarse.start()
    gathered.left()
    level_2.left()
    level_2.arrive()

    def part(x, U):
        for u in range(U):
            for t in range(3):
                rows = pl.ds(8 * t, 8)
                both = pair[x + u, 0, rows, :]
                second = (lane & 1) == 1
                M[2]["NS"][x + u, 0, rows, :] = jnp.where(second, turn(both, 1, 1), both)
                S["smooth2"][x + u, 0, rows, :] = jnp.where(second, both, turn(both, -1, 1))

    loop(2, 18, part, 8)
    scale_source(L2, M[2], "NS", 3, 17, False)
    coarse.arrive()

    for slab in range(5):
        for d in range(2):
            for b in range(2):
                M[2]["E"][2 * slab + d, 0, pl.ds(b, 8, stride=2), :] = S["corr"][slab, 12 * d : 12 * d + 8, :]
                M[2]["E"][2 * slab + d, 0, pl.ds(16 + b, 4, stride=2), :] = S["corr"][slab, 12 * d + 8 : 12 * d + 12, :]

    def emit_2(x, new):
        for j in range(L2.J):
            for b in range(2):
                M[1]["E"][x, 0, pl.ds(2 * j + b, 8, stride=2 * L2.J), :] = new[0][j]

    def spread():
        for r in range(2):
            half = (lane >> 1) + 64 * r
            for x in range(L1.x0 - 2, L1.x0 + L1.nx + 2):
                for j in range(L1.J):
                    value = pick(M[1]["VB"][x, 0, j + 1], half)
                    for b in range(2):
                        M[0]["E"][x, r, pl.ds(2 * j + b, 8, stride=2 * L1.J), :] = value

    def emit_0(x, new):
        for r in range(2):
            for j in range(L0.J):
                S["result"][x - L0.x0, r, rows_of(L0, j), :] = new[r][j]

    ascend(L2, M[2], 6, emit_2, S["smooth2"])
    ascend(L1, M[1], 5, None)
    spread()
    stores = []

    def store(n):
        for r in range(2):
            copy = pltpu.make_async_copy(
                S["result"].at[pl.ds(8 * n, 8), r, pl.ds(8, 32), :],
                out.at[pl.ds(8 * n, 8), :, pl.ds(128 * r, 128)],
                S["local"].at[2 * n + r],
            )
            copy.start()
            stores.append(copy)

    ascend(L0, M[0], 3, emit_0, S["smooth0"], 2, store)
    coarse.left()
    for copy in stores:
        copy.wait()


def solution(mesh):
    gx_size, gy_size = mesh.shape["gx"], mesh.shape["gy"]
    scratch = {}
    for l, L in enumerate(LEVELS):
        for name, shape in L.scratch().items():
            scratch[str(l) + name] = shape
    scratch["xp"] = pltpu.VMEM((3, 2, 4, 2, 32, 128), BF16)
    scratch["xr"] = pltpu.VMEM((3, 2, 4, 2, 32, 128), BF16)
    scratch["yp"] = pltpu.VMEM((3, 2, 8, 16, 128), BF16)
    scratch["yr"] = pltpu.VMEM((3, 2, 12, 16, 128), BF16)
    scratch["k1"] = pltpu.VMEM((32, 1, 48, 128), BF16)
    scratch["s1"] = pltpu.VMEM((32, 1, 48, 128), BF16)
    scratch["cp"] = pltpu.VMEM((2, 4, 16, 128), BF16)
    scratch["cr"] = pltpu.VMEM((2, 2, 4, 16, 128), BF16)
    scratch["s2"] = pltpu.VMEM((20, 1, 24, 128), F32)
    scratch["keep0"] = pltpu.VMEM((18, 2, 48, 128), F32)
    scratch["smooth0"] = pltpu.VMEM((24, 2, 48, 128), F32)
    scratch["keep2"] = pltpu.VMEM((6, 1, 24, 128), F32)
    scratch["pair"] = pltpu.VMEM((20, 1, 24, 128), F32)
    scratch["smooth2"] = pltpu.VMEM((20, 1, 24, 128), F32)
    scratch["size"] = pltpu.VMEM((768, 128), F32)
    scratch["inverse"] = pltpu.VMEM((1, 2, 128, 128), BF16)
    scratch["mp"] = pltpu.VMEM((256, 128), BF16)
    scratch["ms"] = pltpu.VMEM((gy_size, 48, 128), BF16)
    scratch["mm"] = pltpu.VMEM((gy_size, 48, 128), BF16)
    scratch["mine"] = pltpu.VMEM((8, 128), F32)
    scratch["all"] = pltpu.VMEM((gy_size, 8, 128), F32)
    scratch["corr"] = pltpu.VMEM((5, 24, 128), F32)
    scratch["result"] = pltpu.VMEM((16, 2, 48, 128), F32)
    scratch["ready"] = pltpu.SemaphoreType.REGULAR
    scratch["local"] = pltpu.SemaphoreType.DMA((5,))
    for name in EXCHANGES:
        scratch["send_" + name] = pltpu.SemaphoreType.DMA
        scratch["recv_" + name] = pltpu.SemaphoreType.DMA

    def local(pressure_source, conductance, coarse_inverse):
        return pl.pallas_call(
            functools.partial(kernel, gx_size, gy_size, tuple(scratch)),
            out_shape=pltpu.VMEM(pressure_source.shape, F32),
            in_specs=[
                pl.BlockSpec(memory_space=pl.ANY),
                pl.BlockSpec(memory_space=pl.ANY),
                pl.BlockSpec(memory_space=pl.ANY),
            ],
            out_specs=pl.BlockSpec(memory_space=pl.ANY),
            scratch_shapes=list(scratch.values()),
            compiler_params=pltpu.CompilerParams(
                collective_id=0, has_side_effects=True, vmem_limit_bytes=40 * 2**20
            ),
        )(*(pltpu.with_memory_space_constraint(x, pltpu.HBM) for x in (pressure_source, conductance, coarse_inverse)))

    in_specs = (P("gx", "gy", None), P("gx", "gy", None), P("gx", "gy", None, None))
    return jax.shard_map(local, mesh=mesh, in_specs=in_specs, out_specs=P("gx", "gy", None), check_vma=False)
```

```python
import functools
import math

import jax
import jax.numpy as jnp
from jax import lax
from jax.experimental import pallas as pl
from jax.experimental.pallas import tpu as pltpu
from jax.sharding import PartitionSpec as P

MESH = pl.DeviceIdType.MESH

LMAX = 2.0
LMIN = 0.25
THETA = 0.5 * (LMAX + LMIN)
DELTA = 0.5 * (LMAX - LMIN)
SIGMA = THETA / DELTA
RATIO_0 = 1.0 / SIGMA
RATIO_1 = 1.0 / (2.0 * SIGMA - RATIO_0)
RATIO_2 = 1.0 / (2.0 * SIGMA - RATIO_1)
STEP_1 = (RATIO_1 * RATIO_0, 2.0 * RATIO_1 / DELTA)
STEP_2 = (RATIO_2 * RATIO_1, 2.0 * RATIO_2 / DELTA)

F32 = jnp.float32
BF16 = jnp.bfloat16

EXCHANGES = ("side_k", "side_s", "side_v", "kappa_1", "matrix", "source_1", "gather", "level_2", "coarse")
AROUND = [(a, b) for a in (-1, 0, 1) for b in (-1, 0, 1) if (a, b) != (0, 0)]
WIDE = [(a, b) for a in (-2, -1, 0, 1, 2) for b in (-1, 0, 1) if (a, b) != (0, 0)]
AROUND.sort(key=lambda o: -abs(o[0]) - 2 * abs(o[1]))
WIDE.sort(key=lambda o: -abs(o[0]) - 2 * abs(o[1]))
LINE = sorted(range(1, 16), key=lambda n: -min(n // 4, 4 - n // 4) - min(n % 4, 4 - n % 4))


class Level:
    def __init__(self, nx, ny, x0, side, R, J, hold, row0, erow, xc, coarse, most):
        self.nx, self.ny, self.X, self.x0, self.side = nx, ny, nx + 2 * x0, x0, side
        self.R, self.J, self.hold, self.row0, self.most = R, J, hold, row0, most
        self.erow, self.xc, self.coarse = erow, xc, coarse
        self.rows = ny + 2 * side

    def scratch(self):
        X, R, J = self.X, self.R, self.J
        vm = lambda *shape: pltpu.VMEM(shape + (128,), F32)
        blocked = {name: vm(X, R, J, 8) for name in ("CM", "CP", "Q", "D")}
        natural = {name: vm(X, R, self.rows) for name in ("NS", "NK", "RN")}
        return dict(
            E=vm(self.coarse[0], R, self.coarse[1]),
            HK=vm(X, R, J + 2, 8),
            CX=vm(X + 1, R, J, 8),
            CY=vm(X, R, J + 1, 8),
            G=vm(X, R, J + 2, 8),
            VA=vm(X, R, J + 2, 8),
            VB=vm(X, R, J + 2, 8),
            **blocked,
            **natural,
        )


LEVELS = (
    Level(16, 32, 4, 8, 2, 5, 1, 4, 20, 10, (32, 80), 22),
    Level(8, 16, 12, 16, 1, 5, 1, 4, 4, 2, (20, 48), 26),
    Level(4, 8, 8, 8, 1, 3, 2, 0, 0, 0, (10, 24), 16),
)


def lanes(*lead):
    return lax.broadcasted_iota(jnp.int32, lead + (8, 128), len(lead) + 1)


def sublanes():
    return lax.broadcasted_iota(jnp.int32, (8, 128), 0)


def turn(value, shift, axis):
    return pltpu.roll(value, shift % value.shape[axis], axis)


def pick(value, index):
    return jnp.take_along_axis(value, index, axis=1, mode="promise_in_bounds")


def rows_of(L, j):
    return pl.ds(L.row0 + j, 8, stride=L.J)


def beside_z(L, parts):
    h = L.hold
    down = [turn(p, h, 2) for p in parts]
    up = [turn(p, -h, 2) for p in parts]
    if L.R == 2:
        lane = lanes(L.J)
        down[1] = jnp.where(lane == 0, down[0], down[1])
        up[0] = jnp.where(lane == 127, up[1], up[0])
    return down, up


def store_wrapped(ref, x, r, J, values):
    ref[x, r, 1 : J + 1] = values
    ref[x, r, 0] = turn(values[J - 1], 1, 0)
    ref[x, r, J + 1] = turn(values[0], -1, 0)


def rows_from(L, ref, x, r):
    return jnp.stack([ref[x, r, rows_of(L, j), :] for j in range(L.J)])


def rows_to(L, ref, x, r, values):
    for j in range(L.J):
        ref[x, r, rows_of(L, j), :] = values[j]


def loop(lo, hi, body, most=1):
    count = hi - lo
    steps = -(-count // most)
    U = -(-count // steps)
    whole = count // U
    if whole > 1:

        def step(i, carry):
            body(lo + i * U, U)
            return carry

        lax.fori_loop(0, whole, step, 0)
    elif whole == 1:
        body(lo, U)
    if count > whole * U:
        body(lo + whole * U, count - whole * U)


def prepare(L, M, lo, hi, gx, gy, count_x, count_y):
    J, R, h = L.J, L.R, L.hold
    shape = (J, 8, 128)
    lane = lanes(J)
    place = lax.broadcasted_iota(jnp.int32, shape, 0) + J * lax.broadcasted_iota(jnp.int32, shape, 1)
    place = place + (gy * L.ny - L.side + L.row0)
    keep = jnp.where((place >= 0) & (place < L.ny * count_y), 0.5, 0.0).astype(F32)

    def halves(x, U):
        NK, HK = M["NK"].at[pl.ds(x, U)], M["HK"].at[pl.ds(x, U)]
        for u in range(U):
            place = gx * L.nx + x + u - L.x0
            inside = jnp.where((place >= 0) & (place < L.nx * count_x), 1.0, 0.0).astype(F32)
            mask = keep * inside
            for r in range(R):
                store_wrapped(HK, u, r, J, rows_from(L, NK, u, r) * mask)

    loop(lo - 1, hi + 1, halves, L.most)
    for r in range(R):
        M["CX"][lo, r] = M["HK"][lo - 1, r, 1 : J + 1] + M["HK"][lo, r, 1 : J + 1]

    def couple(x, U):
        HK, CX = M["HK"].at[pl.ds(x - 1, U + 2)], M["CX"].at[pl.ds(x, U + 1)]
        CY, CM, CP, D, Q = (M[name].at[pl.ds(x, U)] for name in ("CY", "CM", "CP", "D", "Q"))
        for u in range(U):
            slabs = [beside_y(L, HK, u + 1, r) for r in range(R)]
            down, up = beside_z(L, [slab[0] for slab in slabs])
            down[0] = jnp.where(lane < h, 0.0, down[0])
            up[R - 1] = jnp.where(lane >= 128 - h, 0.0, up[R - 1])
            for r in range(R):
                c, ym, yp = slabs[r]
                xm, xp = HK[u, r, 1 : J + 1], HK[u + 2, r, 1 : J + 1]
                diagonal = (xm + xp) + (ym + yp) + (down[r] + up[r]) + 6.0 * c
                CX[u + 1, r] = c + xp
                CY[u, r, 0:J] = c + ym
                CY[u, r, J] = c[J - 1] + yp[J - 1]
                low, high = c + down[r], c + up[r]
                if r == 0:
                    low = jnp.where(lane < h, 0.0, low)
                if r == R - 1:
                    high = jnp.where(lane >= 128 - h, 0.0, high)
                CM[u, r] = low
                CP[u, r] = high
                D[u, r] = diagonal
                Q[u, r] = jnp.where(c > 0.0, 1.0 / diagonal, 0.0)

    loop(lo, hi, couple, L.most)


def scale_source(L, M, name, lo, hi):
    field = M[name]

    def body(x, U):
        Q, G, NS = (ref.at[pl.ds(x, U)] for ref in (M["Q"], M["G"], field))
        for u in range(U):
            for r in range(L.R):
                store_wrapped(G, u, r, L.J, Q[u, r] * rows_from(L, NS, u, r))

    loop(lo, hi, body, L.most)


def beside_y(L, ref, x, r):
    c = ref[x, r, 1 : L.J + 1]
    low, high = ref[x, r, 0:1], ref[x, r, L.J + 1 : L.J + 2]
    return c, jnp.concatenate([low, c[:-1]], axis=0), jnp.concatenate([c[1:], high], axis=0)


def sweep(L, M, src, dst, lo, hi, step, keep_rows=None, emit=None):
    J, R = L.J, L.R

    def body(x, U):
        V, CX = M[src].at[pl.ds(x - 1, U + 2)], M["CX"].at[pl.ds(x, U + 1)]
        CY, CM, CP, D, Q, GW = (M[name].at[pl.ds(x, U)] for name in ("CY", "CM", "CP", "D", "Q", "G"))
        W = M[dst].at[pl.ds(x, U)] if dst is not None else None
        if step is None:
            RN = M["RN"].at[pl.ds(x, U)]
        if keep_rows is not None:
            kept = keep_rows.at[pl.ds(x - L.x0 + 1, U)]
        for u in range(U):
            slabs = [beside_y(L, V, u + 1, r) for r in range(R)]
            down, up = beside_z(L, [slab[0] for slab in slabs])
            new = []
            for r in range(R):
                c, ym, yp = slabs[r]
                cy = CY[u, r]
                near = CX[u, r] * V[u, r, 1 : J + 1] + CX[u + 1, r] * V[u + 2, r, 1 : J + 1]
                near = near + (cy[:-1] * ym + cy[1:] * yp)
                near = near + (CM[u, r] * down[r] + CP[u, r] * up[r])
                near = Q[u, r] * near
                if step is None:
                    rows_to(L, RN, u, r, D[u, r] * (GW[u, r, 1 : J + 1] + near - c))
                    continue
                p, g, scale, before = step
                if g == scale:
                    value = p * c + scale * (GW[u, r, 1 : J + 1] + near)
                elif g == 0.0:
                    value = p * c + scale * near
                else:
                    value = p * c + g * GW[u, r, 1 : J + 1] + scale * near
                if before != 0.0:
                    value = value - before * W[u, r, 1 : J + 1]
                if emit is None:
                    store_wrapped(W, u, r, J, value)
                if keep_rows is not None:
                    rows_to(L, kept, u, r, value)
                new.append(value)
            if emit is not None:
                emit(x + u, new)

    loop(lo, hi, body, L.most)


def next_step(step):
    a, b = step
    return (1.0 + a - b, b, b, a)


def descend(L, M, margin, keep_rows=None):
    lo, hi = L.x0 - margin, L.x0 + L.nx + margin
    (a, b), (c, d) = STEP_1, STEP_2
    sweep(L, M, "G", "VB", lo - 2, hi + 2, ((1.0 + a - b) / THETA + b, 0.0, b / THETA, 0.0))
    sweep(L, M, "VB", "VA", lo - 1, hi + 1, (1.0 + c - d, d - c / THETA, d, 0.0), keep_rows=keep_rows)
    sweep(L, M, "VA", None, lo, hi, None)


def ascend(L, M, margin, emit, smoothed=None, pieces=1, after=lambda n: None):
    lo, hi = L.x0, L.x0 + L.nx

    def begin(x, U):
        HK, VA = (M[name].at[pl.ds(x, U)] for name in ("HK", "VA"))
        if smoothed is not None:
            NV = smoothed.at[pl.ds(x, U)]
        for u in range(U):
            xc = lax.shift_right_logical(x + u, 1) + L.xc
            for r in range(L.R):
                added = [M["E"][xc, r, pl.ds(L.erow + j, 8, stride=L.J), :] for j in range(L.J)]
                base = VA[u, r, 1 : L.J + 1] if smoothed is None else rows_from(L, NV, u, r)
                inside = HK[u, r, 1 : L.J + 1] > 0.0
                store_wrapped(VA, u, r, L.J, jnp.where(inside, jnp.stack(added) + base, 0.0))

    loop(lo - margin, hi + margin, begin, L.most)
    margin -= 1
    sweep(L, M, "VA", "VB", lo - margin, hi + margin, (1.0 - 1.0 / THETA, 1.0 / THETA, 1.0 / THETA, 0.0))
    margin -= 1
    sweep(L, M, "VB", "VA", lo - margin, hi + margin, next_step(STEP_1))
    margin -= 1
    width = (hi - lo + 2 * margin) // pieces
    for n in range(pieces):
        first = lo - margin + n * width
        sweep(L, M, "VA", "VB", first, first + width, next_step(STEP_2), emit=emit)
        after(n)


def coarsen(L, src, row, tiles, scale, put):
    lane = lanes()
    even = (lane * 2) & 127

    def body(x, U):
        pairs = src.at[pl.ds(2 * x, 2 * U)]
        for u, t in [(u, t) for u in range(U) for t in range(tiles)]:
            sums = []
            for r in range(L.R):
                rows = [pairs[2 * u + dx, r, pl.ds(row + 16 * t + b, 8, stride=2), :] for dx in (0, 1) for b in (0, 1)]
                total = (rows[0] + rows[1]) + (rows[2] + rows[3])
                if L.R == 2:
                    sums.append(pick(total + turn(total, -1, 1), even))
                else:
                    other = jnp.where((lane & L.hold) == 0, turn(total, -L.hold, 1), turn(total, L.hold, 1))
                    sums.append(total + other)
            value = jnp.where(lane < 64, sums[0], sums[1]) if L.R == 2 else sums[0]
            put(x + u, t, value * scale)

    return body


def put_rows(dst, dx, row):
    def put(x, t, value):
        dst[dx + x, 0, row + 8 * t : row + 8 * t + 8, :] = value

    return put


def kernel(gx_size, gy_size, names, source, conductance, inverse, out, *refs):
    S = dict(zip(names, refs))
    M = [{k[1:]: v for k, v in S.items() if k[0] == str(l)} for l in range(3)]
    M[2]["s2"] = S["s2"]
    gx, gy = lax.axis_index("gx"), lax.axis_index("gy")
    L0, L1, L2 = LEVELS

    def device(a, b):
        return {"gx": lax.rem(gx + a + gx_size, gx_size), "gy": lax.rem(gy + b + gy_size, gy_size)}

    class Exchange:
        def __init__(self, name):
            self.out, self.back, self.rows, self.copies = S["send_" + name], S["recv_" + name], 0, []

        def add(self, src, dst, a, b):
            copy = pltpu.make_async_remote_copy(
                src_ref=src, dst_ref=dst, send_sem=self.out, recv_sem=self.back, device_id=device(a, b), device_id_type=MESH
            )
            self.copies.append(copy)
            rows = math.prod(src.shape[:-1])
            self.rows += rows if src.dtype == F32 else rows // 2

        def start(self):
            for copy in self.copies:
                copy.start()
            return self

        def wait(self, semaphore):
            size = S["size"].at[pl.ds(0, self.rows)]
            pltpu.make_async_copy(size, size, semaphore).wait()

        def arrive(self):
            self.wait(self.back)

        def left(self):
            self.wait(self.out)

    def exchange(L, src, sx0, dst, near, far, name):
        both = Exchange(name)
        h = L.side
        for a, b in WIDE if far else AROUND:
            w = {0: L.nx, 1: near, 2: far}[abs(a)]
            xs = sx0 + (L.nx - w if a > 0 else 0)
            xd = {0: L.x0, 1: L.x0 - w, 2: L.x0 - L.nx - w, -1: L.x0 + L.nx, -2: L.x0 + 2 * L.nx}[a]
            ys = h + (L.ny - h if b > 0 else 0)
            yd, wy = {0: (h, L.ny), 1: (0, h), -1: (h + L.ny, h)}[b]
            both.add(src.at[pl.ds(xs, w), :, pl.ds(ys, wy), :], dst.at[pl.ds(xd, w), :, pl.ds(yd, wy), :], a, b)
        return both.start()

    peers = [(0, b) for b in LINE if 1 < b < gy_size - 1] + AROUND
    barrier = pltpu.get_barrier_semaphore()
    for a, b in peers:
        pl.semaphore_signal(barrier, inc=1, device_id=device(a, b), device_id_type=MESH)

    fields = (M[0]["NK"], M[0]["NS"], S["smooth0"])
    XP, YP, XR, YR = S["xp"], S["yp"], S["xr"], S["yr"]
    sub, lane = sublanes(), lanes()

    loads = [pltpu.make_async_copy(inverse, S["inverse"], S["local"].at[4])]
    for n, src in enumerate((conductance, source)):
        for r in range(2):
            loads.append(
                pltpu.make_async_copy(
                    src.at[:, :, pl.ds(128 * r, 128)],
                    fields[n].at[pl.ds(4, 16), r, pl.ds(8, 32), :],
                    S["local"].at[2 * n + r],
                )
            )
    for copy in loads:
        copy.start()

    def pack(a, field, first):
        def pack_x(i, _):
            for r in range(2):
                XP[a, 0, i, r] = field[first + i, r, 8:40, :].astype(BF16)
                XP[a, 1, i, r] = field[first + 12 + i, r, 8:40, :].astype(BF16)

        def pack_y(i, _):
            low, high = [], []
            for d in range(2):
                x = first + 2 * i + d
                near, far = field[x, 0, 8:16, :], field[x, 1, 8:16, :]
                low.append(jnp.where(sub < 4, near, turn(far, 4, 0)))
                near, far = field[x, 0, 32:40, :], field[x, 1, 32:40, :]
                high.append(jnp.where(sub < 4, turn(near, 4, 0), far))
            YP[a, 0, i] = jnp.concatenate(low, axis=0).astype(BF16)
            YP[a, 1, i] = jnp.concatenate(high, axis=0).astype(BF16)

        loop(0, 4, pack_x)
        loop(0, 8, pack_y)

    def sides(a, name):
        both = Exchange(name)
        for x, y in AROUND:
            if y == 0:
                both.add(XP.at[a, (x + 1) // 2], XR.at[a, (1 - x) // 2], x, y)
            else:
                wx = 8 if x == 0 else 2 if a == 0 else 1
                xs, xd = {0: (0, 2), 1: (8 - wx, 2 - wx), -1: (0, 10)}[x]
                both.add(YP.at[a, (y + 1) // 2, pl.ds(xs, wx)], YR.at[a, (1 - y) // 2, pl.ds(xd, wx)], x, y)
        return both.start()

    def unpack(a):
        field = fields[a]

        def unpack_x(i, _):
            for r in range(2):
                field[i, r, 8:40, :] = XR[a, 0, i, r].astype(F32)
                field[20 + i, r, 8:40, :] = XR[a, 1, i, r].astype(F32)

        def unpack_y(i, _):
            low, high = YR[a, 0, i].astype(F32), YR[a, 1, i].astype(F32)
            for d in range(2):
                x = 2 * i + d
                part = low[8 * d : 8 * d + 8]
                field[x, 0, 0:8, :] = turn(part, 4, 0)
                field[x, 1, 0:8, :] = part
                part = high[8 * d : 8 * d + 8]
                field[x, 0, 40:48, :] = part
                field[x, 1, 40:48, :] = turn(part, 4, 0)

        loop(0, 4, unpack_x)
        loop(0, 12, unpack_y)

    for a in range(2):
        loads[1 + 2 * a].wait()
        loads[2 + 2 * a].wait()
        pack(a, fields[a], 4)

    pl.semaphore_wait(barrier, len(peers))
    side_k = sides(0, "side_k")
    side_s = sides(1, "side_s")
    for a in (-1, 1):
        pl.semaphore_signal(S["ready"], inc=1, device_id=device(a, 0), device_id_type=MESH)

    def halve(field, packed):
        packed[12:20, 0, 16:32, :] = field[12:20, 0, 16:32, :].astype(BF16)

    def widen(packed, field, margin, beside):
        def take(parts):
            def body(x, U):
                for u in range(U):
                    for rows in parts:
                        field[x + u, 0, rows, :] = packed[x + u, 0, rows, :].astype(F32)

            return body

        loop(12 - margin, 12, take(beside), 12)
        loop(12, 20, take((pl.ds(0, 16), pl.ds(32, 16))), 8)
        loop(20, 20 + margin, take(beside), 12)

    loop(0, 8, coarsen(L0, M[0]["NK"].at[pl.ds(4, 16)], 8, 2, 0.125, put_rows(M[1]["NK"], 12, 16)), 4)
    halve(M[1]["NK"], S["k1"])

    loads[0].wait()
    one = lambda mask: jnp.where(mask, 1.0, 0.0).astype(BF16)
    row = lax.broadcasted_iota(jnp.int32, (128, 128), 0)
    column = lax.broadcasted_iota(jnp.int32, (128, 128), 1)
    order = one(row == ((column >> 2) & 1) * 64 + (column >> 3) * 4 + (column & 3))
    for k in range(2):
        S["mp"][128 * k : 128 * (k + 1), :] = jnp.dot(
            S["inverse"][0, k], order, preferred_element_type=F32
        ).astype(BF16)

    row = lax.broadcasted_iota(jnp.int32, (4, 48, 256), 1)
    column = lax.broadcasted_iota(jnp.int32, (4, 48, 256), 2)
    layer = jnp.where(row >= 24, 1, 0)
    row = row - 24 * layer
    half = jnp.where(row >= 12, 1, 0)
    row = row - 12 * half + 4 * lax.broadcasted_iota(jnp.int32, (4, 48, 256), 0)
    base = layer * 128 + half * 64

    def share(d, _):
        chosen = one(column == base + ((row + (16 * d + 60)) & 63)).reshape(192, 256)
        rows = jnp.dot(chosen, S["mp"][...], preferred_element_type=F32)
        S["ms"][pl.ds(4 * d, 4)] = rows.astype(BF16).reshape(4, 48, 128)

    loop(0, gy_size // 4, share)
    pl.semaphore_wait(S["ready"], 2)
    kappa_1 = exchange(L1, S["k1"], 12, S["k1"], 8, 4, "kappa_1")

    place = (gx, gy, gx_size, gy_size)
    side_k.arrive()
    unpack(0)
    prepare(L0, M[0], 1, 23, *place)
    side_s.arrive()
    unpack(1)
    scale_source(L0, M[0], "NS", 1, 23)
    descend(L0, M[0], 0, S["keep0"])
    residual = M[0]["RN"].at[pl.ds(4, 16)]
    loop(0, 8, coarsen(L0, residual, 8, 2, 0.5, put_rows(M[1]["NS"], 12, 16)), 8)
    halve(M[1]["NS"], S["s1"])
    for i in range(4):
        for side in range(2):
            rows = pl.ds(16 + 8 * side, 8)
            both = [M[1]["NS"][12 + 2 * i + d, 0, rows, :] for d in range(2)]
            S["cp"][side, i] = jnp.concatenate(both, axis=0).astype(BF16)
    source_1 = Exchange("source_1")
    for a in (-1, 1):
        for b in (-1, 1):
            source_1.add(S["cp"].at[(b + 1) // 2], S["cr"].at[(1 - b) // 2, (1 - a) // 2], a, b)
    own = S["s1"].at[pl.ds(12, 8), :, pl.ds(16, 16), :]
    for b in (-1, 1):
        source_1.add(own, S["s1"].at[pl.ds(12, 8), :, pl.ds(16 - 16 * b, 16), :], 0, b)
    own = pl.ds(16, 16)
    for a, xs, xd, w in ((-2, 12, 28, 1), (2, 19, 3, 1), (-1, 12, 20, 8), (1, 12, 4, 8)):
        source_1.add(S["s1"].at[pl.ds(xs, w), :, own, :], S["s1"].at[pl.ds(xd, w), :, own, :], a, 0)
    source_1.start()

    kappa_1.arrive()
    widen(S["k1"], M[1]["NK"], 12, (pl.ds(0, 48),))
    prepare(L1, M[1], 3, 29, *place)
    loop(0, 16, coarsen(L1, M[1]["NK"], 0, 3, 0.125, put_rows(M[2]["NK"], 2, 0)), 8)
    prepare(L2, M[2], 3, 17, *place)
    matrices = Exchange("matrix")
    for n in LINE:
        matrices.add(S["ms"].at[lax.rem(gy + n, gy_size)], S["mm"].at[gy], 0, n)
    matrices.start()
    S["mm"][gy] = S["ms"][gy]
    pack(2, S["keep0"], 1)
    side_v = sides(2, "side_v")

    source_1.arrive()
    widen(S["s1"], M[1]["NS"], 9, (pl.ds(16, 16),))
    for i in range(4):
        for ys in range(2):
            for xs in range(2):
                both = S["cr"][ys, xs, i].astype(F32)
                for d in range(2):
                    M[1]["NS"][4 + 16 * xs + 2 * i + d, 0, pl.ds(8 + 24 * ys, 8), :] = both[8 * d : 8 * d + 8]
    scale_source(L1, M[1], "NS", 3, 29)
    descend(L1, M[1], 6)

    residual = M[1]["RN"].at[pl.ds(6, 20)]
    loop(0, 10, coarsen(L1, residual, 0, 3, 0.5, put_rows(S["s2"], 5, 0)), 10)
    scale_source(L2, M[2], "s2", 5, 15)
    descend(L2, M[2], 0, S["keep2"])
    tiles = []
    residual = M[2]["RN"].at[pl.ds(8, 4)]
    loop(0, 2, coarsen(L2, residual, 8, 1, 1.0 / 128.0, lambda x, t, value: tiles.append(value)), 2)
    rounded = jnp.where(sub < 4, tiles[0], turn(tiles[1], 4, 0)).astype(BF16).astype(F32)
    S["mine"][...] = rounded
    gathered = Exchange("gather")
    for n in LINE:
        gathered.add(S["mine"], S["all"].at[gy], 0, n)
    gathered.start()
    odd = (lanes(4) & 1) == 1
    pair = S["pair"]
    pair[8:12, 0, 8:16, :] = jnp.where(odd, S["keep2"][1:5, 0, 8:16, :], S["s2"][8:12, 0, 8:16, :])
    level_2 = exchange(L2, pair, 8, pair, 4, 4, "level_2")
    S["all"][gy] = rounded

    kept = pltpu.make_async_copy(
        S["keep0"].at[pl.ds(1, 16), :, pl.ds(8, 32), :],
        S["smooth0"].at[pl.ds(4, 16), :, pl.ds(8, 32), :],
        S["local"].at[0],
    )
    kept.start()
    for old in (side_k, side_s, kappa_1, source_1, matrices, side_v):
        old.left()
    side_v.arrive()
    unpack(2)
    kept.wait()
    matrices.arrive()
    gathered.arrive()
    right = S["all"][...].reshape(gy_size * 8, 128).astype(BF16)
    product = jnp.dot(S["mm"][...].reshape(gy_size * 48, 128), right, preferred_element_type=F32)
    layer_of = lax.broadcasted_iota(jnp.int32, (24, 128), 1) >> 2
    terms = [jnp.where(layer_of == k, product[24 * k : 24 * k + 24], 0.0) for k in range(2 * gy_size)]
    while len(terms) > 1:
        terms = [terms[i] + terms[i + 1] for i in range(0, len(terms), 2)]
    S["corr"][2] = terms[0]
    coarse = Exchange("coarse")
    for a in (-2, -1, 1, 2):
        coarse.add(S["corr"].at[2], S["corr"].at[2 - a], a, 0)
    coarse.start()
    gathered.left()
    level_2.left()
    level_2.arrive()

    def part(x, U):
        for u in range(U):
            for t in range(3):
                rows = pl.ds(8 * t, 8)
                both = pair[x + u, 0, rows, :]
                second = (lane & 1) == 1
                M[2]["NS"][x + u, 0, rows, :] = jnp.where(second, turn(both, 1, 1), both)
                S["smooth2"][x + u, 0, rows, :] = jnp.where(second, both, turn(both, -1, 1))

    loop(2, 18, part, 8)
    scale_source(L2, M[2], "NS", 3, 17)
    coarse.arrive()

    for slab in range(5):
        for d in range(2):
            for b in range(2):
                M[2]["E"][2 * slab + d, 0, pl.ds(b, 8, stride=2), :] = S["corr"][slab, 12 * d : 12 * d + 8, :]
                M[2]["E"][2 * slab + d, 0, pl.ds(16 + b, 4, stride=2), :] = S["corr"][slab, 12 * d + 8 : 12 * d + 12, :]

    def emit_2(x, new):
        for j in range(L2.J):
            for b in range(2):
                M[1]["E"][x, 0, pl.ds(2 * j + b, 8, stride=2 * L2.J), :] = new[0][j]

    def spread():
        for r in range(2):
            half = (lane >> 1) + 64 * r
            for x in range(L1.x0 - 2, L1.x0 + L1.nx + 2):
                for j in range(L1.J):
                    value = pick(M[1]["VB"][x, 0, j + 1], half)
                    for b in range(2):
                        M[0]["E"][x, r, pl.ds(2 * j + b, 8, stride=2 * L1.J), :] = value

    def emit_0(x, new):
        for r in range(2):
            for j in range(L0.J):
                S["result"][x - L0.x0, r, rows_of(L0, j), :] = new[r][j]

    ascend(L2, M[2], 6, emit_2, S["smooth2"])
    ascend(L1, M[1], 5, None)
    spread()
    def store(n):
        for x in range(8 * n, 8 * n + 8):
            for r in range(2):
                out[x, :, 128 * r : 128 * r + 128] = S["result"][x, r, 8:40, :]

    ascend(L0, M[0], 3, emit_0, S["smooth0"], 2, store)
    coarse.left()


def solution(mesh):
    gx_size, gy_size = mesh.shape["gx"], mesh.shape["gy"]
    scratch = {}
    for l, L in enumerate(LEVELS):
        for name, shape in L.scratch().items():
            scratch[str(l) + name] = shape
    scratch["xp"] = pltpu.VMEM((3, 2, 4, 2, 32, 128), BF16)
    scratch["xr"] = pltpu.VMEM((3, 2, 4, 2, 32, 128), BF16)
    scratch["yp"] = pltpu.VMEM((3, 2, 8, 16, 128), BF16)
    scratch["yr"] = pltpu.VMEM((3, 2, 12, 16, 128), BF16)
    scratch["k1"] = pltpu.VMEM((32, 1, 48, 128), BF16)
    scratch["s1"] = pltpu.VMEM((32, 1, 48, 128), BF16)
    scratch["cp"] = pltpu.VMEM((2, 4, 16, 128), BF16)
    scratch["cr"] = pltpu.VMEM((2, 2, 4, 16, 128), BF16)
    scratch["s2"] = pltpu.VMEM((20, 1, 24, 128), F32)
    scratch["keep0"] = pltpu.VMEM((18, 2, 48, 128), F32)
    scratch["smooth0"] = pltpu.VMEM((24, 2, 48, 128), F32)
    scratch["keep2"] = pltpu.VMEM((6, 1, 24, 128), F32)
    scratch["pair"] = pltpu.VMEM((20, 1, 24, 128), F32)
    scratch["smooth2"] = pltpu.VMEM((20, 1, 24, 128), F32)
    scratch["size"] = pltpu.VMEM((768, 128), F32)
    scratch["inverse"] = pltpu.VMEM((1, 2, 128, 128), BF16)
    scratch["mp"] = pltpu.VMEM((256, 128), BF16)
    scratch["ms"] = pltpu.VMEM((gy_size, 48, 128), BF16)
    scratch["mm"] = pltpu.VMEM((gy_size, 48, 128), BF16)
    scratch["mine"] = pltpu.VMEM((8, 128), F32)
    scratch["all"] = pltpu.VMEM((gy_size, 8, 128), F32)
    scratch["corr"] = pltpu.VMEM((5, 24, 128), F32)
    scratch["result"] = pltpu.VMEM((16, 2, 48, 128), F32)
    scratch["ready"] = pltpu.SemaphoreType.REGULAR
    scratch["local"] = pltpu.SemaphoreType.DMA((5,))
    for name in EXCHANGES:
        scratch["send_" + name] = pltpu.SemaphoreType.DMA
        scratch["recv_" + name] = pltpu.SemaphoreType.DMA

    def local(pressure_source, conductance, coarse_inverse):
        return pl.pallas_call(
            functools.partial(kernel, gx_size, gy_size, tuple(scratch)),
            out_shape=pltpu.VMEM(pressure_source.shape, F32),
            in_specs=[
                pl.BlockSpec(memory_space=pl.ANY),
                pl.BlockSpec(memory_space=pl.ANY),
                pl.BlockSpec(memory_space=pl.ANY),
            ],
            out_specs=pl.BlockSpec(memory_space=pltpu.VMEM),
            scratch_shapes=list(scratch.values()),
            compiler_params=pltpu.CompilerParams(
                collective_id=0, has_side_effects=True, vmem_limit_bytes=40 * 2**20
            ),
        )(*(pltpu.with_memory_space_constraint(x, pltpu.HBM) for x in (pressure_source, conductance, coarse_inverse)))

    in_specs = (P("gx", "gy", None), P("gx", "gy", None), P("gx", "gy", None, None))
    return jax.shard_map(local, mesh=mesh, in_specs=in_specs, out_specs=P("gx", "gy", None), check_vma=False)
```

```python
import functools
import math

import jax
import jax.numpy as jnp
from jax import lax
from jax.experimental import pallas as pl
from jax.experimental.pallas import tpu as pltpu
from jax.sharding import PartitionSpec as P

MESH = pl.DeviceIdType.MESH

LMAX = 2.0
LMIN = 0.25
THETA = 0.5 * (LMAX + LMIN)
DELTA = 0.5 * (LMAX - LMIN)
SIGMA = THETA / DELTA
RATIO_0 = 1.0 / SIGMA
RATIO_1 = 1.0 / (2.0 * SIGMA - RATIO_0)
RATIO_2 = 1.0 / (2.0 * SIGMA - RATIO_1)
STEP_1 = (RATIO_1 * RATIO_0, 2.0 * RATIO_1 / DELTA)
STEP_2 = (RATIO_2 * RATIO_1, 2.0 * RATIO_2 / DELTA)

F32 = jnp.float32
BF16 = jnp.bfloat16

EXCHANGES = ("side_k", "side_s", "side_v", "kappa_1", "matrix", "source_1", "gather", "level_2", "coarse")
AROUND = [(a, b) for a in (-1, 0, 1) for b in (-1, 0, 1) if (a, b) != (0, 0)]
WIDE = [(a, b) for a in (-2, -1, 0, 1, 2) for b in (-1, 0, 1) if (a, b) != (0, 0)]
AROUND.sort(key=lambda o: -abs(o[0]) - 2 * abs(o[1]))
WIDE.sort(key=lambda o: -abs(o[0]) - 2 * abs(o[1]))
LINE = sorted(range(1, 16), key=lambda n: -min(n // 4, 4 - n // 4) - min(n % 4, 4 - n % 4))


class Level:
    def __init__(self, nx, ny, x0, side, R, J, hold, row0, erow, xc, coarse, most):
        self.nx, self.ny, self.X, self.x0, self.side = nx, ny, nx + 2 * x0, x0, side
        self.R, self.J, self.hold, self.row0, self.most = R, J, hold, row0, most
        self.erow, self.xc, self.coarse = erow, xc, coarse
        self.rows = ny + 2 * side + (8 if R == 1 else 0)

    def scratch(self):
        X, R, J = self.X, self.R, self.J
        vm = lambda *shape: pltpu.VMEM(shape + (128,), F32)
        blocked = {name: vm(X, R, J, 8) for name in ("CM", "CP", "Q", "D")}
        natural = {name: vm(X, R, self.rows) for name in ("NS", "NK", "RN")}
        return dict(
            E=vm(self.coarse[0], R, self.coarse[1]),
            HK=vm(X, R, J + 2, 8),
            CX=vm(X + 1, R, J, 8),
            CY=vm(X, R, J + 1, 8),
            G=vm(X, R, J + 2, 8),
            VA=vm(X, R, J + 2, 8),
            VB=vm(X, R, J + 2, 8),
            **blocked,
            **natural,
        )


LEVELS = (
    Level(16, 32, 4, 8, 2, 5, 1, 4, 20, 10, (32, 96), 22),
    Level(8, 16, 12, 16, 1, 5, 1, 4, 4, 2, (20, 56), 26),
    Level(4, 8, 8, 8, 1, 3, 2, 0, 0, 0, (10, 32), 16),
)


def lanes(*lead):
    return lax.broadcasted_iota(jnp.int32, lead + (8, 128), len(lead) + 1)


def sublanes():
    return lax.broadcasted_iota(jnp.int32, (8, 128), 0)


def turn(value, shift, axis):
    return pltpu.roll(value, shift % value.shape[axis], axis)


def pick(value, index):
    return jnp.take_along_axis(value, index, axis=1, mode="promise_in_bounds")


def rows_of(L, j):
    return pl.ds(L.row0 + j, 8, stride=L.J)


def beside_z(L, parts):
    h = L.hold
    down = [turn(p, h, 2) for p in parts]
    up = [turn(p, -h, 2) for p in parts]
    if L.R == 2:
        lane = lanes(L.J)
        down[1] = jnp.where(lane == 0, down[0], down[1])
        up[0] = jnp.where(lane == 127, up[1], up[0])
    return down, up


def store_wrapped(ref, x, r, J, values):
    ref[x, r, 1 : J + 1] = values
    ref[x, r, 0] = turn(values[J - 1], 1, 0)
    ref[x, r, J + 1] = turn(values[0], -1, 0)


def rows_from(L, ref, x, r):
    return jnp.stack([ref[x, r, rows_of(L, j), :] for j in range(L.J)])


def rows_to(L, ref, x, r, values):
    for j in range(L.J):
        ref[x, r, rows_of(L, j), :] = values[j]


def loop(lo, hi, body, most=1):
    count = hi - lo
    steps = -(-count // most)
    U = -(-count // steps)
    whole = count // U
    if whole > 1:

        def step(i, carry):
            body(lo + i * U, U)
            return carry

        lax.fori_loop(0, whole, step, 0)
    elif whole == 1:
        body(lo, U)
    if count > whole * U:
        body(lo + whole * U, count - whole * U)


def prepare(L, M, lo, hi, gx, gy, count_x, count_y):
    J, R, h = L.J, L.R, L.hold
    shape = (J, 8, 128)
    lane = lanes(J)
    place = lax.broadcasted_iota(jnp.int32, shape, 0) + J * lax.broadcasted_iota(jnp.int32, shape, 1)
    place = place + (gy * L.ny - L.side + L.row0)
    keep = jnp.where((place >= 0) & (place < L.ny * count_y), 0.5, 0.0).astype(F32)

    def halves(x, U):
        NK, HK = M["NK"].at[pl.ds(x, U)], M["HK"].at[pl.ds(x, U)]
        for u in range(U):
            place = gx * L.nx + x + u - L.x0
            inside = jnp.where((place >= 0) & (place < L.nx * count_x), 1.0, 0.0).astype(F32)
            mask = keep * inside
            for r in range(R):
                store_wrapped(HK, u, r, J, rows_from(L, NK, u, r) * mask)

    loop(lo - 1, hi + 1, halves, L.most)
    for r in range(R):
        M["CX"][lo, r] = M["HK"][lo - 1, r, 1 : J + 1] + M["HK"][lo, r, 1 : J + 1]

    def couple(x, U):
        HK, CX = M["HK"].at[pl.ds(x - 1, U + 2)], M["CX"].at[pl.ds(x, U + 1)]
        CY, CM, CP, D, Q = (M[name].at[pl.ds(x, U)] for name in ("CY", "CM", "CP", "D", "Q"))
        for u in range(U):
            slabs = [beside_y(L, HK, u + 1, r) for r in range(R)]
            down, up = beside_z(L, [slab[0] for slab in slabs])
            down[0] = jnp.where(lane < h, 0.0, down[0])
            up[R - 1] = jnp.where(lane >= 128 - h, 0.0, up[R - 1])
            for r in range(R):
                c, ym, yp = slabs[r]
                xm, xp = HK[u, r, 1 : J + 1], HK[u + 2, r, 1 : J + 1]
                diagonal = (xm + xp) + (ym + yp) + (down[r] + up[r]) + 6.0 * c
                CX[u + 1, r] = c + xp
                CY[u, r, 0:J] = c + ym
                CY[u, r, J] = c[J - 1] + yp[J - 1]
                low, high = c + down[r], c + up[r]
                if r == 0:
                    low = jnp.where(lane < h, 0.0, low)
                if r == R - 1:
                    high = jnp.where(lane >= 128 - h, 0.0, high)
                CM[u, r] = low
                CP[u, r] = high
                D[u, r] = diagonal
                Q[u, r] = jnp.where(c > 0.0, 1.0 / diagonal, 0.0)

    loop(lo, hi, couple, L.most)


def scale_source(L, M, name, lo, hi):
    field = M[name]

    def body(x, U):
        Q, G, NS = (ref.at[pl.ds(x, U)] for ref in (M["Q"], M["G"], field))
        for u in range(U):
            for r in range(L.R):
                store_wrapped(G, u, r, L.J, Q[u, r] * rows_from(L, NS, u, r))

    loop(lo, hi, body, L.most)


def beside_y(L, ref, x, r):
    c = ref[x, r, 1 : L.J + 1]
    low, high = ref[x, r, 0:1], ref[x, r, L.J + 1 : L.J + 2]
    return c, jnp.concatenate([low, c[:-1]], axis=0), jnp.concatenate([c[1:], high], axis=0)


def sweep(L, M, src, dst, lo, hi, step, keep_rows=None, emit=None):
    J, R = L.J, L.R

    def body(x, U):
        V, CX = M[src].at[pl.ds(x - 1, U + 2)], M["CX"].at[pl.ds(x, U + 1)]
        CY, CM, CP, D, Q, GW = (M[name].at[pl.ds(x, U)] for name in ("CY", "CM", "CP", "D", "Q", "G"))
        W = M[dst].at[pl.ds(x, U)] if dst is not None else None
        if step is None:
            RN = M["RN"].at[pl.ds(x, U)]
        if keep_rows is not None:
            kept = keep_rows.at[pl.ds(x - L.x0 + 1, U)]
        for u in range(U):
            slabs = [beside_y(L, V, u + 1, r) for r in range(R)]
            down, up = beside_z(L, [slab[0] for slab in slabs])
            new = []
            for r in range(R):
                c, ym, yp = slabs[r]
                cy = CY[u, r]
                near = CX[u, r] * V[u, r, 1 : J + 1] + CX[u + 1, r] * V[u + 2, r, 1 : J + 1]
                near = near + (cy[:-1] * ym + cy[1:] * yp)
                near = near + (CM[u, r] * down[r] + CP[u, r] * up[r])
                near = Q[u, r] * near
                if step is None:
                    rows_to(L, RN, u, r, D[u, r] * (GW[u, r, 1 : J + 1] + near - c))
                    continue
                p, g, scale, before = step
                if g == scale:
                    value = p * c + scale * (GW[u, r, 1 : J + 1] + near)
                elif g == 0.0:
                    value = p * c + scale * near
                else:
                    value = p * c + g * GW[u, r, 1 : J + 1] + scale * near
                if before != 0.0:
                    value = value - before * W[u, r, 1 : J + 1]
                if emit is None:
                    store_wrapped(W, u, r, J, value)
                if keep_rows is not None:
                    rows_to(L, kept, u, r, value)
                new.append(value)
            if emit is not None:
                emit(x + u, new)

    loop(lo, hi, body, L.most)


def next_step(step):
    a, b = step
    return (1.0 + a - b, b, b, a)


def descend(L, M, margin, keep_rows=None):
    lo, hi = L.x0 - margin, L.x0 + L.nx + margin
    (a, b), (c, d) = STEP_1, STEP_2
    sweep(L, M, "G", "VB", lo - 2, hi + 2, ((1.0 + a - b) / THETA + b, 0.0, b / THETA, 0.0))
    sweep(L, M, "VB", "VA", lo - 1, hi + 1, (1.0 + c - d, d - c / THETA, d, 0.0), keep_rows=keep_rows)
    sweep(L, M, "VA", None, lo, hi, None)


def ascend(L, M, margin, emit, smoothed=None, pieces=1, after=lambda n: None):
    lo, hi = L.x0, L.x0 + L.nx

    def begin(x, U):
        HK, VA = (M[name].at[pl.ds(x, U)] for name in ("HK", "VA"))
        if smoothed is not None:
            NV = smoothed.at[pl.ds(x, U)]
        for u in range(U):
            xc = lax.shift_right_logical(x + u, 1) + L.xc
            for r in range(L.R):
                added = [M["E"][xc, r, pl.ds(L.erow + j, 8, stride=L.J), :] for j in range(L.J)]
                base = VA[u, r, 1 : L.J + 1] if smoothed is None else rows_from(L, NV, u, r)
                inside = HK[u, r, 1 : L.J + 1] > 0.0
                store_wrapped(VA, u, r, L.J, jnp.where(inside, jnp.stack(added) + base, 0.0))

    loop(lo - margin, hi + margin, begin, L.most)
    margin -= 1
    sweep(L, M, "VA", "VB", lo - margin, hi + margin, (1.0 - 1.0 / THETA, 1.0 / THETA, 1.0 / THETA, 0.0))
    margin -= 1
    sweep(L, M, "VB", "VA", lo - margin, hi + margin, next_step(STEP_1))
    margin -= 1
    width = (hi - lo + 2 * margin) // pieces
    for n in range(pieces):
        first = lo - margin + n * width
        sweep(L, M, "VA", "VB", first, first + width, next_step(STEP_2), emit=emit)
        after(n)


def coarsen(L, src, row, tiles, scale, put):
    lane = lanes()
    even = (lane * 2) & 127

    def body(x, U):
        pairs = src.at[pl.ds(2 * x, 2 * U)]
        for u, t in [(u, t) for u in range(U) for t in range(tiles)]:
            sums = []
            for r in range(L.R):
                rows = [pairs[2 * u + dx, r, pl.ds(row + 16 * t + b, 8, stride=2), :] for dx in (0, 1) for b in (0, 1)]
                total = (rows[0] + rows[1]) + (rows[2] + rows[3])
                if L.R == 2:
                    sums.append(pick(total + turn(total, -1, 1), even))
                else:
                    other = jnp.where((lane & L.hold) == 0, turn(total, -L.hold, 1), turn(total, L.hold, 1))
                    sums.append(total + other)
            value = jnp.where(lane < 64, sums[0], sums[1]) if L.R == 2 else sums[0]
            put(x + u, t, value * scale)

    return body


def put_rows(dst, dx, row):
    def put(x, t, value):
        dst[dx + x, 0, row + 8 * t : row + 8 * t + 8, :] = value

    return put


def kernel(gx_size, gy_size, names, source, conductance, inverse, out, *refs):
    S = dict(zip(names, refs))
    M = [{k[1:]: v for k, v in S.items() if k[0] == str(l)} for l in range(3)]
    M[2]["s2"] = S["s2"]
    gx, gy = lax.axis_index("gx"), lax.axis_index("gy")
    L0, L1, L2 = LEVELS

    def device(a, b):
        return {"gx": lax.rem(gx + a + gx_size, gx_size), "gy": lax.rem(gy + b + gy_size, gy_size)}

    class Exchange:
        def __init__(self, name):
            self.out, self.back, self.rows, self.copies = S["send_" + name], S["recv_" + name], 0, []

        def add(self, src, dst, a, b):
            copy = pltpu.make_async_remote_copy(
                src_ref=src, dst_ref=dst, send_sem=self.out, recv_sem=self.back, device_id=device(a, b), device_id_type=MESH
            )
            self.copies.append(copy)
            rows = math.prod(src.shape[:-1])
            self.rows += rows if src.dtype == F32 else rows // 2

        def start(self):
            for copy in self.copies:
                copy.start()
            return self

        def wait(self, semaphore):
            size = S["size"].at[pl.ds(0, self.rows)]
            pltpu.make_async_copy(size, size, semaphore).wait()

        def arrive(self):
            self.wait(self.back)

        def left(self):
            self.wait(self.out)

    def exchange(L, src, sx0, dst, near, far, name):
        both = Exchange(name)
        h = L.side
        for a, b in WIDE if far else AROUND:
            w = {0: L.nx, 1: near, 2: far}[abs(a)]
            xs = sx0 + (L.nx - w if a > 0 else 0)
            xd = {0: L.x0, 1: L.x0 - w, 2: L.x0 - L.nx - w, -1: L.x0 + L.nx, -2: L.x0 + 2 * L.nx}[a]
            ys = h + (L.ny - h if b > 0 else 0)
            yd, wy = {0: (h, L.ny), 1: (0, h), -1: (h + L.ny, h)}[b]
            both.add(src.at[pl.ds(xs, w), :, pl.ds(ys, wy), :], dst.at[pl.ds(xd, w), :, pl.ds(yd, wy), :], a, b)
        return both.start()

    peers = [(0, b) for b in LINE if 1 < b < gy_size - 1] + AROUND
    barrier = pltpu.get_barrier_semaphore()
    for a, b in peers:
        pl.semaphore_signal(barrier, inc=1, device_id=device(a, b), device_id_type=MESH)

    fields = (M[0]["NK"], M[0]["NS"], S["smooth0"])
    XP, YP, XR, YR = S["xp"], S["yp"], S["xr"], S["yr"]
    sub, lane = sublanes(), lanes()

    loads = [pltpu.make_async_copy(inverse, S["inverse"], S["local"].at[4])]
    for n, src in enumerate((conductance, source)):
        for r in range(2):
            loads.append(
                pltpu.make_async_copy(
                    src.at[:, :, pl.ds(128 * r, 128)],
                    fields[n].at[pl.ds(4, 16), r, pl.ds(8, 32), :],
                    S["local"].at[2 * n + r],
                )
            )
    for copy in loads:
        copy.start()

    def pack(a, field, first):
        def pack_x(i, _):
            for r in range(2):
                XP[a, 0, i, r] = field[first + i, r, 8:40, :].astype(BF16)
                XP[a, 1, i, r] = field[first + 12 + i, r, 8:40, :].astype(BF16)

        def pack_y(i, _):
            low, high = [], []
            for d in range(2):
                x = first + 2 * i + d
                near, far = field[x, 0, 8:16, :], field[x, 1, 8:16, :]
                low.append(jnp.where(sub < 4, near, turn(far, 4, 0)))
                near, far = field[x, 0, 32:40, :], field[x, 1, 32:40, :]
                high.append(jnp.where(sub < 4, turn(near, 4, 0), far))
            YP[a, 0, i] = jnp.concatenate(low, axis=0).astype(BF16)
            YP[a, 1, i] = jnp.concatenate(high, axis=0).astype(BF16)

        loop(0, 4, pack_x)
        loop(0, 8, pack_y)

    def sides(a, name):
        both = Exchange(name)
        for x, y in AROUND:
            if y == 0:
                both.add(XP.at[a, (x + 1) // 2], XR.at[a, (1 - x) // 2], x, y)
            else:
                wx = 8 if x == 0 else 2 if a == 0 else 1
                xs, xd = {0: (0, 2), 1: (8 - wx, 2 - wx), -1: (0, 10)}[x]
                both.add(YP.at[a, (y + 1) // 2, pl.ds(xs, wx)], YR.at[a, (1 - y) // 2, pl.ds(xd, wx)], x, y)
        return both.start()

    def unpack(a):
        field = fields[a]

        def unpack_x(i, _):
            for r in range(2):
                field[i, r, 8:40, :] = XR[a, 0, i, r].astype(F32)
                field[20 + i, r, 8:40, :] = XR[a, 1, i, r].astype(F32)

        def unpack_y(i, _):
            low, high = YR[a, 0, i].astype(F32), YR[a, 1, i].astype(F32)
            for d in range(2):
                x = 2 * i + d
                part = low[8 * d : 8 * d + 8]
                field[x, 0, 0:8, :] = turn(part, 4, 0)
                field[x, 1, 0:8, :] = part
                part = high[8 * d : 8 * d + 8]
                field[x, 0, 40:48, :] = part
                field[x, 1, 40:48, :] = turn(part, 4, 0)

        loop(0, 4, unpack_x)
        loop(0, 12, unpack_y)

    for a in range(2):
        loads[1 + 2 * a].wait()
        loads[2 + 2 * a].wait()
        pack(a, fields[a], 4)

    pl.semaphore_wait(barrier, len(peers))
    side_k = sides(0, "side_k")
    side_s = sides(1, "side_s")
    for a in (-1, 1):
        pl.semaphore_signal(S["ready"], inc=1, device_id=device(a, 0), device_id_type=MESH)

    def halve(field, packed):
        packed[12:20, 0, 16:32, :] = field[12:20, 0, 16:32, :].astype(BF16)

    def widen(packed, field, margin, beside):
        def take(parts):
            def body(x, U):
                for u in range(U):
                    for rows in parts:
                        field[x + u, 0, rows, :] = packed[x + u, 0, rows, :].astype(F32)

            return body

        loop(12 - margin, 12, take(beside), 12)
        loop(12, 20, take((pl.ds(0, 16), pl.ds(32, 16))), 8)
        loop(20, 20 + margin, take(beside), 12)

    loop(0, 8, coarsen(L0, M[0]["NK"].at[pl.ds(4, 16)], 8, 2, 0.125, put_rows(M[1]["NK"], 12, 16)), 4)
    halve(M[1]["NK"], S["k1"])

    loads[0].wait()
    one = lambda mask: jnp.where(mask, 1.0, 0.0).astype(BF16)
    row = lax.broadcasted_iota(jnp.int32, (128, 128), 0)
    column = lax.broadcasted_iota(jnp.int32, (128, 128), 1)
    order = one(row == ((column >> 2) & 1) * 64 + (column >> 3) * 4 + (column & 3))
    for k in range(2):
        S["mp"][128 * k : 128 * (k + 1), :] = jnp.dot(
            S["inverse"][0, k], order, preferred_element_type=F32
        ).astype(BF16)

    row = lax.broadcasted_iota(jnp.int32, (4, 48, 256), 1)
    column = lax.broadcasted_iota(jnp.int32, (4, 48, 256), 2)
    layer = jnp.where(row >= 24, 1, 0)
    row = row - 24 * layer
    half = jnp.where(row >= 12, 1, 0)
    row = row - 12 * half + 4 * lax.broadcasted_iota(jnp.int32, (4, 48, 256), 0)
    base = layer * 128 + half * 64

    def share(d, _):
        chosen = one(column == base + ((row + (16 * d + 60)) & 63)).reshape(192, 256)
        rows = jnp.dot(chosen, S["mp"][...], preferred_element_type=F32)
        S["ms"][pl.ds(4 * d, 4)] = rows.astype(BF16).reshape(4, 48, 128)

    loop(0, gy_size // 4, share)
    pl.semaphore_wait(S["ready"], 2)
    kappa_1 = exchange(L1, S["k1"], 12, S["k1"], 8, 4, "kappa_1")

    place = (gx, gy, gx_size, gy_size)
    side_k.arrive()
    unpack(0)
    prepare(L0, M[0], 1, 23, *place)
    side_s.arrive()
    unpack(1)
    scale_source(L0, M[0], "NS", 1, 23)
    descend(L0, M[0], 0, S["keep0"])
    residual = M[0]["RN"].at[pl.ds(4, 16)]
    loop(0, 8, coarsen(L0, residual, 8, 2, 0.5, put_rows(M[1]["NS"], 12, 16)), 8)
    halve(M[1]["NS"], S["s1"])
    for i in range(4):
        for side in range(2):
            rows = pl.ds(16 + 8 * side, 8)
            both = [M[1]["NS"][12 + 2 * i + d, 0, rows, :] for d in range(2)]
            S["cp"][side, i] = jnp.concatenate(both, axis=0).astype(BF16)
    source_1 = Exchange("source_1")
    for a in (-1, 1):
        for b in (-1, 1):
            source_1.add(S["cp"].at[(b + 1) // 2], S["cr"].at[(1 - b) // 2, (1 - a) // 2], a, b)
    own = S["s1"].at[pl.ds(12, 8), :, pl.ds(16, 16), :]
    for b in (-1, 1):
        source_1.add(own, S["s1"].at[pl.ds(12, 8), :, pl.ds(16 - 16 * b, 16), :], 0, b)
    own = pl.ds(16, 16)
    for a, xs, xd, w in ((-2, 12, 28, 1), (2, 19, 3, 1), (-1, 12, 20, 8), (1, 12, 4, 8)):
        source_1.add(S["s1"].at[pl.ds(xs, w), :, own, :], S["s1"].at[pl.ds(xd, w), :, own, :], a, 0)
    source_1.start()

    kappa_1.arrive()
    widen(S["k1"], M[1]["NK"], 12, (pl.ds(0, 48),))
    prepare(L1, M[1], 3, 29, *place)
    loop(0, 16, coarsen(L1, M[1]["NK"], 0, 3, 0.125, put_rows(M[2]["NK"], 2, 0)), 8)
    prepare(L2, M[2], 3, 17, *place)
    matrices = Exchange("matrix")
    for n in LINE:
        matrices.add(S["ms"].at[lax.rem(gy + n, gy_size)], S["mm"].at[gy], 0, n)
    matrices.start()
    S["mm"][gy] = S["ms"][gy]
    pack(2, S["keep0"], 1)
    side_v = sides(2, "side_v")

    source_1.arrive()
    widen(S["s1"], M[1]["NS"], 9, (pl.ds(16, 16),))
    for i in range(4):
        for ys in range(2):
            for xs in range(2):
                both = S["cr"][ys, xs, i].astype(F32)
                for d in range(2):
                    M[1]["NS"][4 + 16 * xs + 2 * i + d, 0, pl.ds(8 + 24 * ys, 8), :] = both[8 * d : 8 * d + 8]
    scale_source(L1, M[1], "NS", 3, 29)
    descend(L1, M[1], 6)

    residual = M[1]["RN"].at[pl.ds(6, 20)]
    loop(0, 10, coarsen(L1, residual, 0, 3, 0.5, put_rows(S["s2"], 5, 0)), 10)
    scale_source(L2, M[2], "s2", 5, 15)
    descend(L2, M[2], 0, S["keep2"])
    tiles = []
    residual = M[2]["RN"].at[pl.ds(8, 4)]
    loop(0, 2, coarsen(L2, residual, 8, 1, 1.0 / 128.0, lambda x, t, value: tiles.append(value)), 2)
    rounded = jnp.where(sub < 4, tiles[0], turn(tiles[1], 4, 0)).astype(BF16).astype(F32)
    S["mine"][...] = rounded
    gathered = Exchange("gather")
    for n in LINE:
        gathered.add(S["mine"], S["all"].at[gy], 0, n)
    gathered.start()
    odd = (lanes(4) & 1) == 1
    pair = S["pair"]
    pair[8:12, 0, 8:16, :] = jnp.where(odd, S["keep2"][1:5, 0, 8:16, :], S["s2"][8:12, 0, 8:16, :])
    level_2 = exchange(L2, pair, 8, pair, 4, 4, "level_2")
    S["all"][gy] = rounded

    kept = pltpu.make_async_copy(
        S["keep0"].at[pl.ds(1, 16), :, pl.ds(8, 32), :],
        S["smooth0"].at[pl.ds(4, 16), :, pl.ds(8, 32), :],
        S["local"].at[0],
    )
    kept.start()
    for old in (side_k, side_s, kappa_1, source_1, matrices, side_v):
        old.left()
    side_v.arrive()
    unpack(2)
    kept.wait()
    matrices.arrive()
    gathered.arrive()
    right = S["all"][...].reshape(gy_size * 8, 128).astype(BF16)
    product = jnp.dot(S["mm"][...].reshape(gy_size * 48, 128), right, preferred_element_type=F32)
    layer_of = lax.broadcasted_iota(jnp.int32, (24, 128), 1) >> 2
    terms = [jnp.where(layer_of == k, product[24 * k : 24 * k + 24], 0.0) for k in range(2 * gy_size)]
    while len(terms) > 1:
        terms = [terms[i] + terms[i + 1] for i in range(0, len(terms), 2)]
    S["corr"][2] = terms[0]
    coarse = Exchange("coarse")
    for a in (-2, -1, 1, 2):
        coarse.add(S["corr"].at[2], S["corr"].at[2 - a], a, 0)
    coarse.start()
    gathered.left()
    level_2.left()
    level_2.arrive()

    def part(x, U):
        for u in range(U):
            for t in range(3):
                rows = pl.ds(8 * t, 8)
                both = pair[x + u, 0, rows, :]
                second = (lane & 1) == 1
                M[2]["NS"][x + u, 0, rows, :] = jnp.where(second, turn(both, 1, 1), both)
                S["smooth2"][x + u, 0, rows, :] = jnp.where(second, both, turn(both, -1, 1))

    loop(2, 18, part, 8)
    scale_source(L2, M[2], "NS", 3, 17)
    coarse.arrive()

    for slab in range(5):
        for d in range(2):
            for b in range(2):
                M[2]["E"][2 * slab + d, 0, pl.ds(b, 8, stride=2), :] = S["corr"][slab, 12 * d : 12 * d + 8, :]
                M[2]["E"][2 * slab + d, 0, pl.ds(16 + b, 4, stride=2), :] = S["corr"][slab, 12 * d + 8 : 12 * d + 12, :]

    def emit_2(x, new):
        for j in range(L2.J):
            for b in range(2):
                M[1]["E"][x, 0, pl.ds(2 * j + b, 8, stride=2 * L2.J), :] = new[0][j]

    def spread():
        for r in range(2):
            half = (lane >> 1) + 64 * r
            for x in range(L1.x0 - 2, L1.x0 + L1.nx + 2):
                for j in range(L1.J):
                    value = pick(M[1]["VB"][x, 0, j + 1], half)
                    for b in range(2):
                        M[0]["E"][x, r, pl.ds(2 * j + b, 8, stride=2 * L1.J), :] = value

    def emit_0(x, new):
        for r in range(2):
            for j in range(L0.J):
                S["result"][x - L0.x0, r, rows_of(L0, j), :] = new[r][j]

    ascend(L2, M[2], 6, emit_2, S["smooth2"])
    ascend(L1, M[1], 5, None)
    spread()
    def store(n):
        for x in range(8 * n, 8 * n + 8):
            for r in range(2):
                out[x, :, 128 * r : 128 * r + 128] = S["result"][x, r, 8:40, :]

    ascend(L0, M[0], 3, emit_0, S["smooth0"], 2, store)
    coarse.left()


def solution(mesh):
    gx_size, gy_size = mesh.shape["gx"], mesh.shape["gy"]
    scratch = {}
    for l, L in enumerate(LEVELS):
        for name, shape in L.scratch().items():
            scratch[str(l) + name] = shape
    scratch["xp"] = pltpu.VMEM((3, 2, 4, 2, 32, 128), BF16)
    scratch["xr"] = pltpu.VMEM((3, 2, 4, 2, 32, 128), BF16)
    scratch["yp"] = pltpu.VMEM((3, 2, 8, 16, 128), BF16)
    scratch["yr"] = pltpu.VMEM((3, 2, 12, 16, 128), BF16)
    scratch["k1"] = pltpu.VMEM((32, 1, 48, 128), BF16)
    scratch["s1"] = pltpu.VMEM((32, 1, 48, 128), BF16)
    scratch["cp"] = pltpu.VMEM((2, 4, 16, 128), BF16)
    scratch["cr"] = pltpu.VMEM((2, 2, 4, 16, 128), BF16)
    scratch["s2"] = pltpu.VMEM((20, 1, 32, 128), F32)
    scratch["keep0"] = pltpu.VMEM((18, 2, 48, 128), F32)
    scratch["smooth0"] = pltpu.VMEM((24, 2, 48, 128), F32)
    scratch["keep2"] = pltpu.VMEM((6, 1, 32, 128), F32)
    scratch["pair"] = pltpu.VMEM((20, 1, 32, 128), F32)
    scratch["smooth2"] = pltpu.VMEM((20, 1, 32, 128), F32)
    scratch["size"] = pltpu.VMEM((768, 128), F32)
    scratch["inverse"] = pltpu.VMEM((1, 2, 128, 128), BF16)
    scratch["mp"] = pltpu.VMEM((256, 128), BF16)
    scratch["ms"] = pltpu.VMEM((gy_size, 48, 128), BF16)
    scratch["mm"] = pltpu.VMEM((gy_size, 48, 128), BF16)
    scratch["mine"] = pltpu.VMEM((8, 128), F32)
    scratch["all"] = pltpu.VMEM((gy_size, 8, 128), F32)
    scratch["corr"] = pltpu.VMEM((5, 24, 128), F32)
    scratch["result"] = pltpu.VMEM((16, 2, 48, 128), F32)
    scratch["ready"] = pltpu.SemaphoreType.REGULAR
    scratch["local"] = pltpu.SemaphoreType.DMA((5,))
    for name in EXCHANGES:
        scratch["send_" + name] = pltpu.SemaphoreType.DMA
        scratch["recv_" + name] = pltpu.SemaphoreType.DMA

    def local(pressure_source, conductance, coarse_inverse):
        return pl.pallas_call(
            functools.partial(kernel, gx_size, gy_size, tuple(scratch)),
            out_shape=pltpu.VMEM(pressure_source.shape, F32),
            in_specs=[
                pl.BlockSpec(memory_space=pl.ANY),
                pl.BlockSpec(memory_space=pl.ANY),
                pl.BlockSpec(memory_space=pl.ANY),
            ],
            out_specs=pl.BlockSpec(memory_space=pltpu.VMEM),
            scratch_shapes=list(scratch.values()),
            compiler_params=pltpu.CompilerParams(
                collective_id=0, has_side_effects=True, vmem_limit_bytes=40 * 2**20
            ),
        )(*(pltpu.with_memory_space_constraint(x, pltpu.HBM) for x in (pressure_source, conductance, coarse_inverse)))

    in_specs = (P("gx", "gy", None), P("gx", "gy", None), P("gx", "gy", None, None))
    return jax.shard_map(local, mesh=mesh, in_specs=in_specs, out_specs=P("gx", "gy", None), check_vma=False)
```
